512 devices in a mesh: ctx: 64 (over z, y), head: 8 (over x, core).
Axes of the slice: x: 4, y: 4, z: 16, core: 2. Of those that a mesh axis runs over, the one named last changes fastest.
Arguments:
- queries: bfloat16 [8192, 16, 128], P('ctx', 'head'), may hold values from -6 to 6
- key_rows: bfloat16 [8192, 2, 16, 128], P('ctx', None, 'head'), may hold values from -6 to 6
- value_rows: bfloat16 [8192, 2, 16, 128], P('ctx', None, 'head'), may hold values from -6 to 6
- strengths: float32 [8192, 2, 16], P('ctx', None, 'head'), may hold values from 0 to 2
- log_decay: float32 [8192, 16], P('ctx', 'head'), may hold values from -2 to 0
- norm_gain: float32 [16, 128], P('head'), may hold values from 0.1 to 1.9
- out_weight: bfloat16 [2048, 2048], P('head'), may hold values from -0.125 to 0.125
Outputs:
- mixer_out: bfloat16 [8192, 2048], P(('ctx', 'head'))
The draws below stay inside these ranges and needn't reach their ends.
All inputs are finite; a program needn't handle non-finite values.
Results may differ from the reference program's by a relative error of at most 0.0049.
Values sent between devices are 32-bit elements; how exact they have to be, the bound alone decides.
No kernel may reach another device: no remote copies, remote signals or barrier semaphores. Data moves between devices by JAX's collectives and lax.ppermute only.
A program may use at most 64 MiB of HBM per device.

```python
import math
import jax
import jax.numpy as jnp
from jax import lax

D = 2048
H = 16
DK = 128
DV = 128
TOKENS = 8192


def slow_choice(key, share):
    picks = jax.random.randint(jax.random.fold_in(key, 901), (H,), 0, 16)
    return picks < share


def log_spread(key, shape, lower, upper):
    return jnp.exp(jax.random.uniform(key, shape, jnp.float32, math.log(lower), math.log(upper)))


def draw_strengths(key, part):
    slow_forgetting_groups = slow_choice(key, 8)
    key = jax.random.fold_in(key, 3)
    first_key, second_key = jax.random.split(key)
    gentle = DK / (4.0 * TOKENS) * log_spread(first_key, (TOKENS, 2, H), 0.5, 2.0)
    strong = jax.random.uniform(second_key, (TOKENS, 2, H), jnp.float32, 0.3, 1.7)
    return jnp.where(slow_forgetting_groups[None, None, :], gentle, strong)


def draw_log_decay(key, part):
    slow_forgetting_groups = slow_choice(key, 8)
    key = jax.random.fold_in(key, 5)
    split_keys = jax.random.split(key, 5)
    jitter = log_spread(split_keys[1], (TOKENS, H), 0.5, 2.0)
    fast_forgetting_factor = log_spread(split_keys[0], (1, H), 1.0 / 50.0, 1.0 / 30.0) * jitter
    slow_forgetting_factor = 0.5 / TOKENS * log_spread(split_keys[2], (1, H), 0.5, 2.0) * jitter
    cache_indices = jax.random.randint(split_keys[3], (2, H), 0, TOKENS)
    sequence_indices = jnp.arange(TOKENS, dtype=jnp.int32)[:, None, None]
    deviation_amounts = jnp.log(jax.random.uniform(split_keys[4], (1, 2, H), jnp.float32, 0.5, 0.8))
    segment_groups = jnp.sum(jnp.where(sequence_indices == cache_indices[None, :, :], deviation_amounts, 0.0), axis=1)
    return segment_groups - jnp.where(slow_forgetting_groups[None, :], slow_forgetting_factor, fast_forgetting_factor)


def block_scale(own_key, shape, cuts, least, high):
    loudness = 1.0
    for dim, blocks in cuts:
        heights = jax.random.uniform(jax.random.fold_in(jax.random.fold_in(own_key, 6), dim), (blocks,), jnp.float32, least / len(cuts), high / len(cuts))
        loudness = loudness * jnp.repeat(jnp.exp(heights), shape[dim] // blocks).reshape((-1,) + (1,) * (len(shape) - 1 - dim))
    return loudness


def bell_draw(stream_key, dims, scale, most, pieces=(), kind=jnp.bfloat16):
    level = block_scale(stream_key, dims, pieces, -0.22, 0.18) if pieces else 1.0
    values = jax.random.normal(stream_key, dims, jnp.float32) * scale * level
    return jnp.minimum(jnp.maximum(values, -most), most).astype(kind)


def setup_inputs(seed: int = 0) -> dict:
    splits = jax.random.split(jax.random.key(seed), 8)
    queries = bell_draw(splits[0], (TOKENS, H, DK), 1.0, 6.0, ((0, 64), (1, 8)))
    key_rows = bell_draw(splits[1], (TOKENS, 2, H, DK), 1.0, 6.0, ((0, 64), (2, 8)))
    value_rows = bell_draw(splits[2], (TOKENS, 2, H, DV), 1.0, 6.0, ((0, 64), (2, 8)))
    strengths = draw_strengths(jax.random.fold_in(splits[7], 71), 0)
    log_decay = draw_log_decay(jax.random.fold_in(splits[7], 71), 0)
    norm_gain = jnp.clip(1.0 + 0.18 * jax.random.normal(splits[5], (H, DV), jnp.float32), 0.1, 1.9)
    out_weight = bell_draw(splits[6], (H * DV, D), (H * DV) ** -0.5, 0.125, ((0, 8),))
    return dict(queries=queries, key_rows=key_rows, value_rows=value_rows, strengths=strengths, log_decay=log_decay, norm_gain=norm_gain, out_weight=out_weight)


HIGHEST = lax.Precision.HIGHEST

def unit_rows(values_in):
    return values_in * lax.rsqrt(lax.optimization_barrier(jnp.sum(values_in * values_in, axis=-1, keepdims=True)) + 1e-06)

def reference(queries, key_rows, value_rows, strengths, log_decay, norm_gain, out_weight):
    query_unit = unit_rows(queries.astype(jnp.float32))
    key_unit = unit_rows(key_rows.astype(jnp.float32))
    value_full = value_rows.astype(jnp.float32)

    def advance(state_now, token_data):
        query_t, key_t, value_t, strength_t, decay_t = token_data
        state_now = jnp.exp(decay_t)[:, None, None] * state_now
        for reflection in range(2):
            predicted = jnp.einsum('hvk,hk->hv', state_now, key_t[reflection], precision=HIGHEST)
            update = strength_t[reflection][:, None] * (value_t[reflection] - predicted)
            state_now = state_now + update[:, :, None] * key_t[reflection][:, None, :]
        return (state_now, jnp.einsum('hvk,hk->hv', state_now, query_t, precision=HIGHEST))
    start_state = jnp.zeros((H, DV, DK), jnp.float32)
    last_state, outputs = lax.scan(advance, start_state, (query_unit, key_unit, value_full, strengths, log_decay))
    scaled = outputs * lax.rsqrt(lax.optimization_barrier(jnp.mean(outputs * outputs, axis=-1, keepdims=True)) + 1e-05) * norm_gain[None, :, :]
    hidden = scaled.reshape(TOKENS, H * DV).astype(jnp.bfloat16)
    return jnp.dot(hidden, out_weight, preferred_element_type=jnp.float32).astype(jnp.bfloat16)
```

```python
import functools

import jax
import jax.numpy as jnp
from jax import lax
from jax.experimental import pallas as pl
from jax.experimental.pallas import tpu as pltpu
from jax.sharding import PartitionSpec as P

F32 = jnp.float32
HIGHEST = lax.Precision.HIGHEST
GROUP = 8


def dot(left, right, left_dim=1, right_dim=0):
    return lax.dot_general(
        left,
        right,
        (((left_dim,), (right_dim,)), ((), ())),
        precision=HIGHEST,
        preferred_element_type=F32,
    )


def unit_rows(rows):
    return rows * lax.rsqrt(jnp.sum(rows * rows, axis=-1, keepdims=True) + 1e-06)


def inverse_blocks(lower, row_ids, col_ids, start, stop):
    size = lower.shape[0]
    eye = jnp.where(row_ids == col_ids, 1.0, 0.0).astype(F32)
    base = jnp.where(row_ids // start == col_ids // start, lower, 0.0)
    square = dot(base, base)
    first = eye - base + square - dot(base, square)
    inverse = first + dot(first, dot(square, square))
    width = start
    while width < stop:
        below = (row_ids // (2 * width) == col_ids // (2 * width)) & (
            row_ids // width != col_ids // width
        )
        corner = jnp.where(below, lower, 0.0)
        inverse = inverse - dot(inverse, dot(corner, inverse))
        width *= 2
    return inverse


def local_kernel(heads, q_ref, k_ref, v_ref, beta_ref, decay_ref, decay_t_ref, msg_ref, own_ref, through_ref):
    tokens = q_ref.shape[0]
    rows = k_ref.shape[0]
    width = k_ref.shape[1] // heads
    row_ids = lax.broadcasted_iota(jnp.int32, (rows, rows), 0)
    col_ids = lax.broadcasted_iota(jnp.int32, (rows, rows), 1)
    tok_ids = lax.broadcasted_iota(jnp.int32, (tokens, rows), 0)
    tok_cols = lax.broadcasted_iota(jnp.int32, (tokens, rows), 1)
    row_tok = lax.broadcasted_iota(jnp.int32, (rows, tokens), 0) // 2
    up_to = jnp.where(row_tok >= lax.broadcasted_iota(jnp.int32, (rows, tokens), 1), 1.0, 0.0).astype(F32)
    tok_up_to = jnp.where(
        lax.broadcasted_iota(jnp.int32, (tokens, tokens), 0)
        >= lax.broadcasted_iota(jnp.int32, (tokens, tokens), 1),
        1.0,
        0.0,
    ).astype(F32)
    cumul_rows = dot(up_to, decay_ref[...])
    cumul_toks = dot(tok_up_to, decay_ref[...])
    cumul_line = dot(decay_t_ref[...], up_to, 1, 1)
    eye_k = jnp.where(
        lax.broadcasted_iota(jnp.int32, (width, width), 0)
        == lax.broadcasted_iota(jnp.int32, (width, width), 1),
        1.0,
        0.0,
    ).astype(F32)
    half = rows // 2
    quarter = width // (GROUP // heads)
    for head in range(heads):
        lanes = slice(head * width, (head + 1) * width)
        keys = unit_rows(k_ref[:, lanes].astype(F32))
        query = unit_rows(q_ref[:, lanes].astype(F32))
        beta = beta_ref[:, head : head + 1]
        cumul = cumul_rows[:, head : head + 1]
        line = cumul_line[head : head + 1, :]
        weight = jnp.exp(jnp.where(row_ids >= col_ids, cumul - line, -1e30))
        lower = jnp.where(row_ids > col_ids, beta * weight * dot(keys, keys, 1, 1), 0.0)
        inverse = inverse_blocks(lower, row_ids, col_ids, 8, half)
        right = jnp.concatenate([beta * v_ref[:, lanes].astype(F32), (beta * jnp.exp(cumul)) * keys], axis=1)
        upper = dot(inverse[:half, :half], right[:half])
        under = dot(inverse[half:, half:], right[half:] - dot(lower[half:, :half], upper))
        solved = jnp.concatenate([upper, under], axis=0)
        last = cumul[rows - 1 : rows, :]
        tail = jnp.exp(last - cumul) * keys
        pair = dot(solved, tail, 0, 0)
        write = pair[:width]
        carry = jnp.exp(last) * eye_k - pair[width:]
        for part in range(GROUP // heads):
            member = head * (GROUP // heads) + part
            msg_ref[member, :width, :] = carry
            msg_ref[member, width:, :] = write[part * quarter : (part + 1) * quarter]
        cumul_tok = cumul_toks[:, head : head + 1]
        scores = dot(query, keys, 1, 1) * jnp.exp(
            jnp.where(tok_ids >= tok_cols // 2, cumul_tok - line, -1e30)
        )
        mixed = dot(scores, solved)
        own_ref[:, lanes] = mixed[:, :width]
        through_ref[:, lanes] = jnp.exp(cumul_tok) * query - mixed[:, width:]


def compose(earlier, later, width):
    both = dot(earlier, later[:width])
    return jnp.concatenate([both[:width], both[width:] + later[width:]], axis=0)


def group_kernel(width, parts_ref, prefix_ref, total_ref):
    count = parts_ref.shape[0]
    runs = [parts_ref[i] for i in range(count)]
    step = 1
    while step < count:
        for start in range(step, count, 2 * step):
            for i in range(start, start + step):
                runs[i] = compose(runs[start - 1], runs[i], width)
        step *= 2
    for i in range(count - 1):
        prefix_ref[i] = runs[i]
    total_ref[...] = runs[count - 1]


def start_kernel(width, place_ref, totals_ref, prefix_ref, state_ref):
    place = place_ref[0]
    count = totals_ref.shape[0]
    state = jnp.zeros((totals_ref.shape[1] - width, width), F32)
    for i in range(count - 1):
        moved = dot(state, totals_ref[i, :width]) + totals_ref[i, width:]
        state = jnp.where(i < place, moved, state)
    state_ref[0] = state
    for i in range(prefix_ref.shape[0]):
        state_ref[i + 1] = dot(state, prefix_ref[i, :width]) + prefix_ref[i, width:]


def output_kernel(heads, own_ref, through_ref, state_ref, gain_ref, weight_ref, out_ref):
    width = own_ref.shape[1] // heads
    hidden = []
    for head in range(heads):
        lanes = slice(head * width, (head + 1) * width)
        outputs = own_ref[:, lanes] + dot(through_ref[:, lanes], state_ref[head], 1, 1)
        scale = lax.rsqrt(jnp.mean(outputs * outputs, axis=-1, keepdims=True) + 1e-05)
        hidden.append((outputs * scale * gain_ref[head : head + 1, :]).astype(jnp.bfloat16))
    hidden = jnp.concatenate(hidden, axis=1)
    out_ref[...] = jnp.dot(hidden, weight_ref[...], preferred_element_type=F32)


def per_device(queries, key_rows, value_rows, strengths, log_decay, norm_gain, out_weight):
    tokens, heads, width = queries.shape
    rows = 2 * tokens
    columns = out_weight.shape[1]
    groups = lax.axis_size("ctx") // GROUP
    spread = lax.axis_size("head")
    inner = [[g * GROUP + j for j in range(GROUP)] for g in range(groups)]
    outer = [[g * GROUP + j for g in range(groups)] for j in range(GROUP)]
    part_rows = width + width * heads // GROUP
    params = pltpu.CompilerParams(vmem_limit_bytes=48 * 1024 * 1024)

    decay_t = jnp.concatenate([log_decay.T, jnp.zeros((8 - heads, tokens), F32)], axis=0)
    msg, own, through = pl.pallas_call(
        functools.partial(local_kernel, heads),
        out_shape=(
            jax.ShapeDtypeStruct((GROUP, part_rows, width), F32),
            jax.ShapeDtypeStruct((tokens, heads * width), F32),
            jax.ShapeDtypeStruct((tokens, heads * width), F32),
        ),
        compiler_params=params,
        name="local_chunk",
    )(
        queries.reshape(tokens, heads * width),
        key_rows.reshape(rows, heads * width),
        value_rows.reshape(rows, heads * width),
        strengths.reshape(rows, heads),
        log_decay,
        decay_t,
    )
    parts = lax.all_to_all(msg, "ctx", 0, 0, axis_index_groups=inner)
    prefix, total = pl.pallas_call(
        functools.partial(group_kernel, width),
        out_shape=(
            jax.ShapeDtypeStruct((GROUP - 1, part_rows, width), F32),
            jax.ShapeDtypeStruct((part_rows, width), F32),
        ),
        compiler_params=params,
        name="group_scan",
    )(parts)
    totals = lax.all_gather(total, "ctx", axis_index_groups=outer)
    place = (lax.axis_index("ctx") // GROUP).astype(jnp.int32).reshape(1)
    starts = pl.pallas_call(
        functools.partial(start_kernel, width),
        out_shape=jax.ShapeDtypeStruct((GROUP, part_rows - width, width), F32),
        in_specs=[
            pl.BlockSpec(memory_space=pltpu.SMEM),
            pl.BlockSpec(memory_space=pltpu.VMEM),
            pl.BlockSpec(memory_space=pltpu.VMEM),
        ],
        compiler_params=params,
        name="start_states",
    )(place, totals, prefix)
    states = lax.all_to_all(starts, "ctx", 0, 0, axis_index_groups=inner)
    sums = pl.pallas_call(
        functools.partial(output_kernel, heads),
        out_shape=jax.ShapeDtypeStruct((tokens, columns), F32),
        compiler_params=params,
        name="project",
    )(own, through, states.reshape(heads, width, width), norm_gain, out_weight)
    shares = lax.all_to_all(sums.reshape(spread, tokens // spread, columns), "head", 0, 0)
    return jnp.sum(shares, axis=0).astype(jnp.bfloat16)


def solution(mesh):
    in_specs = (
        P("ctx", "head", None),
        P("ctx", None, "head", None),
        P("ctx", None, "head", None),
        P("ctx", None, "head"),
        P("ctx", "head"),
        P("head", None),
        P("head", None),
    )
    out_specs = P(("ctx", "head"), None)
    return jax.shard_map(
        per_device, mesh=mesh, in_specs=in_specs, out_specs=out_specs, check_vma=False
    )
```

```python
import functools

import jax
import jax.numpy as jnp
from jax import lax
from jax.experimental import pallas as pl
from jax.experimental.pallas import tpu as pltpu
from jax.sharding import PartitionSpec as P

F32 = jnp.float32
BF16 = jnp.bfloat16
GROUP = 8


def dims(left_dim, right_dim):
    return (((left_dim,), (right_dim,)), ((), ()))


def halves(value):
    high = value.astype(BF16)
    return high, (value - high.astype(F32)).astype(BF16)


def dot_halves(left, right, left_dim=1, right_dim=0):
    mul = functools.partial(
        lax.dot_general, dimension_numbers=dims(left_dim, right_dim), preferred_element_type=F32
    )
    return mul(left[0], right[0]) + (mul(left[0], right[1]) + mul(left[1], right[0]))


def dot(left, right, left_dim=1, right_dim=0):
    return dot_halves(halves(left), halves(right), left_dim, right_dim)


def unit_rows(rows):
    return rows * lax.rsqrt(jnp.sum(rows * rows, axis=-1, keepdims=True) + 1e-06)


def iota(shape, dim):
    return lax.broadcasted_iota(jnp.int32, shape, dim)


def cumulative(decay_ref, decay_t_ref, rows, tokens):
    up_to = jnp.where(iota((rows, tokens), 0) // 2 >= iota((rows, tokens), 1), 1.0, 0.0).astype(BF16)
    first, rest = halves(decay_ref[...])
    third = (decay_ref[...] - first.astype(F32) - rest.astype(F32)).astype(BF16)
    mul = functools.partial(lax.dot_general, preferred_element_type=F32)
    down = sum(mul(up_to, part, dimension_numbers=dims(1, 0)) for part in (third, rest, first))
    first_t, rest_t = halves(decay_t_ref[...])
    third_t = (decay_t_ref[...] - first_t.astype(F32) - rest_t.astype(F32)).astype(BF16)
    along = sum(mul(part, up_to, dimension_numbers=dims(1, 1)) for part in (third_t, rest_t, first_t))
    return down, along


def stack_rows(part, count):
    return jnp.concatenate([part] * count, axis=0)


def inverse_blocks(lowers, stop):
    size = lowers[0].shape[0]
    width = 8
    lane = iota((width, size), 1)
    row = iota((width, size), 0)
    col = lane % width
    packed = []
    for lower in lowers:
        part = jnp.zeros((width, size), F32)
        for block in range(size // width):
            part = jnp.where(lane // width == block, lower[block * width : (block + 1) * width], part)
        packed.append(part)
    same = iota((size, size), 0) // width == iota((size, size), 1) // width
    eye = jnp.where(row == col, 1.0, 0.0).astype(F32)
    inverses = [eye - jnp.where(row // 2 == col // 2, part, 0.0) for part in packed]
    for step in (2, 4):
        below = (row // (2 * step) == col // (2 * step)) & (row // step != col // step)
        corners = [jnp.where(below, part, 0.0) for part in packed]
        count = size // width
        inner = [dot(c, jnp.where(same, stack_rows(t, count), 0.0)) for c, t in zip(corners, inverses)]
        inverses = [
            t - dot(t, jnp.where(same, stack_rows(y, count), 0.0)) for t, y in zip(inverses, inner)
        ]
    while width < stop:
        count = size // width
        lane = iota((width, size), 1) // width
        even = lane % 2 == 0
        rows = iota((size, size), 0) // width
        cols = iota((size, size), 1) // width
        same = rows == cols
        below = (rows == cols + 1) & (cols % 2 == 0)
        corners = []
        for lower in lowers:
            part = jnp.zeros((width, size), F32)
            for block in range(0, count, 2):
                part = jnp.where(lane == block, lower[(block + 1) * width : (block + 2) * width], part)
            corners.append(part)
        inner = [dot(c, jnp.where(same, stack_rows(t, count), 0.0)) for c, t in zip(corners, inverses)]
        outer = [dot(t, jnp.where(below, stack_rows(y, count), 0.0)) for t, y in zip(inverses, inner)]
        inverses = [
            jnp.concatenate([jnp.where(even, t, 0.0), jnp.where(even, -e, t)], axis=0)
            for t, e in zip(inverses, outer)
        ]
        width *= 2
    return inverses


def local_kernel(heads, k_ref, v_ref, beta_ref, decay_ref, decay_t_ref, msg_ref, solved_ref):
    rows = k_ref.shape[0]
    width = k_ref.shape[1] // heads
    half = rows // 2
    quarter = width * heads // GROUP
    cumul_rows, cumul_line = cumulative(decay_ref, decay_t_ref, rows, rows // 2)
    row_ids = iota((rows, rows), 0)
    col_ids = iota((rows, rows), 1)
    eye_k = jnp.where(iota((width, width), 0) == iota((width, width), 1), 1.0, 0.0).astype(F32)
    keys, lowers = [], []
    for head in range(heads):
        unit = unit_rows(k_ref[:, head * width : (head + 1) * width].astype(F32))
        cumul = cumul_rows[:, head : head + 1]
        line = cumul_line[head : head + 1, :]
        weight = jnp.exp(jnp.where(row_ids > col_ids, cumul - line, -1e30))
        parts = halves(unit)
        lowers.append(beta_ref[:, head : head + 1] * weight * dot_halves(parts, parts, 1, 1))
        keys.append(unit)
    inverses = inverse_blocks(lowers, half)
    rights = []
    for head in range(heads):
        beta = beta_ref[:, head : head + 1]
        value = v_ref[:, head * width : (head + 1) * width].astype(F32)
        pull = beta * jnp.exp(cumul_rows[:, head : head + 1])
        rights.append(jnp.concatenate([beta * value, pull * keys[head]], axis=1))
    uppers = [dot(inverse[:, :half], right[:half]) for inverse, right in zip(inverses, rights)]
    moved = [
        right[half:] - dot(lower[half:, :half], upper)
        for lower, right, upper in zip(lowers, rights, uppers)
    ]
    unders = [dot(inverse[:, half:], rest) for inverse, rest in zip(inverses, moved)]
    for head in range(heads):
        solved = jnp.concatenate([uppers[head], unders[head]], axis=0)
        solved_ref[head] = solved
        cumul = cumul_rows[:, head : head + 1]
        last = cumul[rows - 1 : rows, :]
        tail = jnp.exp(last - cumul) * keys[head]
        pair = dot(solved, tail, 0, 0)
        carry = jnp.exp(last) * eye_k - pair[width:]
        for part in range(GROUP // heads):
            member = head * (GROUP // heads) + part
            msg_ref[member, :width, :] = carry
            msg_ref[member, width:, :] = pair[part * quarter : (part + 1) * quarter]


def own_kernel(heads, q_ref, k_ref, decay_ref, decay_t_ref, solved_ref, own_ref, through_ref):
    tokens = q_ref.shape[0]
    rows = k_ref.shape[0]
    width = k_ref.shape[1] // heads
    cumul_rows, cumul_line = cumulative(decay_ref, decay_t_ref, rows, tokens)
    up_to = jnp.where(iota((tokens, tokens), 0) >= iota((tokens, tokens), 1), 1.0, 0.0).astype(BF16)
    first, rest = halves(decay_ref[...])
    third = (decay_ref[...] - first.astype(F32) - rest.astype(F32)).astype(BF16)
    cumul_toks = sum(jnp.dot(up_to, part, preferred_element_type=F32) for part in (third, rest, first))
    reached = iota((tokens, rows), 0) >= iota((tokens, rows), 1) // 2
    for head in range(heads):
        lanes = slice(head * width, (head + 1) * width)
        keys = unit_rows(k_ref[:, lanes].astype(F32))
        query = unit_rows(q_ref[:, lanes].astype(F32))
        cumul = cumul_toks[:, head : head + 1]
        weight = jnp.exp(jnp.where(reached, cumul - cumul_line[head : head + 1, :], -1e30))
        mixed = dot(dot(query, keys, 1, 1) * weight, solved_ref[head])
        own_ref[:, lanes] = mixed[:, :width]
        through_ref[:, lanes] = jnp.exp(cumul) * query - mixed[:, width:]


def compose(earlier, later, width):
    both = dot(earlier, later[:width])
    return jnp.concatenate([both[:width], both[width:] + later[width:]], axis=0)


def group_kernel(width, parts_ref, prefix_ref, total_ref):
    count = parts_ref.shape[0]
    runs = [parts_ref[i] for i in range(count)]
    step = 1
    while step < count:
        for start in range(step, count, 2 * step):
            for i in range(start, start + step):
                runs[i] = compose(runs[start - 1], runs[i], width)
        step *= 2
    for i in range(count - 1):
        prefix_ref[i] = runs[i]
    total_ref[...] = runs[count - 1]


def pair_kernel(width, pair_ref, total_ref):
    total_ref[...] = compose(pair_ref[0], pair_ref[1], width)


def write_kernel(width, pair_ref, write_ref):
    write_ref[...] = dot(pair_ref[0, width:], pair_ref[1, :width]) + pair_ref[1, width:]


def start_kernel(width, place_ref, pair_ref, quad_ref, far_ref, prefix_ref, state_ref):
    place = place_ref[0]
    state = jnp.where(place >= 4, far_ref[0], 0.0)
    moved = dot(state, quad_ref[0, :width]) + quad_ref[0, width:]
    state = jnp.where((place // 2) % 2 == 1, moved, state)
    moved = dot(state, pair_ref[0, :width]) + pair_ref[0, width:]
    state = jnp.where(place % 2 == 1, moved, state)
    state_ref[0] = state
    parts = halves(state)
    for i in range(prefix_ref.shape[0]):
        state_ref[i + 1] = dot_halves(parts, halves(prefix_ref[i, :width])) + prefix_ref[i, width:]


def output_kernel(heads, spread, core_ref, own_ref, through_ref, state_ref, gain_ref, weight_ref, send_ref, keep_ref):
    width = own_ref.shape[1] // heads
    tokens = own_ref.shape[0]
    hidden = []
    for head in range(heads):
        lanes = slice(head * width, (head + 1) * width)
        outputs = own_ref[:, lanes] + dot(through_ref[:, lanes], state_ref[head], 1, 1)
        scale = lax.rsqrt(jnp.mean(outputs * outputs, axis=-1, keepdims=True) + 1e-05)
        hidden.append(outputs * scale * gain_ref[head : head + 1, :])
    hidden = jnp.concatenate(hidden, axis=1)
    share = tokens // spread
    first = jnp.concatenate([hidden[i * share : (i + 1) * share] for i in range(0, spread, 2)], axis=0)
    second = jnp.concatenate([hidden[i * share : (i + 1) * share] for i in range(1, spread, 2)], axis=0)
    on_first = core_ref[0] == 0
    keep_ref[...] = jnp.where(on_first, first, second).astype(BF16)
    send = jnp.where(on_first, second, first).astype(BF16)
    send_ref[...] = jnp.dot(send, weight_ref[...], preferred_element_type=F32)


def keep_kernel(keep_ref, weight_ref, out_ref):
    out_ref[...] = jnp.dot(keep_ref[...], weight_ref[...], preferred_element_type=F32)


def add_kernel(left_ref, right_ref, out_ref):
    out_ref[...] = left_ref[...] + right_ref[...]


def per_device(queries, key_rows, value_rows, strengths, log_decay, norm_gain, out_weight):
    tokens, heads, width = queries.shape
    rows = 2 * tokens
    columns = out_weight.shape[1]
    ctx = lax.axis_size("ctx")
    spread = lax.axis_size("head")
    part_rows = width + width * heads // GROUP
    params = pltpu.CompilerParams(vmem_limit_bytes=48 * 1024 * 1024)

    def call(body, out_shape, name, flops=0, in_specs=None):
        extra = {} if in_specs is None else dict(in_specs=in_specs)
        return pl.pallas_call(
            body,
            out_shape=out_shape,
            compiler_params=params,
            name=name,
            cost_estimate=pl.CostEstimate(flops=flops, bytes_accessed=1 << 20, transcendentals=0),
            **extra,
        )

    def array(*shape):
        return jax.ShapeDtypeStruct(shape, F32)

    def pairs(flip):
        return [[i, i ^ flip] for i in range(ctx) if i < i ^ flip]

    smem = pl.BlockSpec(memory_space=pltpu.SMEM)
    vmem = pl.BlockSpec(memory_space=pltpu.VMEM)
    inner = [[g * GROUP + j for j in range(GROUP)] for g in range(ctx // GROUP)]

    query = queries.reshape(tokens, heads * width)
    keys = key_rows.reshape(rows, heads * width)
    decay_t = jnp.concatenate([log_decay.T, jnp.zeros((8 - heads, tokens), F32)], axis=0)
    msg, solved = call(
        functools.partial(local_kernel, heads),
        (array(GROUP, part_rows, width), array(heads, rows, 2 * width)),
        "local_chunk",
    )(
        keys,
        value_rows.reshape(rows, heads * width),
        strengths.reshape(rows, heads),
        log_decay,
        decay_t,
    )
    parts = lax.all_to_all(msg, "ctx", 0, 0, axis_index_groups=inner)
    own, through = call(
        functools.partial(own_kernel, heads),
        (array(tokens, heads * width), array(tokens, heads * width)),
        "own_outputs",
        flops=4 * 10**9,
    )(query, keys, log_decay, decay_t, solved)
    prefix, total = call(
        functools.partial(group_kernel, width),
        (array(GROUP - 1, part_rows, width), array(part_rows, width)),
        "group_scan",
    )(parts)
    pair = lax.all_gather(total, "ctx", axis_index_groups=pairs(8))
    total = call(functools.partial(pair_kernel, width), array(part_rows, width), "pair_total")(pair)
    quad = lax.all_gather(total, "ctx", axis_index_groups=pairs(16))
    write = call(
        functools.partial(write_kernel, width), array(part_rows - width, width), "half_write"
    )(quad)
    far = lax.all_gather(write, "ctx", axis_index_groups=pairs(48))
    place = (lax.axis_index("ctx") // GROUP).astype(jnp.int32).reshape(1)
    starts = call(
        functools.partial(start_kernel, width),
        array(GROUP, part_rows - width, width),
        "start_states",
        in_specs=[smem, vmem, vmem, vmem, vmem],
    )(place, pair, quad, far, prefix)
    states = lax.all_to_all(starts, "ctx", 0, 0, axis_index_groups=inner)
    core = (lax.axis_index("head") % 2).astype(jnp.int32).reshape(1)
    send, keep = call(
        functools.partial(output_kernel, heads, spread),
        (array(tokens // 2, columns), jax.ShapeDtypeStruct((tokens // 2, heads * width), BF16)),
        "project_send",
        in_specs=[smem, vmem, vmem, vmem, vmem, vmem],
    )(core, own, through, states.reshape(heads, width, width), norm_gain, out_weight)
    arrived = lax.ppermute(send, "head", [(i, i ^ 1) for i in range(spread)])
    kept = call(keep_kernel, array(tokens // 2, columns), "project_keep", flops=10**8)(keep, out_weight)
    sums = call(add_kernel, array(tokens // 2, columns), "add_cores")(kept, arrived)
    ring = [[i * 2 + c for i in range(spread // 2)] for c in range(2)]
    shares = lax.all_to_all(
        sums.reshape(spread // 2, tokens // spread, columns), "head", 0, 0, axis_index_groups=ring
    )
    return jnp.sum(shares, axis=0).astype(BF16)


def solution(mesh):
    in_specs = (
        P("ctx", "head", None),
        P("ctx", None, "head", None),
        P("ctx", None, "head", None),
        P("ctx", None, "head"),
        P("ctx", "head"),
        P("head", None),
        P("head", None),
    )
    out_specs = P(("ctx", "head"), None)
    return jax.shard_map(
        per_device, mesh=mesh, in_specs=in_specs, out_specs=out_specs, check_vma=False
    )
```

```python
import functools

import jax
import jax.numpy as jnp
from jax import lax
from jax.experimental import pallas as pl
from jax.experimental.pallas import tpu as pltpu
from jax.sharding import PartitionSpec as P

F32 = jnp.float32
BF16 = jnp.bfloat16
GROUP = 8


def dims(left_dim, right_dim):
    return (((left_dim,), (right_dim,)), ((), ()))


def halves(value):
    high = value.astype(BF16)
    return high, (value - high.astype(F32)).astype(BF16)


def dot_halves(left, right, left_dim=1, right_dim=0):
    mul = functools.partial(
        lax.dot_general, dimension_numbers=dims(left_dim, right_dim), preferred_element_type=F32
    )
    return mul(left[0], right[0]) + (mul(left[0], right[1]) + mul(left[1], right[0]))


def dot(left, right, left_dim=1, right_dim=0):
    return dot_halves(halves(left), halves(right), left_dim, right_dim)


def unit_rows(rows):
    return rows * lax.rsqrt(jnp.sum(rows * rows, axis=-1, keepdims=True) + 1e-06)


def iota(shape, dim):
    return lax.broadcasted_iota(jnp.int32, shape, dim)


def thirds(value):
    high, rest = halves(value)
    last = (value - high.astype(F32) - rest.astype(F32)).astype(BF16)
    return jnp.concatenate([last.astype(F32), rest.astype(F32), high.astype(F32)], axis=0).astype(BF16)


def picked(mask, small):
    wide = lax.dot_general(
        jnp.where(mask, 1.0, 0.0).astype(BF16), small, dims(1, 1), preferred_element_type=F32
    )
    return wide[:, :8] + wide[:, 8:16] + wide[:, 16:24]


def picked_line(small, mask):
    wide = lax.dot_general(
        small, jnp.where(mask, 1.0, 0.0).astype(BF16), dims(1, 1), preferred_element_type=F32
    )
    return wide[:8] + wide[8:16] + wide[16:24]


def stack_rows(part, count):
    return jnp.concatenate([part] * count, axis=0)


def inverse_blocks(lowers, stop):
    size = lowers[0].shape[0]
    width = 8
    lane = iota((width, size), 1)
    row = iota((width, size), 0)
    col = lane % width
    packed = []
    for lower in lowers:
        part = jnp.zeros((width, size), F32)
        for block in range(size // width):
            part = jnp.where(lane // width == block, lower[block * width : (block + 1) * width], part)
        packed.append(part)
    same = iota((size, size), 0) // width == iota((size, size), 1) // width
    eye = jnp.where(row == col, 1.0, 0.0).astype(F32)
    inverses = [eye - jnp.where(row // 2 == col // 2, part, 0.0) for part in packed]
    for step in (2, 4):
        below = (row // (2 * step) == col // (2 * step)) & (row // step != col // step)
        corners = [jnp.where(below, part, 0.0) for part in packed]
        count = size // width
        inner = [dot(c, jnp.where(same, stack_rows(t, count), 0.0)) for c, t in zip(corners, inverses)]
        inverses = [
            t - dot(t, jnp.where(same, stack_rows(y, count), 0.0)) for t, y in zip(inverses, inner)
        ]
    while width < stop:
        count = size // width
        lane = iota((width, size), 1) // width
        even = lane % 2 == 0
        rows = iota((size, size), 0) // width
        cols = iota((size, size), 1) // width
        same = rows == cols
        below = (rows == cols + 1) & (cols % 2 == 0)
        corners = []
        for lower in lowers:
            part = jnp.zeros((width, size), F32)
            for block in range(0, count, 2):
                part = jnp.where(lane == block, lower[(block + 1) * width : (block + 2) * width], part)
            corners.append(part)
        inner = [dot(c, jnp.where(same, stack_rows(t, count), 0.0)) for c, t in zip(corners, inverses)]
        outer = [dot(t, jnp.where(below, stack_rows(y, count), 0.0)) for t, y in zip(inverses, inner)]
        inverses = [
            jnp.concatenate([jnp.where(even, t, 0.0), jnp.where(even, -e, t)], axis=0)
            for t, e in zip(inverses, outer)
        ]
        width *= 2
    return inverses


def local_kernel(heads, k_ref, v_ref, small_ref, msg_ref, solved_ref, keys_ref, spread_k, spread_v):
    rows = k_ref.shape[0] // heads
    tokens = rows // 2
    width = k_ref.shape[1]
    half = rows // 2
    quarter = width * heads // GROUP
    spread_k[...] = unit_rows(k_ref[...].astype(F32))
    spread_v[...] = v_ref[...].astype(F32)
    small = thirds(small_ref[...])
    row_tok = iota((rows, tokens), 0) // 2
    tok = iota((rows, tokens), 1)
    cumul_rows = picked(row_tok >= tok, small)
    cumul_line = picked_line(small, row_tok >= tok)
    betas = picked(row_tok == tok, small)
    first = iota((rows, 1), 0) % 2 == 0
    row_ids = iota((rows, rows), 0)
    col_ids = iota((rows, rows), 1)
    eye_k = jnp.where(iota((width, width), 0) == iota((width, width), 1), 1.0, 0.0).astype(F32)
    keys, lowers, strength, values = [], [], [], []
    for head in range(heads):
        unit = spread_k[pl.ds(head, rows, stride=heads), :]
        values.append(spread_v[pl.ds(head, rows, stride=heads), :])
        beta = jnp.where(
            first, betas[:, heads + head : heads + head + 1], betas[:, 2 * heads + head : 2 * heads + head + 1]
        )
        cumul = cumul_rows[:, head : head + 1]
        line = cumul_line[head : head + 1, :]
        weight = jnp.exp(jnp.where(row_ids > col_ids, cumul - line, -1e30))
        parts = halves(unit)
        lowers.append(beta * weight * dot_halves(parts, parts, 1, 1))
        keys.append(unit)
        strength.append(beta)
        keys_ref[head] = unit
    inverses = inverse_blocks(lowers, half)
    rights = [
        jnp.concatenate([beta * value, (beta * jnp.exp(cumul_rows[:, head : head + 1])) * unit], axis=1)
        for head, (beta, value, unit) in enumerate(zip(strength, values, keys))
    ]
    uppers = [dot(inverse[:, :half], right[:half]) for inverse, right in zip(inverses, rights)]
    moved = [
        right[half:] - dot(lower[half:, :half], upper)
        for lower, right, upper in zip(lowers, rights, uppers)
    ]
    unders = [dot(inverse[:, half:], rest) for inverse, rest in zip(inverses, moved)]
    for head in range(heads):
        solved = jnp.concatenate([uppers[head], unders[head]], axis=0)
        solved_ref[head] = solved
        cumul = cumul_rows[:, head : head + 1]
        last = cumul[rows - 1 : rows, :]
        tail = jnp.exp(last - cumul) * keys[head]
        pair = dot(solved, tail, 0, 0)
        carry = jnp.exp(last) * eye_k - pair[width:]
        for part in range(GROUP // heads):
            member = head * (GROUP // heads) + part
            msg_ref[member, :width, :] = carry
            msg_ref[member, width:, :] = pair[part * quarter : (part + 1) * quarter]


def own_kernel(heads, q_ref, keys_ref, small_ref, solved_ref, own_ref, through_ref, spread_q):
    tokens = q_ref.shape[0] // heads
    rows = keys_ref.shape[1]
    spread_q[...] = unit_rows(q_ref[...].astype(F32))
    small = thirds(small_ref[...])
    reached = iota((rows, tokens), 0) // 2 >= iota((rows, tokens), 1)
    cumul_line = picked_line(small, reached)
    cumul_toks = picked(iota((tokens, tokens), 0) >= iota((tokens, tokens), 1), small)
    reached = iota((tokens, rows), 0) >= iota((tokens, rows), 1) // 2
    width = keys_ref.shape[2]
    for head in range(heads):
        lanes = slice(head * width, (head + 1) * width)
        query = spread_q[pl.ds(head, tokens, stride=heads), :]
        cumul = cumul_toks[:, head : head + 1]
        weight = jnp.exp(jnp.where(reached, cumul - cumul_line[head : head + 1, :], -1e30))
        mixed = dot(dot(query, keys_ref[head], 1, 1) * weight, solved_ref[head])
        own_ref[:, lanes] = mixed[:, :width]
        through_ref[:, lanes] = jnp.exp(cumul) * query - mixed[:, width:]


def widen_kernel(in_ref, out_ref):
    out_ref[...] = in_ref[...].astype(F32)


def weight_kernel(core_ref, own_ref, other_ref, both_ref):
    rows = own_ref.shape[0]
    other = other_ref[...].astype(BF16)
    on_first = core_ref[0] == 0

    @pl.when(on_first)
    def _():
        both_ref[:rows] = own_ref[...]
        both_ref[rows:] = other

    @pl.when(jnp.logical_not(on_first))
    def _():
        both_ref[:rows] = other
        both_ref[rows:] = own_ref[...]


def compose(earlier, later, width):
    both = dot(earlier, later[:width])
    return jnp.concatenate([both[:width], both[width:] + later[width:]], axis=0)


def group_kernel(width, parts_ref, prefix_ref, total_ref):
    count = parts_ref.shape[0]
    runs = [parts_ref[i] for i in range(count)]
    step = 1
    while step < count:
        for start in range(step, count, 2 * step):
            for i in range(start, start + step):
                runs[i] = compose(runs[start - 1], runs[i], width)
        step *= 2
    for i in range(count - 1):
        prefix_ref[i] = runs[i]
    total_ref[...] = runs[count - 1]


def pair_kernel(width, pair_ref, total_ref):
    total_ref[...] = compose(pair_ref[0], pair_ref[1], width)


def write_kernel(width, pair_ref, write_ref):
    write_ref[...] = dot(pair_ref[0, width:], pair_ref[1, :width]) + pair_ref[1, width:]


def start_kernel(width, place_ref, pair_ref, quad_ref, far_ref, prefix_ref, state_ref):
    place = place_ref[0]
    state = jnp.where(place >= 4, far_ref[0], 0.0)
    moved = dot(state, quad_ref[0, :width]) + quad_ref[0, width:]
    state = jnp.where((place // 2) % 2 == 1, moved, state)
    moved = dot(state, pair_ref[0, :width]) + pair_ref[0, width:]
    state = jnp.where(place % 2 == 1, moved, state)
    state_ref[0] = state
    parts = halves(state)
    for i in range(prefix_ref.shape[0]):
        state_ref[i + 1] = dot_halves(parts, halves(prefix_ref[i, :width])) + prefix_ref[i, width:]


def hidden_kernel(heads, own_ref, through_ref, state_ref, gain_ref, hidden_ref):
    width = own_ref.shape[1] // heads
    for head in range(heads):
        lanes = slice(head * width, (head + 1) * width)
        outputs = own_ref[:, lanes] + dot(through_ref[:, lanes], state_ref[head], 1, 1)
        scale = lax.rsqrt(jnp.mean(outputs * outputs, axis=-1, keepdims=True) + 1e-05)
        scaled = outputs * scale * gain_ref[head : head + 1, :]
        hidden_ref[:, lanes] = scaled.astype(BF16).astype(F32)


def project_kernel(spread, core_ref, hidden_ref, weight_ref, out_ref):
    share = hidden_ref.shape[1] // spread
    kept = []
    for i in range(0, spread, 2):
        even = jnp.concatenate([hidden_ref[c, i * share : (i + 1) * share] for c in range(2)], axis=1)
        odd = jnp.concatenate([hidden_ref[c, (i + 1) * share : (i + 2) * share] for c in range(2)], axis=1)
        kept.append(jnp.where(core_ref[0] == 0, even, odd))
    kept = jnp.concatenate(kept, axis=0).astype(BF16)
    out_ref[...] = jnp.dot(kept, weight_ref[...], preferred_element_type=F32)


def per_device(queries, key_rows, value_rows, strengths, log_decay, norm_gain, out_weight):
    tokens, heads, width = queries.shape
    rows = 2 * tokens
    columns = out_weight.shape[1]
    ctx = lax.axis_size("ctx")
    spread = lax.axis_size("head")
    part_rows = width + width * heads // GROUP
    params = pltpu.CompilerParams(vmem_limit_bytes=48 * 1024 * 1024)

    def call(body, out_shape, name, flops=0, in_specs=None, scratch=()):
        extra = {} if in_specs is None else dict(in_specs=in_specs)
        return pl.pallas_call(
            body,
            out_shape=out_shape,
            compiler_params=params,
            name=name,
            cost_estimate=pl.CostEstimate(flops=flops, bytes_accessed=1 << 20, transcendentals=0),
            scratch_shapes=scratch,
            **extra,
        )

    def array(*shape, dtype=F32):
        return jax.ShapeDtypeStruct(shape, dtype)

    def pairs(flip):
        return [[i, i ^ flip] for i in range(ctx) if i < i ^ flip]

    smem = pl.BlockSpec(memory_space=pltpu.SMEM)
    vmem = pl.BlockSpec(memory_space=pltpu.VMEM)
    inner = [[g * GROUP + j for j in range(GROUP)] for g in range(ctx // GROUP)]
    cores = [[i, i + 1] for i in range(0, spread, 2)]
    core = (lax.axis_index("head") % 2).astype(jnp.int32).reshape(1)

    small = jnp.concatenate(
        [
            log_decay.T,
            strengths.transpose(1, 2, 0).reshape(2 * heads, tokens),
            jnp.zeros((8 - 3 * heads, tokens), F32),
        ],
        axis=0,
    )
    msg, solved, keys = call(
        functools.partial(local_kernel, heads),
        (array(GROUP, part_rows, width), array(heads, rows, 2 * width), array(heads, rows, width)),
        "local_chunk",
        scratch=[pltpu.VMEM((heads * rows, width), F32)] * 2,
    )(key_rows.reshape(heads * rows, width), value_rows.reshape(heads * rows, width), small)
    parts = lax.all_to_all(msg, "ctx", 0, 0, axis_index_groups=inner)
    late_weight, _ = lax.optimization_barrier((out_weight, solved))
    wide = call(widen_kernel, array(*out_weight.shape), "widen", flops=10**9)(late_weight)
    other = lax.ppermute(wide, "head", [(i, i ^ 1) for i in range(spread)])
    both = call(
        weight_kernel,
        array(2 * out_weight.shape[0], columns, dtype=BF16),
        "chip_weight",
        flops=10**9,
        in_specs=[smem, vmem, vmem],
    )(core, late_weight, other)
    own, through = call(
        functools.partial(own_kernel, heads),
        (array(tokens, heads * width), array(tokens, heads * width)),
        "own_outputs",
        flops=4 * 10**9,
        scratch=[pltpu.VMEM((heads * tokens, width), F32)],
    )(queries.reshape(heads * tokens, width), keys, small, solved)
    prefix, total = call(
        functools.partial(group_kernel, width),
        (array(GROUP - 1, part_rows, width), array(part_rows, width)),
        "group_scan",
    )(parts)
    pair = lax.all_gather(total, "ctx", axis_index_groups=pairs(8))
    total = call(functools.partial(pair_kernel, width), array(part_rows, width), "pair_total")(pair)
    quad = lax.all_gather(total, "ctx", axis_index_groups=pairs(16))
    write = call(
        functools.partial(write_kernel, width), array(part_rows - width, width), "half_write"
    )(quad)
    far = lax.all_gather(write, "ctx", axis_index_groups=pairs(48))
    place = (lax.axis_index("ctx") // GROUP).astype(jnp.int32).reshape(1)
    starts = call(
        functools.partial(start_kernel, width),
        array(GROUP, part_rows - width, width),
        "start_states",
        in_specs=[smem, vmem, vmem, vmem, vmem],
    )(place, pair, quad, far, prefix)
    states = lax.all_to_all(starts, "ctx", 0, 0, axis_index_groups=inner)
    hidden = call(
        functools.partial(hidden_kernel, heads), array(tokens, heads * width), "hidden"
    )(own, through, states.reshape(heads, width, width), norm_gain)
    hidden = lax.all_gather(hidden, "head", axis_index_groups=cores)
    sums = call(
        functools.partial(project_kernel, spread),
        array(tokens // 2, columns),
        "project",
        in_specs=[smem, vmem, vmem],
    )(core, hidden, both)
    ring = [[i * 2 + c for i in range(spread // 2)] for c in range(2)]
    shares = lax.all_to_all(
        sums.reshape(spread // 2, tokens // spread, columns), "head", 0, 0, axis_index_groups=ring
    )
    return jnp.sum(shares, axis=0).astype(BF16)


def solution(mesh):
    in_specs = (
        P("ctx", "head", None),
        P("ctx", None, "head", None),
        P("ctx", None, "head", None),
        P("ctx", None, "head"),
        P("ctx", "head"),
        P("head", None),
        P("head", None),
    )
    out_specs = P(("ctx", "head"), None)
    return jax.shard_map(
        per_device, mesh=mesh, in_specs=in_specs, out_specs=out_specs, check_vma=False
    )
```

```python
import functools

import jax
import jax.numpy as jnp
from jax import lax
from jax.experimental import pallas as pl
from jax.experimental.pallas import tpu as pltpu
from jax.sharding import PartitionSpec as P

F32 = jnp.float32
BF16 = jnp.bfloat16
GROUP = 8


def dims(left_dim, right_dim):
    return (((left_dim,), (right_dim,)), ((), ()))


def halves(value):
    high = value.astype(BF16)
    return high, (value - high.astype(F32)).astype(BF16)


def dot_halves(left, right, left_dim=1, right_dim=0):
    mul = functools.partial(
        lax.dot_general, dimension_numbers=dims(left_dim, right_dim), preferred_element_type=F32
    )
    if left_dim == 0:
        return mul(left[0], right[0]) + (mul(left[0], right[1]) + mul(left[1], right[0]))
    count = left[0].shape[0]
    both = mul(jnp.concatenate(left, axis=0), right[0])
    return both[:count] + (both[count:] + mul(left[0], right[1]))


def dot(left, right, left_dim=1, right_dim=0):
    return dot_halves(halves(left), halves(right), left_dim, right_dim)


def unit_rows(rows):
    return rows * lax.rsqrt(jnp.sum(rows * rows, axis=-1, keepdims=True) + 1e-06)


def iota(shape, dim):
    return lax.broadcasted_iota(jnp.int32, shape, dim)


def thirds(value):
    high, rest = halves(value)
    last = (value - high.astype(F32) - rest.astype(F32)).astype(BF16)
    return jnp.concatenate([last.astype(F32), rest.astype(F32), high.astype(F32)], axis=0).astype(BF16)


def picked(mask, small):
    wide = lax.dot_general(
        jnp.where(mask, 1.0, 0.0).astype(BF16), small, dims(1, 1), preferred_element_type=F32
    )
    return wide[:, :8] + wide[:, 8:16] + wide[:, 16:24]


def picked_line(small, mask):
    wide = lax.dot_general(
        small, jnp.where(mask, 1.0, 0.0).astype(BF16), dims(1, 1), preferred_element_type=F32
    )
    return wide[:8] + wide[8:16] + wide[16:24]


def blocks_of(part, count, mask):
    if part.shape[0] % 16:
        part, count = jnp.concatenate([part, part], axis=0), count // 2
    return tuple(jnp.concatenate([piece] * count, axis=0) * mask for piece in halves(part))


def inverse_blocks(lowers, stop):
    size = lowers[0].shape[0]
    width = 8
    lane = iota((width, size), 1)
    row = iota((width, size), 0)
    col = lane % width
    rows = iota((size, size), 0)
    cols = iota((size, size), 1)
    packed = []
    for lower in lowers:
        part = jnp.zeros((width, size), F32)
        for block in range(size // width):
            part = jnp.where(lane // width == block, lower[block * width : (block + 1) * width], part)
        packed.append(part)
    same = jnp.where(rows // width == cols // width, 1.0, 0.0).astype(BF16)
    eye = jnp.where(row == col, 1.0, 0.0).astype(F32)
    inverses = [eye - jnp.where(row // 2 == col // 2, part, 0.0) for part in packed]
    count = size // width
    for step in (2, 4):
        below = (row // (2 * step) == col // (2 * step)) & (row // step != col // step)
        corners = [halves(jnp.where(below, part, 0.0)) for part in packed]
        inner = [dot_halves(c, blocks_of(t, count, same)) for c, t in zip(corners, inverses)]
        inverses = [
            t - dot_halves(halves(t), blocks_of(y, count, same)) for t, y in zip(inverses, inner)
        ]
    while width < stop:
        count = size // width
        lane = iota((width, size), 1) // width
        even = lane % 2 == 0
        same = jnp.where(rows // width == cols // width, 1.0, 0.0).astype(BF16)
        below = jnp.where((rows // width == cols // width + 1) & ((cols // width) % 2 == 0), 1.0, 0.0).astype(BF16)
        corners = []
        for lower in lowers:
            part = jnp.zeros((width, size), F32)
            for block in range(0, count, 2):
                part = jnp.where(lane == block, lower[(block + 1) * width : (block + 2) * width], part)
            corners.append(halves(part))
        inner = [dot_halves(c, blocks_of(t, count, same)) for c, t in zip(corners, inverses)]
        outer = [dot_halves(halves(t), blocks_of(y, count, below)) for t, y in zip(inverses, inner)]
        inverses = [
            jnp.concatenate([jnp.where(even, t, 0.0), jnp.where(even, -e, t)], axis=0)
            for t, e in zip(inverses, outer)
        ]
        width *= 2
    return inverses


def local_kernel(
    heads, k_hbm, v_hbm, decay_hbm, beta_hbm, msg_hbm, solved_hbm, keys_hbm,
    k_ref, v_ref, small_ref, spread_k, spread_v, keys_ref, solved_ref, carry_ref, write_ref, in_sems, out_sems,
):
    rows = k_ref.shape[0] // heads
    tokens = rows // 2
    width = k_ref.shape[1]
    half = rows // 2
    quarter = width * heads // GROUP
    sends = []

    def send(source, target):
        sends.append(pltpu.make_async_copy(source, target, out_sems.at[len(sends)]))
        sends[-1].start()

    small_ref[3 * heads :] = jnp.zeros((8 - 3 * heads, tokens), F32)
    fetches = [
        pltpu.make_async_copy(source, target, in_sems.at[i])
        for i, (source, target) in enumerate(
            (
                (k_hbm, k_ref),
                (decay_hbm, small_ref.at[:heads]),
                (beta_hbm, small_ref.at[heads : 3 * heads]),
                (v_hbm, v_ref),
            )
        )
    ]
    for fetch in fetches:
        fetch.start()
    row_tok = iota((rows, tokens), 0) // 2
    tok = iota((rows, tokens), 1)
    first = iota((rows, 1), 0) % 2 == 0
    row_ids = iota((rows, rows), 0)
    col_ids = iota((rows, rows), 1)
    eye_k = jnp.where(iota((width, width), 0) == iota((width, width), 1), 1.0, 0.0).astype(F32)
    for fetch in fetches[:3]:
        fetch.wait()
    small = thirds(small_ref[...])
    cumul_rows = picked(row_tok >= tok, small)
    cumul_line = picked_line(small, row_tok >= tok)
    betas = picked(row_tok == tok, small)
    spread_k[...] = unit_rows(k_ref[...].astype(F32))
    keys, lowers, strength = [], [], []
    for head in range(heads):
        unit = spread_k[pl.ds(head, rows, stride=heads), :]
        beta = jnp.where(
            first, betas[:, heads + head : heads + head + 1], betas[:, 2 * heads + head : 2 * heads + head + 1]
        )
        cumul = cumul_rows[:, head : head + 1]
        line = cumul_line[head : head + 1, :]
        weight = jnp.exp(jnp.where(row_ids > col_ids, cumul - line, -1e30))
        parts = halves(unit)
        lowers.append(beta * weight * dot_halves(parts, parts, 1, 1))
        keys.append(unit)
        strength.append(beta)
        keys_ref[head] = unit
        send(keys_ref.at[head], keys_hbm.at[head])
    inverses = inverse_blocks(lowers, half)
    fetches[3].wait()
    spread_v[...] = v_ref[...].astype(F32)
    rights = [
        jnp.concatenate(
            [
                strength[head] * spread_v[pl.ds(head, rows, stride=heads), :],
                (strength[head] * jnp.exp(cumul_rows[:, head : head + 1])) * keys[head],
            ],
            axis=1,
        )
        for head in range(heads)
    ]
    uppers = [dot(inverse[:, :half], right[:half]) for inverse, right in zip(inverses, rights)]
    moved = [
        right[half:] - dot(lower[half:, :half], upper)
        for lower, right, upper in zip(lowers, rights, uppers)
    ]
    unders = [dot(inverse[:, half:], rest) for inverse, rest in zip(inverses, moved)]
    for head in range(heads):
        solved = jnp.concatenate([uppers[head], unders[head]], axis=0)
        solved_ref[head] = solved
        send(solved_ref.at[head], solved_hbm.at[head])
        cumul = cumul_rows[:, head : head + 1]
        last = cumul[rows - 1 : rows, :]
        tail = jnp.exp(last - cumul) * keys[head]
        pair = dot(solved, tail, 0, 0)
        write_ref[head] = pair[:width]
        carry_ref[head] = jnp.exp(last) * eye_k - pair[width:]
        for part in range(GROUP // heads):
            member = head * (GROUP // heads) + part
            send(carry_ref.at[head], msg_hbm.at[member, :width])
            send(write_ref.at[head, part * quarter : (part + 1) * quarter], msg_hbm.at[member, width:])
    for copy in sends:
        copy.wait()


def local_call(keys, values, decay, beta):
    heads, tokens = decay.shape
    rows, width = keys.shape[0] // heads, keys.shape[1]
    any_space = pl.BlockSpec(memory_space=pl.ANY)
    return pl.pallas_call(
        functools.partial(local_kernel, heads),
        out_shape=(
            jax.ShapeDtypeStruct((GROUP, width + width * heads // GROUP, width), F32),
            jax.ShapeDtypeStruct((heads, rows, 2 * width), F32),
            jax.ShapeDtypeStruct((heads, rows, width), F32),
        ),
        in_specs=[any_space] * 4,
        out_specs=(any_space,) * 3,
        scratch_shapes=[
            pltpu.VMEM(keys.shape, BF16),
            pltpu.VMEM(values.shape, BF16),
            pltpu.VMEM((8, tokens), F32),
            pltpu.VMEM(keys.shape, F32),
            pltpu.VMEM(values.shape, F32),
            pltpu.VMEM((heads, rows, width), F32),
            pltpu.VMEM((heads, rows, 2 * width), F32),
            pltpu.VMEM((heads, width, width), F32),
            pltpu.VMEM((heads, width, width), F32),
            pltpu.SemaphoreType.DMA((4,)),
            pltpu.SemaphoreType.DMA((2 * heads + 2 * GROUP,)),
        ],
        compiler_params=pltpu.CompilerParams(vmem_limit_bytes=60 * 1024 * 1024),
        name="local_chunk",
    )(keys, values, decay, beta)


def own_kernel(heads, q_ref, keys_ref, decay_ref, solved_ref, own_ref, through_ref, spread_q):
    tokens = q_ref.shape[0] // heads
    rows = keys_ref.shape[1]
    spread_q[...] = unit_rows(q_ref[...].astype(F32))
    small = thirds(jnp.concatenate([decay_ref[...], jnp.zeros((8 - heads, tokens), F32)], axis=0))
    reached = iota((rows, tokens), 0) // 2 >= iota((rows, tokens), 1)
    cumul_line = picked_line(small, reached)
    cumul_toks = picked(iota((tokens, tokens), 0) >= iota((tokens, tokens), 1), small)
    reached = iota((tokens, rows), 0) >= iota((tokens, rows), 1) // 2
    width = keys_ref.shape[2]
    for head in range(heads):
        lanes = slice(head * width, (head + 1) * width)
        query = spread_q[pl.ds(head, tokens, stride=heads), :]
        cumul = cumul_toks[:, head : head + 1]
        weight = jnp.exp(jnp.where(reached, cumul - cumul_line[head : head + 1, :], -1e30))
        mixed = dot(dot(query, keys_ref[head], 1, 1) * weight, solved_ref[head])
        own_ref[:, lanes] = mixed[:, :width]
        through_ref[:, lanes] = jnp.exp(cumul) * query - mixed[:, width:]


def widen_kernel(in_ref, out_ref):
    out_ref[...] = in_ref[...].astype(F32)


def weight_kernel(core_ref, own_ref, other_ref, both_ref):
    rows = own_ref.shape[0]
    other = other_ref[...].astype(BF16)
    on_first = core_ref[0] == 0

    @pl.when(on_first)
    def _():
        both_ref[:rows] = own_ref[...]
        both_ref[rows:] = other

    @pl.when(jnp.logical_not(on_first))
    def _():
        both_ref[:rows] = other
        both_ref[rows:] = own_ref[...]


def compose(earlier, later, width):
    both = dot(earlier, later[:width])
    return jnp.concatenate([both[:width], both[width:] + later[width:]], axis=0)


def group_kernel(width, parts_ref, prefix_ref, total_ref):
    count = parts_ref.shape[0]
    runs = [parts_ref[i] for i in range(count)]
    step = 1
    while step < count:
        for start in range(step, count, 2 * step):
            for i in range(start, start + step):
                runs[i] = compose(runs[start - 1], runs[i], width)
        step *= 2
    for i in range(count - 1):
        prefix_ref[i] = runs[i]
    total_ref[...] = runs[count - 1]


def pair_kernel(width, pair_ref, total_ref):
    total_ref[...] = compose(pair_ref[0], pair_ref[1], width)


def write_kernel(width, pair_ref, write_ref):
    write_ref[...] = dot(pair_ref[0, width:], pair_ref[1, :width]) + pair_ref[1, width:]


def start_kernel(width, place_ref, pair_ref, quad_ref, far_ref, prefix_ref, state_ref):
    place = place_ref[0]
    state = jnp.where(place >= 4, far_ref[0], 0.0)
    moved = dot(state, quad_ref[0, :width]) + quad_ref[0, width:]
    state = jnp.where((place // 2) % 2 == 1, moved, state)
    moved = dot(state, pair_ref[0, :width]) + pair_ref[0, width:]
    state = jnp.where(place % 2 == 1, moved, state)
    state_ref[0] = state
    parts = halves(state)
    for i in range(prefix_ref.shape[0]):
        state_ref[i + 1] = dot_halves(parts, halves(prefix_ref[i, :width])) + prefix_ref[i, width:]


def hidden_kernel(heads, own_ref, through_ref, state_ref, gain_ref, hidden_ref):
    width = own_ref.shape[1] // heads
    for head in range(heads):
        lanes = slice(head * width, (head + 1) * width)
        outputs = own_ref[:, lanes] + dot(through_ref[:, lanes], state_ref[head], 1, 1)
        scale = lax.rsqrt(jnp.mean(outputs * outputs, axis=-1, keepdims=True) + 1e-05)
        scaled = outputs * scale * gain_ref[head : head + 1, :]
        hidden_ref[:, lanes] = scaled.astype(BF16).astype(F32)


def project_kernel(spread, core_ref, hidden_ref, weight_ref, out_ref):
    share = hidden_ref.shape[1] // spread
    kept = []
    for i in range(0, spread, 2):
        even = jnp.concatenate([hidden_ref[c, i * share : (i + 1) * share] for c in range(2)], axis=1)
        odd = jnp.concatenate([hidden_ref[c, (i + 1) * share : (i + 2) * share] for c in range(2)], axis=1)
        kept.append(jnp.where(core_ref[0] == 0, even, odd))
    kept = jnp.concatenate(kept, axis=0).astype(BF16)
    out_ref[...] = jnp.dot(kept, weight_ref[...], preferred_element_type=F32)


def per_device(queries, key_rows, value_rows, strengths, log_decay, norm_gain, out_weight):
    tokens, heads, width = queries.shape
    rows = 2 * tokens
    columns = out_weight.shape[1]
    ctx = lax.axis_size("ctx")
    spread = lax.axis_size("head")
    part_rows = width + width * heads // GROUP
    params = pltpu.CompilerParams(vmem_limit_bytes=48 * 1024 * 1024)

    def call(body, out_shape, name, flops=0, in_specs=None, scratch=()):
        extra = {} if in_specs is None else dict(in_specs=in_specs)
        return pl.pallas_call(
            body,
            out_shape=out_shape,
            compiler_params=params,
            name=name,
            cost_estimate=pl.CostEstimate(flops=flops, bytes_accessed=1 << 20, transcendentals=0),
            scratch_shapes=scratch,
            **extra,
        )

    def array(*shape, dtype=F32):
        return jax.ShapeDtypeStruct(shape, dtype)

    def pairs(flip):
        return [[i, i ^ flip] for i in range(ctx) if i < i ^ flip]

    smem = pl.BlockSpec(memory_space=pltpu.SMEM)
    vmem = pl.BlockSpec(memory_space=pltpu.VMEM)
    inner = [[g * GROUP + j for j in range(GROUP)] for g in range(ctx // GROUP)]
    cores = [[i, i + 1] for i in range(0, spread, 2)]
    core = (lax.axis_index("head") % 2).astype(jnp.int32).reshape(1)

    msg, solved, keys = local_call(
        key_rows.reshape(heads * rows, width),
        value_rows.reshape(heads * rows, width),
        log_decay.T,
        strengths.transpose(1, 2, 0).reshape(2 * heads, tokens),
    )
    parts = lax.all_to_all(msg, "ctx", 0, 0, axis_index_groups=inner)
    late_weight, _ = lax.optimization_barrier((out_weight, solved))
    wide = call(widen_kernel, array(*out_weight.shape), "widen", flops=10**9)(late_weight)
    other = lax.ppermute(wide, "head", [(i, i ^ 1) for i in range(spread)])
    both = call(
        weight_kernel,
        array(2 * out_weight.shape[0], columns, dtype=BF16),
        "chip_weight",
        flops=10**9,
        in_specs=[smem, vmem, vmem],
    )(core, late_weight, other)
    own, through = call(
        functools.partial(own_kernel, heads),
        (array(tokens, heads * width), array(tokens, heads * width)),
        "own_outputs",
        flops=4 * 10**9,
        scratch=[pltpu.VMEM((heads * tokens, width), F32)],
    )(queries.reshape(heads * tokens, width), keys, log_decay.T, solved)
    parts, own, through = lax.optimization_barrier((parts, own, through))
    prefix, total = call(
        functools.partial(group_kernel, width),
        (array(GROUP - 1, part_rows, width), array(part_rows, width)),
        "group_scan",
    )(parts)
    pair = lax.all_gather(total, "ctx", axis_index_groups=pairs(8))
    total = call(functools.partial(pair_kernel, width), array(part_rows, width), "pair_total")(pair)
    quad = lax.all_gather(total, "ctx", axis_index_groups=pairs(16))
    write = call(
        functools.partial(write_kernel, width), array(part_rows - width, width), "half_write"
    )(quad)
    far = lax.all_gather(write, "ctx", axis_index_groups=pairs(48))
    place = (lax.axis_index("ctx") // GROUP).astype(jnp.int32).reshape(1)
    starts = call(
        functools.partial(start_kernel, width),
        array(GROUP, part_rows - width, width),
        "start_states",
        in_specs=[smem, vmem, vmem, vmem, vmem],
    )(place, pair, quad, far, prefix)
    states = lax.all_to_all(starts, "ctx", 0, 0, axis_index_groups=inner)
    hidden = call(
        functools.partial(hidden_kernel, heads), array(tokens, heads * width), "hidden"
    )(own, through, states.reshape(heads, width, width), norm_gain)
    hidden = lax.all_gather(hidden, "head", axis_index_groups=cores)
    sums = call(
        functools.partial(project_kernel, spread),
        array(tokens // 2, columns),
        "project",
        in_specs=[smem, vmem, vmem],
    )(core, hidden, both)
    ring = [[i * 2 + c for i in range(spread // 2)] for c in range(2)]
    shares = lax.all_to_all(
        sums.reshape(spread // 2, tokens // spread, columns), "head", 0, 0, axis_index_groups=ring
    )
    return jnp.sum(shares, axis=0).astype(BF16)


def solution(mesh):
    in_specs = (
        P("ctx", "head", None),
        P("ctx", None, "head", None),
        P("ctx", None, "head", None),
        P("ctx", None, "head"),
        P("ctx", "head"),
        P("head", None),
        P("head", None),
    )
    out_specs = P(("ctx", "head"), None)
    return jax.shard_map(
        per_device, mesh=mesh, in_specs=in_specs, out_specs=out_specs, check_vma=False
    )
```

```python
import functools

import jax
import jax.numpy as jnp
from jax import lax
from jax.experimental import pallas as pl
from jax.experimental.pallas import tpu as pltpu
from jax.sharding import PartitionSpec as P

F32 = jnp.float32
BF16 = jnp.bfloat16
GROUP = 8


def dims(left_dim, right_dim):
    return (((left_dim,), (right_dim,)), ((), ()))


def halves(value):
    high = value.astype(BF16)
    return high, (value - high.astype(F32)).astype(BF16)


def dot_halves(left, right, left_dim=1, right_dim=0):
    mul = functools.partial(
        lax.dot_general, dimension_numbers=dims(left_dim, right_dim), preferred_element_type=F32
    )
    if left_dim == 0:
        return mul(left[0], right[0]) + (mul(left[0], right[1]) + mul(left[1], right[0]))
    count = left[0].shape[0]
    both = mul(jnp.concatenate(left, axis=0), right[0])
    return both[:count] + (both[count:] + mul(left[0], right[1]))


def dot(left, right, left_dim=1, right_dim=0):
    return dot_halves(halves(left), halves(right), left_dim, right_dim)


def unit_rows(rows):
    return rows * lax.rsqrt(jnp.sum(rows * rows, axis=-1, keepdims=True) + 1e-06)


def iota(shape, dim):
    return lax.broadcasted_iota(jnp.int32, shape, dim)


def thirds(value):
    high, rest = halves(value)
    last = (value - high.astype(F32) - rest.astype(F32)).astype(BF16)
    return jnp.concatenate([last.astype(F32), rest.astype(F32), high.astype(F32)], axis=0).astype(BF16)


def picked(mask, small):
    wide = lax.dot_general(
        jnp.where(mask, 1.0, 0.0).astype(BF16), small, dims(1, 1), preferred_element_type=F32
    )
    return wide[:, :8] + wide[:, 8:16] + wide[:, 16:24]


def picked_line(small, mask):
    wide = lax.dot_general(
        small, jnp.where(mask, 1.0, 0.0).astype(BF16), dims(1, 1), preferred_element_type=F32
    )
    return wide[:8] + wide[8:16] + wide[16:24]


def blocks_of(part, count, mask):
    if part.shape[0] % 16:
        part, count = jnp.concatenate([part, part], axis=0), count // 2
    return tuple(jnp.concatenate([piece] * count, axis=0) * mask for piece in halves(part))


def inverse_blocks(lowers, stop):
    size = lowers[0].shape[0]
    width = 8
    lane = iota((width, size), 1)
    row = iota((width, size), 0)
    col = lane % width
    rows = iota((size, size), 0)
    cols = iota((size, size), 1)
    packed = []
    for lower in lowers:
        part = jnp.zeros((width, size), F32)
        for block in range(size // width):
            part = jnp.where(lane // width == block, lower[block * width : (block + 1) * width], part)
        packed.append(part)
    same = jnp.where(rows // width == cols // width, 1.0, 0.0).astype(BF16)
    eye = jnp.where(row == col, 1.0, 0.0).astype(F32)
    inverses = [eye - jnp.where(row // 2 == col // 2, part, 0.0) for part in packed]
    count = size // width
    for step in (2, 4):
        below = (row // (2 * step) == col // (2 * step)) & (row // step != col // step)
        corners = [halves(jnp.where(below, part, 0.0)) for part in packed]
        inner = [dot_halves(c, blocks_of(t, count, same)) for c, t in zip(corners, inverses)]
        inverses = [
            t - dot_halves(halves(t), blocks_of(y, count, same)) for t, y in zip(inverses, inner)
        ]
    while width < stop:
        count = size // width
        lane = iota((width, size), 1) // width
        even = lane % 2 == 0
        same = jnp.where(rows // width == cols // width, 1.0, 0.0).astype(BF16)
        below = jnp.where((rows // width == cols // width + 1) & ((cols // width) % 2 == 0), 1.0, 0.0).astype(BF16)
        corners = []
        for lower in lowers:
            part = jnp.zeros((width, size), F32)
            for block in range(0, count, 2):
                part = jnp.where(lane == block, lower[(block + 1) * width : (block + 2) * width], part)
            corners.append(halves(part))
        inner = [dot_halves(c, blocks_of(t, count, same)) for c, t in zip(corners, inverses)]
        outer = [dot_halves(halves(t), blocks_of(y, count, below)) for t, y in zip(inverses, inner)]
        inverses = [
            jnp.concatenate([jnp.where(even, t, 0.0), jnp.where(even, -e, t)], axis=0)
            for t, e in zip(inverses, outer)
        ]
        width *= 2
    return inverses


def local_kernel(
    heads, k_hbm, v_hbm, decay_hbm, beta_hbm, msg_hbm, solved_hbm, keys_hbm,
    k_ref, v_ref, small_ref, spread_k, spread_v, keys_ref, solved_ref, carry_ref, write_ref, in_sems, out_sems,
):
    rows = k_ref.shape[0] // heads
    tokens = rows // 2
    width = k_ref.shape[1]
    half = rows // 2
    quarter = width * heads // GROUP
    sends = []

    def send(source, target):
        sends.append(pltpu.make_async_copy(source, target, out_sems.at[len(sends)]))
        sends[-1].start()

    small_ref[3 * heads :] = jnp.zeros((8 - 3 * heads, tokens), F32)
    fetches = [
        pltpu.make_async_copy(source, target, in_sems.at[i])
        for i, (source, target) in enumerate(
            (
                (k_hbm, k_ref),
                (decay_hbm, small_ref.at[:heads]),
                (beta_hbm, small_ref.at[heads : 3 * heads]),
                (v_hbm, v_ref),
            )
        )
    ]
    for fetch in fetches:
        fetch.start()
    row_tok = iota((rows, tokens), 0) // 2
    tok = iota((rows, tokens), 1)
    first = iota((rows, 1), 0) % 2 == 0
    row_ids = iota((rows, rows), 0)
    col_ids = iota((rows, rows), 1)
    eye_k = jnp.where(iota((width, width), 0) == iota((width, width), 1), 1.0, 0.0).astype(F32)
    for fetch in fetches[:3]:
        fetch.wait()
    small = thirds(small_ref[...])
    cumul_rows = picked(row_tok >= tok, small)
    cumul_line = picked_line(small, row_tok >= tok)
    betas = picked(row_tok == tok, small)
    spread_k[...] = unit_rows(k_ref[...].astype(F32))
    keys, lowers, strength = [], [], []
    for head in range(heads):
        unit = spread_k[pl.ds(head, rows, stride=heads), :]
        beta = jnp.where(
            first, betas[:, heads + head : heads + head + 1], betas[:, 2 * heads + head : 2 * heads + head + 1]
        )
        cumul = cumul_rows[:, head : head + 1]
        line = cumul_line[head : head + 1, :]
        weight = jnp.exp(jnp.where(row_ids > col_ids, cumul - line, -1e30))
        parts = halves(unit)
        lowers.append(beta * weight * dot_halves(parts, parts, 1, 1))
        keys.append(unit)
        strength.append(beta)
        keys_ref[head] = unit
        send(keys_ref.at[head], keys_hbm.at[head])
    inverses = inverse_blocks(lowers, half)
    fetches[3].wait()
    spread_v[...] = v_ref[...].astype(F32)
    rights = [
        jnp.concatenate(
            [
                strength[head] * spread_v[pl.ds(head, rows, stride=heads), :],
                (strength[head] * jnp.exp(cumul_rows[:, head : head + 1])) * keys[head],
            ],
            axis=1,
        )
        for head in range(heads)
    ]
    uppers = [dot(inverse[:, :half], right[:half]) for inverse, right in zip(inverses, rights)]
    moved = [
        right[half:] - dot(lower[half:, :half], upper)
        for lower, right, upper in zip(lowers, rights, uppers)
    ]
    unders = [dot(inverse[:, half:], rest) for inverse, rest in zip(inverses, moved)]
    for head in range(heads):
        solved = jnp.concatenate([uppers[head], unders[head]], axis=0)
        solved_ref[head] = solved
        send(solved_ref.at[head], solved_hbm.at[head])
        cumul = cumul_rows[:, head : head + 1]
        last = cumul[rows - 1 : rows, :]
        tail = jnp.exp(last - cumul) * keys[head]
        pair = dot(solved, tail, 0, 0)
        write_ref[head] = pair[:width]
        carry_ref[head] = jnp.exp(last) * eye_k - pair[width:]
        for part in range(GROUP // heads):
            member = head * (GROUP // heads) + part
            send(carry_ref.at[head], msg_hbm.at[member, :width])
            send(write_ref.at[head, part * quarter : (part + 1) * quarter], msg_hbm.at[member, width:])
    for copy in sends:
        copy.wait()


def local_call(keys, values, decay, beta):
    heads, tokens = decay.shape
    rows, width = keys.shape[0] // heads, keys.shape[1]
    any_space = pl.BlockSpec(memory_space=pl.ANY)
    return pl.pallas_call(
        functools.partial(local_kernel, heads),
        out_shape=(
            jax.ShapeDtypeStruct((GROUP, width + width * heads // GROUP, width), F32),
            jax.ShapeDtypeStruct((heads, rows, 2 * width), F32),
            jax.ShapeDtypeStruct((heads, rows, width), F32),
        ),
        in_specs=[any_space] * 4,
        out_specs=(any_space,) * 3,
        scratch_shapes=[
            pltpu.VMEM(keys.shape, BF16),
            pltpu.VMEM(values.shape, BF16),
            pltpu.VMEM((8, tokens), F32),
            pltpu.VMEM(keys.shape, F32),
            pltpu.VMEM(values.shape, F32),
            pltpu.VMEM((heads, rows, width), F32),
            pltpu.VMEM((heads, rows, 2 * width), F32),
            pltpu.VMEM((heads, width, width), F32),
            pltpu.VMEM((heads, width, width), F32),
            pltpu.SemaphoreType.DMA((4,)),
            pltpu.SemaphoreType.DMA((2 * heads + 2 * GROUP,)),
        ],
        compiler_params=pltpu.CompilerParams(vmem_limit_bytes=60 * 1024 * 1024),
        name="local_chunk",
    )(keys, values, decay, beta)


def own_kernel(heads, q_ref, keys_ref, decay_ref, solved_ref, own_ref, through_ref, spread_q):
    tokens = q_ref.shape[0] // heads
    rows = keys_ref.shape[1]
    spread_q[...] = unit_rows(q_ref[...].astype(F32))
    small = thirds(jnp.concatenate([decay_ref[...], jnp.zeros((8 - heads, tokens), F32)], axis=0))
    reached = iota((rows, tokens), 0) // 2 >= iota((rows, tokens), 1)
    cumul_line = picked_line(small, reached)
    cumul_toks = picked(iota((tokens, tokens), 0) >= iota((tokens, tokens), 1), small)
    reached = iota((tokens, rows), 0) >= iota((tokens, rows), 1) // 2
    width = keys_ref.shape[2]
    for head in range(heads):
        lanes = slice(head * width, (head + 1) * width)
        query = spread_q[pl.ds(head, tokens, stride=heads), :]
        cumul = cumul_toks[:, head : head + 1]
        weight = jnp.exp(jnp.where(reached, cumul - cumul_line[head : head + 1, :], -1e30))
        mixed = dot(dot(query, keys_ref[head], 1, 1) * weight, solved_ref[head])
        own_ref[:, lanes] = mixed[:, :width]
        through_ref[:, lanes] = jnp.exp(cumul) * query - mixed[:, width:]


def widen_kernel(in_ref, out_ref):
    out_ref[...] = in_ref[...].astype(F32)


def weight_kernel(core_ref, own_ref, other_ref, both_ref):
    rows = own_ref.shape[0]
    other = other_ref[...].astype(BF16)
    on_first = core_ref[0] == 0

    @pl.when(on_first)
    def _():
        both_ref[:rows] = own_ref[...]
        both_ref[rows:] = other

    @pl.when(jnp.logical_not(on_first))
    def _():
        both_ref[:rows] = other
        both_ref[rows:] = own_ref[...]


def compose(earlier, later, width):
    both = dot(earlier, later[:width])
    return jnp.concatenate([both[:width], both[width:] + later[width:]], axis=0)


def group_kernel(width, parts_ref, prefix_ref, total_ref):
    count = parts_ref.shape[0]
    runs = [parts_ref[i] for i in range(count)]
    step = 1
    while step < count:
        for start in range(step, count, 2 * step):
            for i in range(start, start + step):
                runs[i] = compose(runs[start - 1], runs[i], width)
        step *= 2
    for i in range(count - 1):
        prefix_ref[i] = runs[i]
    total_ref[...] = runs[count - 1]


def in_order(place, own, arrived):
    is_first = place % 2 == 0
    return jnp.where(is_first, own, arrived), jnp.where(is_first, arrived, own)


def first_kernel(width, place_ref, own_ref, arrived_ref, write_ref):
    earlier, later = in_order(place_ref[0], own_ref[...], arrived_ref[...])
    write_ref[...] = dot(earlier[width:], later[:width]) + later[width:]


def write_kernel(width, place_ref, state_ref, own_ref, arrived_ref, write_ref):
    earlier, later = in_order(place_ref[0], own_ref[...], arrived_ref[...])
    middle = dot(state_ref[...], earlier[:width]) + earlier[width:]
    write_ref[...] = dot(middle, later[:width]) + later[width:]


def start_kernel(width, place_ref, own_ref, *refs):
    swap_refs, state_refs, prefix_ref, out_ref = refs[:4], refs[4:7], refs[7], refs[8]
    place = place_ref[0]
    arrived = swap_refs[0][...]
    for ref in swap_refs[1:]:
        arrived = arrived + ref[...]
    state = state_refs[0][...] + state_refs[1][...] + state_refs[2][...]
    moved = dot(state, arrived[:width]) + arrived[width:]
    state = jnp.where(place % 2 == 1, moved, state)
    out_ref[0] = state
    parts = halves(state)
    for i in range(prefix_ref.shape[0]):
        out_ref[i + 1] = dot_halves(parts, halves(prefix_ref[i, :width])) + prefix_ref[i, width:]


def copy_kernel(in_ref, _, out_ref):
    out_ref[...] = in_ref[...]


def hidden_kernel(heads, own_ref, through_ref, state_ref, gain_ref, hidden_ref):
    width = own_ref.shape[1] // heads
    for head in range(heads):
        lanes = slice(head * width, (head + 1) * width)
        outputs = own_ref[:, lanes] + dot(through_ref[:, lanes], state_ref[head], 1, 1)
        scale = lax.rsqrt(jnp.mean(outputs * outputs, axis=-1, keepdims=True) + 1e-05)
        scaled = outputs * scale * gain_ref[head : head + 1, :]
        hidden_ref[:, lanes] = scaled.astype(BF16).astype(F32)


def project_kernel(spread, core_ref, hidden_ref, weight_ref, out_ref):
    share = hidden_ref.shape[1] // spread
    kept = []
    for i in range(0, spread, 2):
        even = jnp.concatenate([hidden_ref[c, i * share : (i + 1) * share] for c in range(2)], axis=1)
        odd = jnp.concatenate([hidden_ref[c, (i + 1) * share : (i + 2) * share] for c in range(2)], axis=1)
        kept.append(jnp.where(core_ref[0] == 0, even, odd))
    kept = jnp.concatenate(kept, axis=0).astype(BF16)
    out_ref[...] = jnp.dot(kept, weight_ref[...], preferred_element_type=F32)


def per_device(queries, key_rows, value_rows, strengths, log_decay, norm_gain, out_weight):
    tokens, heads, width = queries.shape
    rows = 2 * tokens
    columns = out_weight.shape[1]
    ctx = lax.axis_size("ctx")
    spread = lax.axis_size("head")
    part_rows = width + width * heads // GROUP
    params = pltpu.CompilerParams(vmem_limit_bytes=48 * 1024 * 1024)

    def call(body, out_shape, name, flops=0, in_specs=None, scratch=()):
        extra = {} if in_specs is None else dict(in_specs=in_specs)
        return pl.pallas_call(
            body,
            out_shape=out_shape,
            compiler_params=params,
            name=name,
            cost_estimate=pl.CostEstimate(flops=flops, bytes_accessed=1 << 20, transcendentals=0),
            scratch_shapes=scratch,
            **extra,
        )

    def array(*shape, dtype=F32):
        return jax.ShapeDtypeStruct(shape, dtype)

    def pairs(flip):
        return [[i, i ^ flip] for i in range(ctx) if i < i ^ flip]

    smem = pl.BlockSpec(memory_space=pltpu.SMEM)
    vmem = pl.BlockSpec(memory_space=pltpu.VMEM)
    inner = [[g * GROUP + j for j in range(GROUP)] for g in range(ctx // GROUP)]
    cores = [[i, i + 1] for i in range(0, spread, 2)]
    core = (lax.axis_index("head") % 2).astype(jnp.int32).reshape(1)

    msg, solved, keys = local_call(
        key_rows.reshape(heads * rows, width),
        value_rows.reshape(heads * rows, width),
        log_decay.T,
        strengths.transpose(1, 2, 0).reshape(2 * heads, tokens),
    )
    parts = lax.all_to_all(msg, "ctx", 0, 0, axis_index_groups=inner)
    late_weight, _ = lax.optimization_barrier((out_weight, solved))
    wide = call(widen_kernel, array(*out_weight.shape), "widen", flops=10**9)(late_weight)
    other = lax.ppermute(wide, "head", [(i, i ^ 1) for i in range(spread)])
    both = call(
        weight_kernel,
        array(2 * out_weight.shape[0], columns, dtype=BF16),
        "chip_weight",
        flops=10**9,
        in_specs=[smem, vmem, vmem],
    )(core, late_weight, other)
    own, through = call(
        functools.partial(own_kernel, heads),
        (array(tokens, heads * width), array(tokens, heads * width)),
        "own_outputs",
        flops=4 * 10**9,
        scratch=[pltpu.VMEM((heads * tokens, width), F32)],
    )(queries.reshape(heads * tokens, width), keys, log_decay.T, solved)
    parts, own, through = lax.optimization_barrier((parts, own, through))
    prefix, total = call(
        functools.partial(group_kernel, width),
        (array(GROUP - 1, part_rows, width), array(part_rows, width)),
        "group_scan",
    )(parts)
    quarter = ctx // 4
    group = [[g * quarter + i for i in range(quarter)] for g in range(4)]

    place = (lax.axis_index("ctx") // GROUP).astype(jnp.int32).reshape(1)
    state_shape = array(part_rows - width, width)
    swapped, arrived, offered = [], [], total
    for g in range(4):
        swapped.append(lax.ppermute(offered, "ctx", [(i, i ^ GROUP) for i in group[g]]))
        if g == 0:
            write = call(
                functools.partial(first_kernel, width), state_shape, "first_write", in_specs=[smem, vmem, vmem]
            )(place, total, swapped[0])
        elif g < 3:
            write = call(
                functools.partial(write_kernel, width),
                state_shape,
                "next_write",
                in_specs=[smem, vmem, vmem, vmem],
            )(place, arrived[-1], total, swapped[g])
        if g < 3:
            came = lax.ppermute(write, "ctx", list(zip(group[g], group[g + 1])))
            arrived.append(call(copy_kernel, state_shape, "state", flops=10**9)(came, came))
            offered = call(copy_kernel, array(part_rows, width), "offer")(total, write)
    starts = call(
        functools.partial(start_kernel, width),
        array(GROUP, part_rows - width, width),
        "start_states",
        in_specs=[smem] + [vmem] * 9,
    )(place, total, *swapped, *arrived, prefix)
    states = lax.all_to_all(starts, "ctx", 0, 0, axis_index_groups=inner)
    hidden = call(
        functools.partial(hidden_kernel, heads), array(tokens, heads * width), "hidden"
    )(own, through, states.reshape(heads, width, width), norm_gain)
    hidden = lax.all_gather(hidden, "head", axis_index_groups=cores)
    sums = call(
        functools.partial(project_kernel, spread),
        array(tokens // 2, columns),
        "project",
        in_specs=[smem, vmem, vmem],
    )(core, hidden, both)
    ring = [[i * 2 + c for i in range(spread // 2)] for c in range(2)]
    shares = lax.all_to_all(
        sums.reshape(spread // 2, tokens // spread, columns), "head", 0, 0, axis_index_groups=ring
    )
    return jnp.sum(shares, axis=0).astype(BF16)


def solution(mesh):
    in_specs = (
        P("ctx", "head", None),
        P("ctx", None, "head", None),
        P("ctx", None, "head", None),
        P("ctx", None, "head"),
        P("ctx", "head"),
        P("head", None),
        P("head", None),
    )
    out_specs = P(("ctx", "head"), None)
    return jax.shard_map(
        per_device, mesh=mesh, in_specs=in_specs, out_specs=out_specs, check_vma=False
    )
```

```python
import functools

import jax
import jax.numpy as jnp
from jax import lax
from jax.experimental import pallas as pl
from jax.experimental.pallas import tpu as pltpu
from jax.sharding import PartitionSpec as P

F32 = jnp.float32
BF16 = jnp.bfloat16
GROUP = 8


def dims(left_dim, right_dim):
    return (((left_dim,), (right_dim,)), ((), ()))


def halves(value):
    high = value.astype(BF16)
    return high, (value - high.astype(F32)).astype(BF16)


def dot_halves(left, right, left_dim=1, right_dim=0):
    mul = functools.partial(
        lax.dot_general, dimension_numbers=dims(left_dim, right_dim), preferred_element_type=F32
    )
    if left_dim == 0:
        return mul(left[0], right[0]) + (mul(left[0], right[1]) + mul(left[1], right[0]))
    count = left[0].shape[0]
    both = mul(jnp.concatenate(left, axis=0), right[0])
    return both[:count] + (both[count:] + mul(left[0], right[1]))


def dot(left, right, left_dim=1, right_dim=0):
    return dot_halves(halves(left), halves(right), left_dim, right_dim)


def unit_rows(rows):
    return rows * lax.rsqrt(jnp.sum(rows * rows, axis=-1, keepdims=True) + 1e-06)


def iota(shape, dim):
    return lax.broadcasted_iota(jnp.int32, shape, dim)


def thirds(value):
    high, rest = halves(value)
    last = (value - high.astype(F32) - rest.astype(F32)).astype(BF16)
    return jnp.concatenate([last.astype(F32), rest.astype(F32), high.astype(F32)], axis=0).astype(BF16)


def picked(mask, small):
    wide = lax.dot_general(
        jnp.where(mask, 1.0, 0.0).astype(BF16), small, dims(1, 1), preferred_element_type=F32
    )
    return wide[:, :8] + wide[:, 8:16] + wide[:, 16:24]


def picked_line(small, mask):
    wide = lax.dot_general(
        small, jnp.where(mask, 1.0, 0.0).astype(BF16), dims(1, 1), preferred_element_type=F32
    )
    return wide[:8] + wide[8:16] + wide[16:24]


def blocks_of(part, count, mask):
    if part.shape[0] % 16:
        part, count = jnp.concatenate([part, part], axis=0), count // 2
    return tuple(jnp.concatenate([piece] * count, axis=0) * mask for piece in halves(part))


def small_inverses(lower, width):
    lanes = 128
    row = iota((width, lanes), 0)
    lane = iota((width, lanes), 1)
    tiles = []
    for start in range(0, lower.shape[0], lanes):
        part = jnp.zeros((width, lanes), F32)
        for block in range(lanes // width):
            first = start + block * width
            part = jnp.where(lane // width == block, lower[first : first + width, start : start + lanes], part)
        inverse = jnp.where(row == lane % width, 1.0, 0.0).astype(F32)
        for column in range(width - 1):
            factor = jnp.take_along_axis(part, lane - lane % width + column, axis=1)
            inverse = inverse - factor * inverse[column : column + 1, :]
        tiles.append(inverse)
    return jnp.concatenate(tiles, axis=1)


def inverse_blocks(lowers, stop):
    size = lowers[0].shape[0]
    width = 16
    rows = iota((size, size), 0)
    cols = iota((size, size), 1)
    inverses = [small_inverses(lower, width) for lower in lowers]
    while width < stop:
        count = size // width
        lane = iota((width, size), 1) // width
        even = lane % 2 == 0
        same = jnp.where(rows // width == cols // width, 1.0, 0.0).astype(BF16)
        below = jnp.where((rows // width == cols // width + 1) & ((cols // width) % 2 == 0), 1.0, 0.0).astype(BF16)
        corners = []
        for lower in lowers:
            part = jnp.zeros((width, size), F32)
            for block in range(0, count, 2):
                part = jnp.where(lane == block, lower[(block + 1) * width : (block + 2) * width], part)
            corners.append(halves(part))
        inner = [dot_halves(c, blocks_of(t, count, same)) for c, t in zip(corners, inverses)]
        outer = [dot_halves(halves(t), blocks_of(y, count, below)) for t, y in zip(inverses, inner)]
        inverses = [
            jnp.concatenate([jnp.where(even, t, 0.0), jnp.where(even, -e, t)], axis=0)
            for t, e in zip(inverses, outer)
        ]
        width *= 2
    return inverses


def local_kernel(
    heads, k_hbm, v_hbm, decay_hbm, beta_hbm, msg_hbm, solved_hbm, keys_hbm,
    k_ref, v_ref, small_ref, spread_k, spread_v, keys_ref, solved_ref, carry_ref, write_ref, in_sems, out_sems,
):
    rows = k_ref.shape[0] // heads
    tokens = rows // 2
    width = k_ref.shape[1]
    half = rows // 2
    quarter = width * heads // GROUP
    sends = []

    def send(source, target):
        sends.append(pltpu.make_async_copy(source, target, out_sems.at[len(sends)]))
        sends[-1].start()

    small_ref[3 * heads :] = jnp.zeros((8 - 3 * heads, tokens), F32)
    fetches = [
        pltpu.make_async_copy(source, target, in_sems.at[i])
        for i, (source, target) in enumerate(
            (
                (k_hbm, k_ref),
                (decay_hbm, small_ref.at[:heads]),
                (beta_hbm, small_ref.at[heads : 3 * heads]),
                (v_hbm, v_ref),
            )
        )
    ]
    for fetch in fetches:
        fetch.start()
    row_tok = iota((rows, tokens), 0) // 2
    tok = iota((rows, tokens), 1)
    first = iota((rows, 1), 0) % 2 == 0
    row_ids = iota((rows, rows), 0)
    col_ids = iota((rows, rows), 1)
    eye_k = jnp.where(iota((width, width), 0) == iota((width, width), 1), 1.0, 0.0).astype(F32)
    for fetch in fetches[:3]:
        fetch.wait()
    small = thirds(small_ref[...])
    cumul_rows = picked(row_tok >= tok, small)
    cumul_line = picked_line(small, row_tok >= tok)
    betas = picked(row_tok == tok, small)
    spread_k[...] = unit_rows(k_ref[...].astype(F32))
    keys, lowers, strength = [], [], []
    for head in range(heads):
        unit = spread_k[pl.ds(head, rows, stride=heads), :]
        beta = jnp.where(
            first, betas[:, heads + head : heads + head + 1], betas[:, 2 * heads + head : 2 * heads + head + 1]
        )
        cumul = cumul_rows[:, head : head + 1]
        line = cumul_line[head : head + 1, :]
        weight = jnp.exp(jnp.where(row_ids > col_ids, cumul - line, -1e30))
        parts = halves(unit)
        lowers.append(beta * weight * dot_halves(parts, parts, 1, 1))
        keys.append(unit)
        strength.append(beta)
        keys_ref[head] = unit
        send(keys_ref.at[head], keys_hbm.at[head])
    inverses = inverse_blocks(lowers, half)
    fetches[3].wait()
    spread_v[...] = v_ref[...].astype(F32)
    rights = [
        jnp.concatenate(
            [
                strength[head] * spread_v[pl.ds(head, rows, stride=heads), :],
                (strength[head] * jnp.exp(cumul_rows[:, head : head + 1])) * keys[head],
            ],
            axis=1,
        )
        for head in range(heads)
    ]
    uppers = [dot(inverse[:, :half], right[:half]) for inverse, right in zip(inverses, rights)]
    moved = [
        right[half:] - dot(lower[half:, :half], upper)
        for lower, right, upper in zip(lowers, rights, uppers)
    ]
    unders = [dot(inverse[:, half:], rest) for inverse, rest in zip(inverses, moved)]
    for head in range(heads):
        solved = jnp.concatenate([uppers[head], unders[head]], axis=0)
        solved_ref[head] = solved
        send(solved_ref.at[head], solved_hbm.at[head])
        cumul = cumul_rows[:, head : head + 1]
        last = cumul[rows - 1 : rows, :]
        tail = jnp.exp(last - cumul) * keys[head]
        pair = dot(solved, tail, 0, 0)
        write_ref[head] = pair[:width]
        carry_ref[head] = jnp.exp(last) * eye_k - pair[width:]
        for part in range(GROUP // heads):
            member = head * (GROUP // heads) + part
            send(carry_ref.at[head], msg_hbm.at[member, :width])
            send(write_ref.at[head, part * quarter : (part + 1) * quarter], msg_hbm.at[member, width:])
    for copy in sends:
        copy.wait()


def local_call(keys, values, decay, beta):
    heads, tokens = decay.shape
    rows, width = keys.shape[0] // heads, keys.shape[1]
    any_space = pl.BlockSpec(memory_space=pl.ANY)
    return pl.pallas_call(
        functools.partial(local_kernel, heads),
        out_shape=(
            jax.ShapeDtypeStruct((GROUP, width + width * heads // GROUP, width), F32),
            jax.ShapeDtypeStruct((heads, rows, 2 * width), F32),
            jax.ShapeDtypeStruct((heads, rows, width), F32),
        ),
        in_specs=[any_space] * 4,
        out_specs=(any_space,) * 3,
        scratch_shapes=[
            pltpu.VMEM(keys.shape, BF16),
            pltpu.VMEM(values.shape, BF16),
            pltpu.VMEM((8, tokens), F32),
            pltpu.VMEM(keys.shape, F32),
            pltpu.VMEM(values.shape, F32),
            pltpu.VMEM((heads, rows, width), F32),
            pltpu.VMEM((heads, rows, 2 * width), F32),
            pltpu.VMEM((heads, width, width), F32),
            pltpu.VMEM((heads, width, width), F32),
            pltpu.SemaphoreType.DMA((4,)),
            pltpu.SemaphoreType.DMA((2 * heads + 2 * GROUP,)),
        ],
        compiler_params=pltpu.CompilerParams(vmem_limit_bytes=60 * 1024 * 1024),
        name="local_chunk",
    )(keys, values, decay, beta)


def own_kernel(heads, q_ref, keys_ref, decay_ref, solved_ref, own_ref, through_ref, spread_q):
    tokens = q_ref.shape[0] // heads
    rows = keys_ref.shape[1]
    spread_q[...] = unit_rows(q_ref[...].astype(F32))
    small = thirds(jnp.concatenate([decay_ref[...], jnp.zeros((8 - heads, tokens), F32)], axis=0))
    reached = iota((rows, tokens), 0) // 2 >= iota((rows, tokens), 1)
    cumul_line = picked_line(small, reached)
    cumul_toks = picked(iota((tokens, tokens), 0) >= iota((tokens, tokens), 1), small)
    reached = iota((tokens, rows), 0) >= iota((tokens, rows), 1) // 2
    width = keys_ref.shape[2]
    for head in range(heads):
        lanes = slice(head * width, (head + 1) * width)
        query = spread_q[pl.ds(head, tokens, stride=heads), :]
        cumul = cumul_toks[:, head : head + 1]
        weight = jnp.exp(jnp.where(reached, cumul - cumul_line[head : head + 1, :], -1e30))
        mixed = dot(dot(query, keys_ref[head], 1, 1) * weight, solved_ref[head])
        own_ref[:, lanes] = mixed[:, :width]
        through_ref[:, lanes] = jnp.exp(cumul) * query - mixed[:, width:]


def widen_kernel(in_ref, out_ref, copy_ref):
    out_ref[...] = in_ref[...].astype(F32)
    copy_ref[...] = in_ref[...]


def compose(earlier, later, width):
    both = dot(earlier, later[:width])
    return jnp.concatenate([both[:width], both[width:] + later[width:]], axis=0)


def group_kernel(width, parts_ref, prefix_ref, total_ref):
    count = parts_ref.shape[0]
    runs = [parts_ref[i] for i in range(count)]
    step = 1
    while step < count:
        for start in range(step, count, 2 * step):
            for i in range(start, start + step):
                runs[i] = compose(runs[start - 1], runs[i], width)
        step *= 2
    for i in range(count - 1):
        prefix_ref[i] = runs[i]
    total_ref[...] = runs[count - 1]


def in_order(place, own, arrived):
    is_first = place % 2 == 0
    return jnp.where(is_first, own, arrived), jnp.where(is_first, arrived, own)


def first_kernel(width, place_ref, own_ref, arrived_ref, write_ref):
    earlier, later = in_order(place_ref[0], own_ref[...], arrived_ref[...])
    write_ref[...] = dot(earlier[width:], later[:width]) + later[width:]


def write_kernel(width, place_ref, state_ref, own_ref, arrived_ref, write_ref):
    earlier, later = in_order(place_ref[0], own_ref[...], arrived_ref[...])
    middle = dot(state_ref[...], earlier[:width]) + earlier[width:]
    write_ref[...] = dot(middle, later[:width]) + later[width:]


def start_kernel(width, place_ref, own_ref, *refs):
    swap_refs, state_refs, prefix_ref, out_ref = refs[:4], refs[4:7], refs[7], refs[8]
    place = place_ref[0]
    arrived = swap_refs[0][...]
    for ref in swap_refs[1:]:
        arrived = arrived + ref[...]
    state = state_refs[0][...] + state_refs[1][...] + state_refs[2][...]
    moved = dot(state, arrived[:width]) + arrived[width:]
    state = jnp.where(place % 2 == 1, moved, state)
    out_ref[0] = state
    parts = halves(state)
    for i in range(prefix_ref.shape[0]):
        out_ref[i + 1] = dot_halves(parts, halves(prefix_ref[i, :width])) + prefix_ref[i, width:]


def copy_kernel(in_ref, _, out_ref):
    out_ref[...] = in_ref[...]


def hidden_kernel(heads, own_ref, through_ref, state_ref, gain_ref, hidden_ref):
    width = own_ref.shape[1] // heads
    for head in range(heads):
        lanes = slice(head * width, (head + 1) * width)
        outputs = own_ref[:, lanes] + dot(through_ref[:, lanes], state_ref[head], 1, 1)
        scale = lax.rsqrt(jnp.mean(outputs * outputs, axis=-1, keepdims=True) + 1e-05)
        scaled = outputs * scale * gain_ref[head : head + 1, :]
        hidden_ref[:, lanes] = scaled.astype(BF16).astype(F32)


def project_kernel(spread, core_ref, hidden_ref, own_ref, other_ref, out_ref):
    share = hidden_ref.shape[1] // spread
    on_first = core_ref[0] == 0
    kept = []
    for core in range(2):
        even = jnp.concatenate([hidden_ref[core, i * share : (i + 1) * share] for i in range(0, spread, 2)], axis=0)
        odd = jnp.concatenate([hidden_ref[core, i * share : (i + 1) * share] for i in range(1, spread, 2)], axis=0)
        kept.append(jnp.where(on_first, even, odd))
    mine = jnp.where(on_first, kept[0], kept[1]).astype(BF16)
    others = jnp.where(on_first, kept[1], kept[0]).astype(BF16)
    out_ref[...] = jnp.dot(mine, own_ref[...], preferred_element_type=F32) + jnp.dot(
        others, other_ref[...].astype(BF16), preferred_element_type=F32
    )


def per_device(queries, key_rows, value_rows, strengths, log_decay, norm_gain, out_weight):
    tokens, heads, width = queries.shape
    rows = 2 * tokens
    columns = out_weight.shape[1]
    ctx = lax.axis_size("ctx")
    spread = lax.axis_size("head")
    part_rows = width + width * heads // GROUP
    params = pltpu.CompilerParams(vmem_limit_bytes=48 * 1024 * 1024)

    def call(body, out_shape, name, flops=0, in_specs=None, scratch=()):
        extra = {} if in_specs is None else dict(in_specs=in_specs)
        return pl.pallas_call(
            body,
            out_shape=out_shape,
            compiler_params=params,
            name=name,
            cost_estimate=pl.CostEstimate(flops=flops, bytes_accessed=1 << 20, transcendentals=0),
            scratch_shapes=scratch,
            **extra,
        )

    def array(*shape, dtype=F32):
        return jax.ShapeDtypeStruct(shape, dtype)

    def pairs(flip):
        return [[i, i ^ flip] for i in range(ctx) if i < i ^ flip]

    smem = pl.BlockSpec(memory_space=pltpu.SMEM)
    vmem = pl.BlockSpec(memory_space=pltpu.VMEM)
    inner = [[g * GROUP + j for j in range(GROUP)] for g in range(ctx // GROUP)]
    cores = [[i, i + 1] for i in range(0, spread, 2)]
    core = (lax.axis_index("head") % 2).astype(jnp.int32).reshape(1)

    msg, solved, keys = local_call(
        key_rows.reshape(heads * rows, width),
        value_rows.reshape(heads * rows, width),
        log_decay.T,
        strengths.transpose(1, 2, 0).reshape(2 * heads, tokens),
    )
    place = (lax.axis_index("ctx") // GROUP).astype(jnp.int32).reshape(1)
    msg, place, core = lax.optimization_barrier((msg, place, core))
    parts = lax.all_to_all(msg, "ctx", 0, 0, axis_index_groups=inner)
    late_weight, _ = lax.optimization_barrier((out_weight, solved))
    wide, held = call(
        widen_kernel,
        (array(*out_weight.shape), array(*out_weight.shape, dtype=BF16)),
        "widen",
        flops=10**9,
    )(late_weight)
    other = lax.ppermute(wide, "head", [(i, i ^ 1) for i in range(spread)])
    own, through = call(
        functools.partial(own_kernel, heads),
        (array(tokens, heads * width), array(tokens, heads * width)),
        "own_outputs",
        flops=4 * 10**9,
        scratch=[pltpu.VMEM((heads * tokens, width), F32)],
    )(queries.reshape(heads * tokens, width), keys, log_decay.T, solved)
    parts, own, through = lax.optimization_barrier((parts, own, through))
    prefix, total = call(
        functools.partial(group_kernel, width),
        (array(GROUP - 1, part_rows, width), array(part_rows, width)),
        "group_scan",
    )(parts)
    quarter = ctx // 4
    group = [[g * quarter + i for i in range(quarter)] for g in range(4)]

    state_shape = array(part_rows - width, width)
    swapped, arrived, offered = [], [], total
    for g in range(4):
        swapped.append(lax.ppermute(offered, "ctx", [(i, i ^ GROUP) for i in group[g]]))
        if g == 0:
            write = call(
                functools.partial(first_kernel, width), state_shape, "first_write", in_specs=[smem, vmem, vmem]
            )(place, total, swapped[0])
        elif g < 3:
            write = call(
                functools.partial(write_kernel, width),
                state_shape,
                "next_write",
                in_specs=[smem, vmem, vmem, vmem],
            )(place, arrived[-1], total, swapped[g])
        if g < 3:
            came = lax.ppermute(write, "ctx", list(zip(group[g], group[g + 1])))
            arrived.append(call(copy_kernel, state_shape, "state", flops=10**9)(came, came))
            offered = call(copy_kernel, array(part_rows, width), "offer")(total, write)
    starts = call(
        functools.partial(start_kernel, width),
        array(GROUP, part_rows - width, width),
        "start_states",
        in_specs=[smem] + [vmem] * 9,
    )(place, total, *swapped, *arrived, prefix)
    states = lax.all_to_all(starts, "ctx", 0, 0, axis_index_groups=inner)
    hidden = call(
        functools.partial(hidden_kernel, heads), array(tokens, heads * width), "hidden"
    )(own, through, states.reshape(heads, width, width), norm_gain)
    hidden = lax.all_gather(hidden, "head", axis_index_groups=cores)
    sums = call(
        functools.partial(project_kernel, spread),
        array(tokens // 2, columns),
        "project",
        in_specs=[smem, vmem, vmem, vmem],
    )(core, hidden, held, other)
    ring = [[i * 2 + c for i in range(spread // 2)] for c in range(2)]
    shares = lax.all_to_all(
        sums.reshape(spread // 2, tokens // spread, columns), "head", 0, 0, axis_index_groups=ring
    )
    return jnp.sum(shares, axis=0).astype(BF16)


def solution(mesh):
    in_specs = (
        P("ctx", "head", None),
        P("ctx", None, "head", None),
        P("ctx", None, "head", None),
        P("ctx", None, "head"),
        P("ctx", "head"),
        P("head", None),
        P("head", None),
    )
    out_specs = P(("ctx", "head"), None)
    return jax.shard_map(
        per_device, mesh=mesh, in_specs=in_specs, out_specs=out_specs, check_vma=False
    )
```

```python
import functools

import jax
import jax.numpy as jnp
from jax import lax
from jax.experimental import pallas as pl
from jax.experimental.pallas import tpu as pltpu
from jax.sharding import PartitionSpec as P

F32 = jnp.float32
BF16 = jnp.bfloat16
GROUP = 8


def dims(left_dim, right_dim):
    return (((left_dim,), (right_dim,)), ((), ()))


def halves(value):
    high = value.astype(BF16)
    return high, (value - high.astype(F32)).astype(BF16)


def dot_halves(left, right, left_dim=1, right_dim=0):
    mul = functools.partial(
        lax.dot_general, dimension_numbers=dims(left_dim, right_dim), preferred_element_type=F32
    )
    if left_dim == 0:
        return mul(left[0], right[0]) + (mul(left[0], right[1]) + mul(left[1], right[0]))
    count = left[0].shape[0]
    both = mul(jnp.concatenate(left, axis=0), right[0])
    return both[:count] + (both[count:] + mul(left[0], right[1]))


def dot(left, right, left_dim=1, right_dim=0):
    return dot_halves(halves(left), halves(right), left_dim, right_dim)


def unit_rows(rows):
    return rows * lax.rsqrt(jnp.sum(rows * rows, axis=-1, keepdims=True) + 1e-06)


def iota(shape, dim):
    return lax.broadcasted_iota(jnp.int32, shape, dim)


def thirds(value):
    high, rest = halves(value)
    last = (value - high.astype(F32) - rest.astype(F32)).astype(BF16)
    return jnp.concatenate([last.astype(F32), rest.astype(F32), high.astype(F32)], axis=0).astype(BF16)


def picked(mask, small):
    wide = lax.dot_general(
        jnp.where(mask, 1.0, 0.0).astype(BF16), small, dims(1, 1), preferred_element_type=F32
    )
    return wide[:, :8] + wide[:, 8:16] + wide[:, 16:24]


def picked_line(small, mask):
    wide = lax.dot_general(
        small, jnp.where(mask, 1.0, 0.0).astype(BF16), dims(1, 1), preferred_element_type=F32
    )
    return wide[:8] + wide[8:16] + wide[16:24]


def blocks_of(part, count, mask):
    if part.shape[0] % 16:
        part, count = jnp.concatenate([part, part], axis=0), count // 2
    return tuple(jnp.concatenate([piece] * count, axis=0) * mask for piece in halves(part))


def small_inverses(lower, width):
    lanes = 128
    row = iota((width, lanes), 0)
    lane = iota((width, lanes), 1)
    tiles = []
    for start in range(0, lower.shape[0], lanes):
        part = jnp.zeros((width, lanes), F32)
        for block in range(lanes // width):
            first = start + block * width
            part = jnp.where(lane // width == block, lower[first : first + width, start : start + lanes], part)
        inverse = jnp.where(row == lane % width, 1.0, 0.0).astype(F32)
        for column in range(width - 1):
            factor = jnp.take_along_axis(part, lane - lane % width + column, axis=1)
            inverse = inverse - factor * inverse[column : column + 1, :]
        tiles.append(inverse)
    return jnp.concatenate(tiles, axis=1)


def inverse_blocks(lowers, stop):
    size = lowers[0].shape[0]
    width = 16
    rows = iota((size, size), 0)
    cols = iota((size, size), 1)
    inverses = [small_inverses(lower, width) for lower in lowers]
    while width < stop:
        count = size // width
        lane = iota((width, size), 1) // width
        even = lane % 2 == 0
        same = jnp.where(rows // width == cols // width, 1.0, 0.0).astype(BF16)
        below = jnp.where((rows // width == cols // width + 1) & ((cols // width) % 2 == 0), 1.0, 0.0).astype(BF16)
        corners = []
        for lower in lowers:
            part = jnp.zeros((width, size), F32)
            for block in range(0, count, 2):
                part = jnp.where(lane == block, lower[(block + 1) * width : (block + 2) * width], part)
            corners.append(halves(part))
        inner = [dot_halves(c, blocks_of(t, count, same)) for c, t in zip(corners, inverses)]
        outer = [dot_halves(halves(t), blocks_of(y, count, below)) for t, y in zip(inverses, inner)]
        inverses = [
            jnp.concatenate([jnp.where(even, t, 0.0), jnp.where(even, -e, t)], axis=0)
            for t, e in zip(inverses, outer)
        ]
        width *= 2
    return inverses


def local_kernel(
    heads, k_hbm, v_hbm, decay_hbm, beta_hbm, msg_hbm, solved_hbm, keys_hbm,
    k_ref, v_ref, small_ref, spread_k, spread_v, keys_ref, solved_ref, carry_ref, write_ref, in_sems, out_sems,
):
    rows = k_ref.shape[0] // heads
    tokens = rows // 2
    width = k_ref.shape[1]
    half = rows // 2
    quarter = width * heads // GROUP
    sends = []

    def send(source, target):
        sends.append(pltpu.make_async_copy(source, target, out_sems.at[len(sends)]))
        sends[-1].start()

    small_ref[3 * heads :] = jnp.zeros((8 - 3 * heads, tokens), F32)
    fetches = [
        pltpu.make_async_copy(source, target, in_sems.at[i])
        for i, (source, target) in enumerate(
            (
                (k_hbm, k_ref),
                (decay_hbm, small_ref.at[:heads]),
                (beta_hbm, small_ref.at[heads : 3 * heads]),
                (v_hbm, v_ref),
            )
        )
    ]
    for fetch in fetches:
        fetch.start()
    row_tok = iota((rows, tokens), 0) // 2
    tok = iota((rows, tokens), 1)
    first = iota((rows, 1), 0) % 2 == 0
    row_ids = iota((rows, rows), 0)
    col_ids = iota((rows, rows), 1)
    eye_k = jnp.where(iota((width, width), 0) == iota((width, width), 1), 1.0, 0.0).astype(F32)
    for fetch in fetches[:3]:
        fetch.wait()
    small = thirds(small_ref[...])
    cumul_rows = picked(row_tok >= tok, small)
    cumul_line = picked_line(small, row_tok >= tok)
    betas = picked(row_tok == tok, small)
    spread_k[...] = unit_rows(k_ref[...].astype(F32))
    keys, lowers, strength = [], [], []
    for head in range(heads):
        unit = spread_k[pl.ds(head, rows, stride=heads), :]
        beta = jnp.where(
            first, betas[:, heads + head : heads + head + 1], betas[:, 2 * heads + head : 2 * heads + head + 1]
        )
        cumul = cumul_rows[:, head : head + 1]
        line = cumul_line[head : head + 1, :]
        weight = jnp.exp(jnp.where(row_ids > col_ids, cumul - line, -1e30))
        parts = halves(unit)
        lowers.append(beta * weight * dot_halves(parts, parts, 1, 1))
        keys.append(unit)
        strength.append(beta)
        keys_ref[head] = unit
        send(keys_ref.at[head], keys_hbm.at[head])
    inverses = inverse_blocks(lowers, half)
    fetches[3].wait()
    spread_v[...] = v_ref[...].astype(F32)
    rights = [
        jnp.concatenate(
            [
                strength[head] * spread_v[pl.ds(head, rows, stride=heads), :],
                (strength[head] * jnp.exp(cumul_rows[:, head : head + 1])) * keys[head],
            ],
            axis=1,
        )
        for head in range(heads)
    ]
    uppers = [dot(inverse[:, :half], right[:half]) for inverse, right in zip(inverses, rights)]
    moved = [
        right[half:] - dot(lower[half:, :half], upper)
        for lower, right, upper in zip(lowers, rights, uppers)
    ]
    unders = [dot(inverse[:, half:], rest) for inverse, rest in zip(inverses, moved)]
    for head in range(heads):
        solved = jnp.concatenate([uppers[head], unders[head]], axis=0)
        solved_ref[head] = solved
        send(solved_ref.at[head], solved_hbm.at[head])
        cumul = cumul_rows[:, head : head + 1]
        last = cumul[rows - 1 : rows, :]
        tail = jnp.exp(last - cumul) * keys[head]
        pair = dot(solved, tail, 0, 0)
        write_ref[head] = pair[:width]
        carry_ref[head] = jnp.exp(last) * eye_k - pair[width:]
        for part in range(GROUP // heads):
            member = head * (GROUP // heads) + part
            send(carry_ref.at[head], msg_hbm.at[member, :width])
            send(write_ref.at[head, part * quarter : (part + 1) * quarter], msg_hbm.at[member, width:])
    for copy in sends:
        copy.wait()


def local_call(keys, values, decay, beta):
    heads, tokens = decay.shape
    rows, width = keys.shape[0] // heads, keys.shape[1]
    any_space = pl.BlockSpec(memory_space=pl.ANY)
    return pl.pallas_call(
        functools.partial(local_kernel, heads),
        out_shape=(
            jax.ShapeDtypeStruct((GROUP, width + width * heads // GROUP, width), F32),
            jax.ShapeDtypeStruct((heads, rows, 2 * width), F32),
            jax.ShapeDtypeStruct((heads, rows, width), F32),
        ),
        in_specs=[any_space] * 4,
        out_specs=(any_space,) * 3,
        scratch_shapes=[
            pltpu.VMEM(keys.shape, BF16),
            pltpu.VMEM(values.shape, BF16),
            pltpu.VMEM((8, tokens), F32),
            pltpu.VMEM(keys.shape, F32),
            pltpu.VMEM(values.shape, F32),
            pltpu.VMEM((heads, rows, width), F32),
            pltpu.VMEM((heads, rows, 2 * width), F32),
            pltpu.VMEM((heads, width, width), F32),
            pltpu.VMEM((heads, width, width), F32),
            pltpu.SemaphoreType.DMA((4,)),
            pltpu.SemaphoreType.DMA((2 * heads + 2 * GROUP,)),
        ],
        compiler_params=pltpu.CompilerParams(vmem_limit_bytes=60 * 1024 * 1024),
        name="local_chunk",
    )(keys, values, decay, beta)


def own_kernel(heads, q_ref, keys_ref, decay_ref, solved_ref, own_ref, through_ref, spread_q):
    tokens = q_ref.shape[0] // heads
    rows = keys_ref.shape[1]
    spread_q[...] = unit_rows(q_ref[...].astype(F32))
    small = thirds(jnp.concatenate([decay_ref[...], jnp.zeros((8 - heads, tokens), F32)], axis=0))
    reached = iota((rows, tokens), 0) // 2 >= iota((rows, tokens), 1)
    cumul_line = picked_line(small, reached)
    cumul_toks = picked(iota((tokens, tokens), 0) >= iota((tokens, tokens), 1), small)
    reached = iota((tokens, rows), 0) >= iota((tokens, rows), 1) // 2
    width = keys_ref.shape[2]
    for head in range(heads):
        lanes = slice(head * width, (head + 1) * width)
        query = spread_q[pl.ds(head, tokens, stride=heads), :]
        cumul = cumul_toks[:, head : head + 1]
        weight = jnp.exp(jnp.where(reached, cumul - cumul_line[head : head + 1, :], -1e30))
        mixed = dot(dot(query, keys_ref[head], 1, 1) * weight, solved_ref[head])
        own_ref[:, lanes] = mixed[:, :width]
        through_ref[:, lanes] = jnp.exp(cumul) * query - mixed[:, width:]


def widen_kernel(in_ref, out_ref, copy_ref):
    out_ref[...] = in_ref[...].astype(F32)
    copy_ref[...] = in_ref[...]


def compose(earlier, later, width):
    both = dot(earlier, later[:width])
    return jnp.concatenate([both[:width], both[width:] + later[width:]], axis=0)


def group_kernel(width, parts_ref, prefix_ref, total_ref):
    count = parts_ref.shape[0]
    runs = [parts_ref[i] for i in range(count)]
    step = 1
    while step < count:
        for start in range(step, count, 2 * step):
            for i in range(start, start + step):
                runs[i] = compose(runs[start - 1], runs[i], width)
        step *= 2
    for i in range(count - 1):
        prefix_ref[i] = runs[i]
    total_ref[...] = runs[count - 1]


def in_order(place, own, arrived):
    is_first = place % 2 == 0
    return jnp.where(is_first, own, arrived), jnp.where(is_first, arrived, own)


def first_kernel(width, place_ref, own_ref, arrived_ref, write_ref):
    earlier, later = in_order(place_ref[0], own_ref[...], arrived_ref[...])
    write_ref[...] = dot(earlier[width:], later[:width]) + later[width:]


def write_kernel(width, place_ref, state_ref, own_ref, arrived_ref, write_ref):
    earlier, later = in_order(place_ref[0], own_ref[...], arrived_ref[...])
    middle = dot(state_ref[...], earlier[:width]) + earlier[width:]
    write_ref[...] = dot(middle, later[:width]) + later[width:]


def start_kernel(width, place_ref, own_ref, *refs):
    swap_refs, state_refs, prefix_ref, out_ref = refs[:4], refs[4:7], refs[7], refs[8]
    place = place_ref[0]
    arrived = swap_refs[0][...]
    for ref in swap_refs[1:]:
        arrived = arrived + ref[...]
    state = state_refs[0][...] + state_refs[1][...] + state_refs[2][...]
    moved = dot(state, arrived[:width]) + arrived[width:]
    state = jnp.where(place % 2 == 1, moved, state)
    out_ref[0] = state
    parts = halves(state)
    for i in range(prefix_ref.shape[0]):
        out_ref[i + 1] = dot_halves(parts, halves(prefix_ref[i, :width])) + prefix_ref[i, width:]


def copy_kernel(in_ref, _, out_ref):
    out_ref[...] = in_ref[...]


def hidden_kernel(heads, own_ref, through_ref, state_ref, gain_ref, hidden_ref):
    width = own_ref.shape[1] // heads
    for head in range(heads):
        lanes = slice(head * width, (head + 1) * width)
        outputs = own_ref[:, lanes] + dot(through_ref[:, lanes], state_ref[head], 1, 1)
        scale = lax.rsqrt(jnp.mean(outputs * outputs, axis=-1, keepdims=True) + 1e-05)
        scaled = outputs * scale * gain_ref[head : head + 1, :]
        hidden_ref[:, lanes] = scaled.astype(BF16).astype(F32)


def project_kernel(spread, core_ref, hidden_ref, own_ref, other_ref, out_ref):
    share = hidden_ref.shape[1] // spread
    on_first = core_ref[0] == 0
    kept = []
    for core in range(2):
        even = jnp.concatenate([hidden_ref[core, i * share : (i + 1) * share] for i in range(0, spread, 2)], axis=0)
        odd = jnp.concatenate([hidden_ref[core, i * share : (i + 1) * share] for i in range(1, spread, 2)], axis=0)
        kept.append(jnp.where(on_first, even, odd))
    mine = jnp.where(on_first, kept[0], kept[1]).astype(BF16)
    others = jnp.where(on_first, kept[1], kept[0]).astype(BF16)
    out_ref[...] = jnp.dot(mine, own_ref[...], preferred_element_type=F32) + jnp.dot(
        others, other_ref[...].astype(BF16), preferred_element_type=F32
    )


def per_device(queries, key_rows, value_rows, strengths, log_decay, norm_gain, out_weight):
    tokens, heads, width = queries.shape
    rows = 2 * tokens
    columns = out_weight.shape[1]
    ctx = lax.axis_size("ctx")
    spread = lax.axis_size("head")
    part_rows = width + width * heads // GROUP
    params = pltpu.CompilerParams(vmem_limit_bytes=48 * 1024 * 1024)

    def call(body, out_shape, name, flops=0, in_specs=None, scratch=()):
        extra = {} if in_specs is None else dict(in_specs=in_specs)
        return pl.pallas_call(
            body,
            out_shape=out_shape,
            compiler_params=params,
            name=name,
            cost_estimate=pl.CostEstimate(flops=flops, bytes_accessed=1 << 20, transcendentals=0),
            scratch_shapes=scratch,
            **extra,
        )

    def array(*shape, dtype=F32):
        return jax.ShapeDtypeStruct(shape, dtype)

    def pairs(flip):
        return [[i, i ^ flip] for i in range(ctx) if i < i ^ flip]

    smem = pl.BlockSpec(memory_space=pltpu.SMEM)
    vmem = pl.BlockSpec(memory_space=pltpu.VMEM)
    inner = [[g * GROUP + j for j in range(GROUP)] for g in range(ctx // GROUP)]
    cores = [[i, i + 1] for i in range(0, spread, 2)]
    core = (lax.axis_index("head") % 2).astype(jnp.int32).reshape(1)

    msg, solved, keys = local_call(
        key_rows.reshape(heads * rows, width),
        value_rows.reshape(heads * rows, width),
        log_decay.T,
        strengths.transpose(1, 2, 0).reshape(2 * heads, tokens),
    )
    place = (lax.axis_index("ctx") // GROUP).astype(jnp.int32).reshape(1)
    msg, place, core = lax.optimization_barrier((msg, place, core))
    parts = lax.all_to_all(msg, "ctx", 0, 0, axis_index_groups=inner)
    late_weight, _ = lax.optimization_barrier((out_weight, solved))
    wide, held = call(
        widen_kernel,
        (array(*out_weight.shape), array(*out_weight.shape, dtype=BF16)),
        "widen",
        flops=10**9,
    )(late_weight)
    other = lax.ppermute(wide, "head", [(i, i ^ 1) for i in range(spread)])
    own, through = call(
        functools.partial(own_kernel, heads),
        (array(tokens, heads * width), array(tokens, heads * width)),
        "own_outputs",
        flops=4 * 10**9,
        scratch=[pltpu.VMEM((heads * tokens, width), F32)],
    )(queries.reshape(heads * tokens, width), keys, log_decay.T, solved)
    parts, own, through = lax.optimization_barrier((parts, own, through))
    prefix, total = call(
        functools.partial(group_kernel, width),
        (array(GROUP - 1, part_rows, width), array(part_rows, width)),
        "group_scan",
    )(parts)
    quarter = ctx // 4
    group = [[g * quarter + i for i in range(quarter)] for g in range(4)]

    state_shape = array(part_rows - width, width)
    swapped, arrived, offered = [], [], total
    for g in range(4):
        swapped.append(lax.ppermute(offered, "ctx", [(i, i ^ GROUP) for i in group[g]]))
        if g == 0:
            write = call(
                functools.partial(first_kernel, width), state_shape, "first_write", in_specs=[smem, vmem, vmem]
            )(place, total, swapped[0])
        elif g < 3:
            write = call(
                functools.partial(write_kernel, width),
                state_shape,
                "next_write",
                in_specs=[smem, vmem, vmem, vmem],
            )(place, arrived[-1], total, swapped[g])
        if g < 3:
            came = lax.ppermute(write, "ctx", [(i, j ^ GROUP if g == 2 else j) for i, j in zip(group[g], group[g + 1])])
            arrived.append(call(copy_kernel, state_shape, "state", flops=10**9)(came, came))
            offered = call(copy_kernel, array(part_rows, width), "offer")(total, write)
    starts = call(
        functools.partial(start_kernel, width),
        array(GROUP, part_rows - width, width),
        "start_states",
        in_specs=[smem] + [vmem] * 9,
    )(place, total, *swapped, *arrived, prefix)
    states = lax.all_to_all(starts, "ctx", 0, 0, axis_index_groups=inner)
    hidden = call(
        functools.partial(hidden_kernel, heads), array(tokens, heads * width), "hidden"
    )(own, through, states.reshape(heads, width, width), norm_gain)
    hidden = lax.all_gather(hidden, "head", axis_index_groups=cores)
    sums = call(
        functools.partial(project_kernel, spread),
        array(tokens // 2, columns),
        "project",
        in_specs=[smem, vmem, vmem, vmem],
    )(core, hidden, held, other)
    ring = [[i * 2 + c for i in range(spread // 2)] for c in range(2)]
    shares = lax.all_to_all(
        sums.reshape(spread // 2, tokens // spread, columns), "head", 0, 0, axis_index_groups=ring
    )
    return jnp.sum(shares, axis=0).astype(BF16)


def solution(mesh):
    in_specs = (
        P("ctx", "head", None),
        P("ctx", None, "head", None),
        P("ctx", None, "head", None),
        P("ctx", None, "head"),
        P("ctx", "head"),
        P("head", None),
        P("head", None),
    )
    out_specs = P(("ctx", "head"), None)
    return jax.shard_map(
        per_device, mesh=mesh, in_specs=in_specs, out_specs=out_specs, check_vma=False
    )
```

```python
import functools

import jax
import jax.numpy as jnp
from jax import lax
from jax.experimental import pallas as pl
from jax.experimental.pallas import tpu as pltpu
from jax.sharding import PartitionSpec as P

F32 = jnp.float32
BF16 = jnp.bfloat16
GROUP = 8


def dims(left_dim, right_dim):
    return (((left_dim,), (right_dim,)), ((), ()))


def halves(value):
    high = value.astype(BF16)
    return high, (value - high.astype(F32)).astype(BF16)


def dot_halves(left, right, left_dim=1, right_dim=0):
    mul = functools.partial(
        lax.dot_general, dimension_numbers=dims(left_dim, right_dim), preferred_element_type=F32
    )
    if left_dim == 0:
        return mul(left[0], right[0]) + (mul(left[0], right[1]) + mul(left[1], right[0]))
    count = left[0].shape[0]
    both = mul(jnp.concatenate(left, axis=0), right[0])
    return both[:count] + (both[count:] + mul(left[0], right[1]))


def dot(left, right, left_dim=1, right_dim=0):
    return dot_halves(halves(left), halves(right), left_dim, right_dim)


def unit_rows(rows):
    return rows * lax.rsqrt(jnp.sum(rows * rows, axis=-1, keepdims=True) + 1e-06)


def iota(shape, dim):
    return lax.broadcasted_iota(jnp.int32, shape, dim)


def thirds(value):
    high, rest = halves(value)
    last = (value - high.astype(F32) - rest.astype(F32)).astype(BF16)
    return jnp.concatenate([last.astype(F32), rest.astype(F32), high.astype(F32)], axis=0).astype(BF16)


def picked(mask, small):
    wide = lax.dot_general(
        jnp.where(mask, 1.0, 0.0).astype(BF16), small, dims(1, 1), preferred_element_type=F32
    )
    return wide[:, :8] + wide[:, 8:16] + wide[:, 16:24]


def picked_line(small, mask):
    wide = lax.dot_general(
        small, jnp.where(mask, 1.0, 0.0).astype(BF16), dims(1, 1), preferred_element_type=F32
    )
    return wide[:8] + wide[8:16] + wide[16:24]


def blocks_of(part, count, mask):
    if part.shape[0] % 16:
        part, count = jnp.concatenate([part, part], axis=0), count // 2
    return tuple(jnp.concatenate([piece] * count, axis=0) * mask for piece in halves(part))


def small_inverses(lower, width):
    lanes = 128
    row = iota((width, lanes), 0)
    lane = iota((width, lanes), 1)
    tiles = []
    for start in range(0, lower.shape[0], lanes):
        part = jnp.zeros((width, lanes), F32)
        for block in range(lanes // width):
            first = start + block * width
            part = jnp.where(lane // width == block, lower[first : first + width, start : start + lanes], part)
        inverse = jnp.where(row == lane % width, 1.0, 0.0).astype(F32)
        for column in range(width - 1):
            factor = jnp.take_along_axis(part, lane - lane % width + column, axis=1)
            inverse = inverse - factor * inverse[column : column + 1, :]
        tiles.append(inverse)
    return jnp.concatenate(tiles, axis=1)


def inverse_blocks(lowers, stop):
    size = lowers[0].shape[0]
    width = 16
    rows = iota((size, size), 0)
    cols = iota((size, size), 1)
    inverses = [small_inverses(lower, width) for lower in lowers]
    while width < stop:
        count = size // width
        lane = iota((width, size), 1) // width
        even = lane % 2 == 0
        same = jnp.where(rows // width == cols // width, 1.0, 0.0).astype(BF16)
        below = jnp.where((rows // width == cols // width + 1) & ((cols // width) % 2 == 0), 1.0, 0.0).astype(BF16)
        corners = []
        for lower in lowers:
            part = jnp.zeros((width, size), F32)
            for block in range(0, count, 2):
                part = jnp.where(lane == block, lower[(block + 1) * width : (block + 2) * width], part)
            corners.append(halves(part))
        inner = [dot_halves(c, blocks_of(t, count, same)) for c, t in zip(corners, inverses)]
        outer = [dot_halves(halves(t), blocks_of(y, count, below)) for t, y in zip(inverses, inner)]
        inverses = [
            jnp.concatenate([jnp.where(even, t, 0.0), jnp.where(even, -e, t)], axis=0)
            for t, e in zip(inverses, outer)
        ]
        width *= 2
    return inverses


def local_kernel(
    heads, k_hbm, v_hbm, decay_hbm, beta_hbm, msg_hbm, solved_hbm, keys_hbm,
    k_ref, v_ref, small_ref, spread_k, spread_v, keys_ref, solved_ref, carry_ref, write_ref, in_sems, out_sems,
):
    rows = k_ref.shape[0] // heads
    tokens = rows // 2
    width = k_ref.shape[1]
    half = rows // 2
    quarter = width * heads // GROUP
    sends = []

    def send(source, target):
        sends.append(pltpu.make_async_copy(source, target, out_sems.at[len(sends)]))
        sends[-1].start()

    small_ref[3 * heads :] = jnp.zeros((8 - 3 * heads, tokens), F32)
    fetches = [
        pltpu.make_async_copy(source, target, in_sems.at[i])
        for i, (source, target) in enumerate(
            (
                (k_hbm, k_ref),
                (decay_hbm, small_ref.at[:heads]),
                (beta_hbm, small_ref.at[heads : 3 * heads]),
                (v_hbm, v_ref),
            )
        )
    ]
    for fetch in fetches:
        fetch.start()
    row_tok = iota((rows, tokens), 0) // 2
    tok = iota((rows, tokens), 1)
    first = iota((rows, 1), 0) % 2 == 0
    row_ids = iota((rows, rows), 0)
    col_ids = iota((rows, rows), 1)
    eye_k = jnp.where(iota((width, width), 0) == iota((width, width), 1), 1.0, 0.0).astype(F32)
    for fetch in fetches[:3]:
        fetch.wait()
    small = thirds(small_ref[...])
    cumul_rows = picked(row_tok >= tok, small)
    cumul_line = picked_line(small, row_tok >= tok)
    betas = picked(row_tok == tok, small)
    spread_k[...] = unit_rows(k_ref[...].astype(F32))
    keys, lowers, strength = [], [], []
    for head in range(heads):
        unit = spread_k[pl.ds(head, rows, stride=heads), :]
        beta = jnp.where(
            first, betas[:, heads + head : heads + head + 1], betas[:, 2 * heads + head : 2 * heads + head + 1]
        )
        cumul = cumul_rows[:, head : head + 1]
        line = cumul_line[head : head + 1, :]
        weight = jnp.exp(jnp.where(row_ids > col_ids, cumul - line, -1e30))
        parts = halves(unit)
        lowers.append(beta * weight * dot_halves(parts, parts, 1, 1))
        keys.append(unit)
        strength.append(beta)
        keys_ref[head] = unit
        send(keys_ref.at[head], keys_hbm.at[head])
    inverses = inverse_blocks(lowers, half)
    fetches[3].wait()
    spread_v[...] = v_ref[...].astype(F32)
    rights = [
        jnp.concatenate(
            [
                strength[head] * spread_v[pl.ds(head, rows, stride=heads), :],
                (strength[head] * jnp.exp(cumul_rows[:, head : head + 1])) * keys[head],
            ],
            axis=1,
        )
        for head in range(heads)
    ]
    uppers = [dot(inverse[:, :half], right[:half]) for inverse, right in zip(inverses, rights)]
    moved = [
        right[half:] - dot(lower[half:, :half], upper)
        for lower, right, upper in zip(lowers, rights, uppers)
    ]
    unders = [dot(inverse[:, half:], rest) for inverse, rest in zip(inverses, moved)]
    for head in range(heads):
        solved = jnp.concatenate([uppers[head], unders[head]], axis=0)
        solved_ref[head] = solved
        send(solved_ref.at[head], solved_hbm.at[head])
        cumul = cumul_rows[:, head : head + 1]
        last = cumul[rows - 1 : rows, :]
        tail = jnp.exp(last - cumul) * keys[head]
        pair = dot(solved, tail, 0, 0)
        write_ref[head] = pair[:width]
        carry_ref[head] = jnp.exp(last) * eye_k - pair[width:]
        for part in range(GROUP // heads):
            member = head * (GROUP // heads) + part
            send(carry_ref.at[head], msg_hbm.at[member, :width])
            send(write_ref.at[head, part * quarter : (part + 1) * quarter], msg_hbm.at[member, width:])
    for copy in sends:
        copy.wait()


def local_call(keys, values, decay, beta):
    heads, tokens = decay.shape
    rows, width = keys.shape[0] // heads, keys.shape[1]
    any_space = pl.BlockSpec(memory_space=pl.ANY)
    return pl.pallas_call(
        functools.partial(local_kernel, heads),
        out_shape=(
            jax.ShapeDtypeStruct((GROUP, width + width * heads // GROUP, width), F32),
            jax.ShapeDtypeStruct((heads, rows, 2 * width), F32),
            jax.ShapeDtypeStruct((heads, rows, width), F32),
        ),
        in_specs=[any_space] * 4,
        out_specs=(any_space,) * 3,
        scratch_shapes=[
            pltpu.VMEM(keys.shape, BF16),
            pltpu.VMEM(values.shape, BF16),
            pltpu.VMEM((8, tokens), F32),
            pltpu.VMEM(keys.shape, F32),
            pltpu.VMEM(values.shape, F32),
            pltpu.VMEM((heads, rows, width), F32),
            pltpu.VMEM((heads, rows, 2 * width), F32),
            pltpu.VMEM((heads, width, width), F32),
            pltpu.VMEM((heads, width, width), F32),
            pltpu.SemaphoreType.DMA((4,)),
            pltpu.SemaphoreType.DMA((2 * heads + 2 * GROUP,)),
        ],
        compiler_params=pltpu.CompilerParams(vmem_limit_bytes=60 * 1024 * 1024),
        name="local_chunk",
    )(keys, values, decay, beta)


def own_kernel(heads, q_ref, keys_ref, decay_ref, solved_ref, own_ref, through_ref, spread_q):
    tokens = q_ref.shape[0] // heads
    rows = keys_ref.shape[1]
    spread_q[...] = unit_rows(q_ref[...].astype(F32))
    small = thirds(jnp.concatenate([decay_ref[...], jnp.zeros((8 - heads, tokens), F32)], axis=0))
    reached = iota((rows, tokens), 0) // 2 >= iota((rows, tokens), 1)
    cumul_line = picked_line(small, reached)
    cumul_toks = picked(iota((tokens, tokens), 0) >= iota((tokens, tokens), 1), small)
    reached = iota((tokens, rows), 0) >= iota((tokens, rows), 1) // 2
    width = keys_ref.shape[2]
    for head in range(heads):
        lanes = slice(head * width, (head + 1) * width)
        query = spread_q[pl.ds(head, tokens, stride=heads), :]
        cumul = cumul_toks[:, head : head + 1]
        weight = jnp.exp(jnp.where(reached, cumul - cumul_line[head : head + 1, :], -1e30))
        mixed = dot(dot(query, keys_ref[head], 1, 1) * weight, solved_ref[head])
        own_ref[:, lanes] = mixed[:, :width]
        through_ref[:, lanes] = jnp.exp(cumul) * query - mixed[:, width:]


def widen_kernel(in_ref, out_ref, copy_ref):
    out_ref[...] = in_ref[...].astype(F32)
    copy_ref[...] = in_ref[...]


def compose(earlier, later, width):
    both = dot(earlier, later[:width])
    return jnp.concatenate([both[:width], both[width:] + later[width:]], axis=0)


def group_kernel(width, parts_ref, prefix_ref, total_ref):
    count = parts_ref.shape[0]
    runs = [parts_ref[i] for i in range(count)]
    step = 1
    while step < count:
        for start in range(step, count, 2 * step):
            for i in range(start, start + step):
                runs[i] = compose(runs[start - 1], runs[i], width)
        step *= 2
    for i in range(count - 1):
        prefix_ref[i] = runs[i]
    total_ref[...] = runs[count - 1]


def in_order(place, own, arrived):
    is_first = place % 2 == 0
    return jnp.where(is_first, own, arrived), jnp.where(is_first, arrived, own)


def first_kernel(width, place_ref, own_ref, arrived_ref, write_ref):
    earlier, later = in_order(place_ref[0], own_ref[...], arrived_ref[...])
    write_ref[...] = dot(earlier[width:], later[:width]) + later[width:]


def write_kernel(width, place_ref, state_ref, own_ref, arrived_ref, write_ref):
    earlier, later = in_order(place_ref[0], own_ref[...], arrived_ref[...])
    middle = dot(state_ref[...], earlier[:width]) + earlier[width:]
    write_ref[...] = dot(middle, later[:width]) + later[width:]


def start_kernel(width, place_ref, own_ref, *refs):
    swap_refs, state_refs, prefix_ref, out_ref = refs[:4], refs[4:7], refs[7], refs[8]
    place = place_ref[0]
    arrived = swap_refs[0][...]
    for ref in swap_refs[1:]:
        arrived = arrived + ref[...]
    state = state_refs[0][...] + state_refs[1][...] + state_refs[2][...]
    moved = dot(state, arrived[:width]) + arrived[width:]
    state = jnp.where(place % 2 == 1, moved, state)
    out_ref[0] = state
    parts = halves(state)
    for i in range(prefix_ref.shape[0]):
        out_ref[i + 1] = dot_halves(parts, halves(prefix_ref[i, :width])) + prefix_ref[i, width:]


def copy_kernel(in_ref, _, out_ref):
    out_ref[...] = in_ref[...]


def hidden_kernel(heads, spread, core_ref, own_ref, through_ref, state_ref, gain_ref, keep_ref, give_ref):
    width = own_ref.shape[1] // heads
    share = own_ref.shape[0] // spread
    on_first = core_ref[0] == 0
    for head in range(heads):
        lanes = slice(head * width, (head + 1) * width)
        outputs = own_ref[:, lanes] + dot(through_ref[:, lanes], state_ref[head], 1, 1)
        scale = lax.rsqrt(jnp.mean(outputs * outputs, axis=-1, keepdims=True) + 1e-05)
        scaled = outputs * scale * gain_ref[head : head + 1, :]
        even = jnp.concatenate([scaled[i * share : (i + 1) * share] for i in range(0, spread, 2)], axis=0)
        odd = jnp.concatenate([scaled[i * share : (i + 1) * share] for i in range(1, spread, 2)], axis=0)
        keep_ref[:, lanes] = jnp.where(on_first, even, odd).astype(BF16)
        give_ref[:, lanes] = jnp.where(on_first, odd, even).astype(BF16).astype(F32)


def project_kernel(core_ref, keep_ref, both_ref, own_ref, other_ref, out_ref):
    got = jnp.where(core_ref[0] == 0, both_ref[1], both_ref[0]).astype(BF16)
    out_ref[...] = jnp.dot(keep_ref[...], own_ref[...], preferred_element_type=F32) + jnp.dot(
        got, other_ref[...].astype(BF16), preferred_element_type=F32
    )


def sum_kernel(shares_ref, out_ref):
    total = shares_ref[0]
    for i in range(1, shares_ref.shape[0]):
        total = total + shares_ref[i]
    out_ref[...] = total.astype(BF16)


def per_device(queries, key_rows, value_rows, strengths, log_decay, norm_gain, out_weight):
    tokens, heads, width = queries.shape
    rows = 2 * tokens
    columns = out_weight.shape[1]
    ctx = lax.axis_size("ctx")
    spread = lax.axis_size("head")
    part_rows = width + width * heads // GROUP
    params = pltpu.CompilerParams(vmem_limit_bytes=48 * 1024 * 1024)

    def call(body, out_shape, name, flops=0, in_specs=None, scratch=()):
        extra = {} if in_specs is None else dict(in_specs=in_specs)
        return pl.pallas_call(
            body,
            out_shape=out_shape,
            compiler_params=params,
            name=name,
            cost_estimate=pl.CostEstimate(flops=flops, bytes_accessed=1 << 20, transcendentals=0),
            scratch_shapes=scratch,
            **extra,
        )

    def array(*shape, dtype=F32):
        return jax.ShapeDtypeStruct(shape, dtype)

    def pairs(flip):
        return [[i, i ^ flip] for i in range(ctx) if i < i ^ flip]

    smem = pl.BlockSpec(memory_space=pltpu.SMEM)
    vmem = pl.BlockSpec(memory_space=pltpu.VMEM)
    inner = [[g * GROUP + j for j in range(GROUP)] for g in range(ctx // GROUP)]
    cores = [[i, i + 1] for i in range(0, spread, 2)]
    core = (lax.axis_index("head") % 2).astype(jnp.int32).reshape(1)

    msg, solved, keys = local_call(
        key_rows.reshape(heads * rows, width),
        value_rows.reshape(heads * rows, width),
        log_decay.T,
        strengths.transpose(1, 2, 0).reshape(2 * heads, tokens),
    )
    place = (lax.axis_index("ctx") // GROUP).astype(jnp.int32).reshape(1)
    msg, place, core = lax.optimization_barrier((msg, place, core))
    parts = lax.all_to_all(msg, "ctx", 0, 0, axis_index_groups=inner)
    late_weight, _ = lax.optimization_barrier((out_weight, solved))
    wide, held = call(
        widen_kernel,
        (array(*out_weight.shape), array(*out_weight.shape, dtype=BF16)),
        "widen",
        flops=10**9,
    )(late_weight)
    other = lax.ppermute(wide, "head", [(i, i ^ 1) for i in range(spread)])
    own, through = call(
        functools.partial(own_kernel, heads),
        (array(tokens, heads * width), array(tokens, heads * width)),
        "own_outputs",
        flops=4 * 10**9,
        scratch=[pltpu.VMEM((heads * tokens, width), F32)],
    )(queries.reshape(heads * tokens, width), keys, log_decay.T, solved)
    parts, own, through = lax.optimization_barrier((parts, own, through))
    prefix, total = call(
        functools.partial(group_kernel, width),
        (array(GROUP - 1, part_rows, width), array(part_rows, width)),
        "group_scan",
    )(parts)
    quarter = ctx // 4
    group = [[g * quarter + i for i in range(quarter)] for g in range(4)]

    state_shape = array(part_rows - width, width)
    swapped, arrived, offered = [], [], total
    for g in range(4):
        swapped.append(lax.ppermute(offered, "ctx", [(i, i ^ GROUP) for i in group[g]]))
        if g == 0:
            write = call(
                functools.partial(first_kernel, width), state_shape, "first_write", in_specs=[smem, vmem, vmem]
            )(place, total, swapped[0])
        elif g < 3:
            write = call(
                functools.partial(write_kernel, width),
                state_shape,
                "next_write",
                in_specs=[smem, vmem, vmem, vmem],
            )(place, arrived[-1], total, swapped[g])
        if g < 3:
            came = lax.ppermute(write, "ctx", [(i, j ^ GROUP if g == 2 else j) for i, j in zip(group[g], group[g + 1])])
            arrived.append(call(copy_kernel, state_shape, "state", flops=10**9)(came, came))
            offered = call(copy_kernel, array(part_rows, width), "offer")(total, write)
    starts = call(
        functools.partial(start_kernel, width),
        array(GROUP, part_rows - width, width),
        "start_states",
        in_specs=[smem] + [vmem] * 9,
    )(place, total, *swapped, *arrived, prefix)
    states = lax.all_to_all(starts, "ctx", 0, 0, axis_index_groups=inner)
    keep, give = call(
        functools.partial(hidden_kernel, heads, spread),
        (array(tokens // 2, heads * width, dtype=BF16), array(tokens // 2, heads * width)),
        "hidden",
        in_specs=[smem] + [vmem] * 4,
    )(core, own, through, states.reshape(heads, width, width), norm_gain)
    given = lax.all_gather(give, "head", axis_index_groups=cores)
    sums = call(
        project_kernel,
        array(tokens // 2, columns),
        "project",
        in_specs=[smem] + [vmem] * 4,
    )(core, keep, given, held, other)
    ring = [[i * 2 + c for i in range(spread // 2)] for c in range(2)]
    shares = lax.all_to_all(
        sums.reshape(spread // 2, tokens // spread, columns), "head", 0, 0, axis_index_groups=ring
    )
    return call(sum_kernel, array(tokens // spread, columns, dtype=BF16), "row_sums")(shares)


def solution(mesh):
    in_specs = (
        P("ctx", "head", None),
        P("ctx", None, "head", None),
        P("ctx", None, "head", None),
        P("ctx", None, "head"),
        P("ctx", "head"),
        P("head", None),
        P("head", None),
    )
    out_specs = P(("ctx", "head"), None)
    return jax.shard_map(
        per_device, mesh=mesh, in_specs=in_specs, out_specs=out_specs, check_vma=False
    )
```

```python
import functools

import jax
import jax.numpy as jnp
from jax import lax
from jax.experimental import pallas as pl
from jax.experimental.pallas import tpu as pltpu
from jax.sharding import PartitionSpec as P

F32 = jnp.float32
BF16 = jnp.bfloat16
GROUP = 8


def dims(left_dim, right_dim):
    return (((left_dim,), (right_dim,)), ((), ()))


def halves(value):
    high = value.astype(BF16)
    return high, (value - high.astype(F32)).astype(BF16)


def dot_halves(left, right, left_dim=1, right_dim=0):
    mul = functools.partial(
        lax.dot_general, dimension_numbers=dims(left_dim, right_dim), preferred_element_type=F32
    )
    if left_dim == 0:
        return mul(left[0], right[0]) + (mul(left[0], right[1]) + mul(left[1], right[0]))
    count = left[0].shape[0]
    both = mul(jnp.concatenate(left, axis=0), right[0])
    return both[:count] + (both[count:] + mul(left[0], right[1]))


def dot(left, right, left_dim=1, right_dim=0):
    return dot_halves(halves(left), halves(right), left_dim, right_dim)


def unit_rows(rows):
    return rows * lax.rsqrt(jnp.sum(rows * rows, axis=-1, keepdims=True) + 1e-06)


def iota(shape, dim):
    return lax.broadcasted_iota(jnp.int32, shape, dim)


def thirds(value):
    high, rest = halves(value)
    last = (value - high.astype(F32) - rest.astype(F32)).astype(BF16)
    return jnp.concatenate([last.astype(F32), rest.astype(F32), high.astype(F32)], axis=0).astype(BF16)


def picked(mask, small):
    wide = lax.dot_general(
        jnp.where(mask, 1.0, 0.0).astype(BF16), small, dims(1, 1), preferred_element_type=F32
    )
    return wide[:, :8] + wide[:, 8:16] + wide[:, 16:24]


def picked_line(small, mask):
    wide = lax.dot_general(
        small, jnp.where(mask, 1.0, 0.0).astype(BF16), dims(1, 1), preferred_element_type=F32
    )
    return wide[:8] + wide[8:16] + wide[16:24]


def blocks_of(part, count, mask):
    if part.shape[0] % 16:
        part, count = jnp.concatenate([part, part], axis=0), count // 2
    return tuple(jnp.concatenate([piece] * count, axis=0) * mask for piece in halves(part))


def small_inverses(lower, width):
    lanes = 128
    row = iota((width, lanes), 0)
    lane = iota((width, lanes), 1)
    tiles = []
    for start in range(0, lower.shape[0], lanes):
        part = jnp.zeros((width, lanes), F32)
        for block in range(lanes // width):
            first = start + block * width
            part = jnp.where(lane // width == block, lower[first : first + width, start : start + lanes], part)
        inverse = jnp.where(row == lane % width, 1.0, 0.0).astype(F32)
        for column in range(width - 1):
            factor = jnp.take_along_axis(part, lane - lane % width + column, axis=1)
            inverse = inverse - factor * inverse[column : column + 1, :]
        tiles.append(inverse)
    return jnp.concatenate(tiles, axis=1)


def inverse_blocks(lowers, stop):
    size = lowers[0].shape[0]
    width = 16
    rows = iota((size, size), 0)
    cols = iota((size, size), 1)
    inverses = [small_inverses(lower, width) for lower in lowers]
    while width < stop:
        count = size // width
        lane = iota((width, size), 1) // width
        even = lane % 2 == 0
        same = jnp.where(rows // width == cols // width, 1.0, 0.0).astype(BF16)
        below = jnp.where((rows // width == cols // width + 1) & ((cols // width) % 2 == 0), 1.0, 0.0).astype(BF16)
        corners = []
        for lower in lowers:
            part = jnp.zeros((width, size), F32)
            for block in range(0, count, 2):
                part = jnp.where(lane == block, lower[(block + 1) * width : (block + 2) * width], part)
            corners.append(halves(part))
        inner = [dot_halves(c, blocks_of(t, count, same)) for c, t in zip(corners, inverses)]
        outer = [dot_halves(halves(t), blocks_of(y, count, below)) for t, y in zip(inverses, inner)]
        inverses = [
            jnp.concatenate([jnp.where(even, t, 0.0), jnp.where(even, -e, t)], axis=0)
            for t, e in zip(inverses, outer)
        ]
        width *= 2
    return inverses


def local_kernel(
    heads, k_hbm, v_hbm, decay_hbm, beta_hbm, msg_hbm, solved_hbm, keys_hbm,
    k_ref, v_ref, small_ref, spread_k, spread_v, keys_ref, solved_ref, carry_ref, write_ref, in_sems, out_sems,
):
    rows = k_ref.shape[0] // heads
    tokens = rows // 2
    width = k_ref.shape[1]
    half = rows // 2
    quarter = width * heads // GROUP
    sends = []

    def send(source, target):
        sends.append(pltpu.make_async_copy(source, target, out_sems.at[len(sends)]))
        sends[-1].start()

    small_ref[3 * heads :] = jnp.zeros((8 - 3 * heads, tokens), F32)
    fetches = [
        pltpu.make_async_copy(source, target, in_sems.at[i])
        for i, (source, target) in enumerate(
            (
                (k_hbm, k_ref),
                (decay_hbm, small_ref.at[:heads]),
                (beta_hbm, small_ref.at[heads : 3 * heads]),
                (v_hbm, v_ref),
            )
        )
    ]
    for fetch in fetches:
        fetch.start()
    row_tok = iota((rows, tokens), 0) // 2
    tok = iota((rows, tokens), 1)
    first = iota((rows, 1), 0) % 2 == 0
    row_ids = iota((rows, rows), 0)
    col_ids = iota((rows, rows), 1)
    eye_k = jnp.where(iota((width, width), 0) == iota((width, width), 1), 1.0, 0.0).astype(F32)
    for fetch in fetches[:3]:
        fetch.wait()
    small = thirds(small_ref[...])
    cumul_rows = picked(row_tok >= tok, small)
    cumul_line = picked_line(small, row_tok >= tok)
    betas = picked(row_tok == tok, small)
    spread_k[...] = unit_rows(k_ref[...].astype(F32))
    keys, lowers, strength = [], [], []
    for head in range(heads):
        unit = spread_k[pl.ds(head, rows, stride=heads), :]
        beta = jnp.where(
            first, betas[:, heads + head : heads + head + 1], betas[:, 2 * heads + head : 2 * heads + head + 1]
        )
        cumul = cumul_rows[:, head : head + 1]
        line = cumul_line[head : head + 1, :]
        weight = jnp.exp(jnp.where(row_ids > col_ids, cumul - line, -1e30))
        parts = halves(unit)
        lowers.append(beta * weight * dot_halves(parts, parts, 1, 1))
        keys.append(unit)
        strength.append(beta)
        keys_ref[head] = unit
        send(keys_ref.at[head], keys_hbm.at[head])
    inverses = inverse_blocks(lowers, half)
    fetches[3].wait()
    spread_v[...] = v_ref[...].astype(F32)
    rights = [
        jnp.concatenate(
            [
                strength[head] * spread_v[pl.ds(head, rows, stride=heads), :],
                (strength[head] * jnp.exp(cumul_rows[:, head : head + 1])) * keys[head],
            ],
            axis=1,
        )
        for head in range(heads)
    ]
    uppers = [dot(inverse[:, :half], right[:half]) for inverse, right in zip(inverses, rights)]
    moved = [
        right[half:] - dot(lower[half:, :half], upper)
        for lower, right, upper in zip(lowers, rights, uppers)
    ]
    unders = [dot(inverse[:, half:], rest) for inverse, rest in zip(inverses, moved)]
    for head in range(heads):
        solved = jnp.concatenate([uppers[head], unders[head]], axis=0)
        solved_ref[head] = solved
        send(solved_ref.at[head], solved_hbm.at[head])
        cumul = cumul_rows[:, head : head + 1]
        last = cumul[rows - 1 : rows, :]
        tail = jnp.exp(last - cumul) * keys[head]
        pair = dot(solved, tail, 0, 0)
        write_ref[head] = pair[:width]
        carry_ref[head] = jnp.exp(last) * eye_k - pair[width:]
        for part in range(GROUP // heads):
            member = head * (GROUP // heads) + part
            send(carry_ref.at[head], msg_hbm.at[member, :width])
            send(write_ref.at[head, part * quarter : (part + 1) * quarter], msg_hbm.at[member, width:])
    for copy in sends:
        copy.wait()


def local_call(keys, values, decay, beta):
    heads, tokens = decay.shape
    rows, width = keys.shape[0] // heads, keys.shape[1]
    any_space = pl.BlockSpec(memory_space=pl.ANY)
    return pl.pallas_call(
        functools.partial(local_kernel, heads),
        out_shape=(
            jax.ShapeDtypeStruct((GROUP, width + width * heads // GROUP, width), F32),
            jax.ShapeDtypeStruct((heads, rows, 2 * width), F32),
            jax.ShapeDtypeStruct((heads, rows, width), F32),
        ),
        in_specs=[any_space] * 4,
        out_specs=(any_space,) * 3,
        scratch_shapes=[
            pltpu.VMEM(keys.shape, BF16),
            pltpu.VMEM(values.shape, BF16),
            pltpu.VMEM((8, tokens), F32),
            pltpu.VMEM(keys.shape, F32),
            pltpu.VMEM(values.shape, F32),
            pltpu.VMEM((heads, rows, width), F32),
            pltpu.VMEM((heads, rows, 2 * width), F32),
            pltpu.VMEM((heads, width, width), F32),
            pltpu.VMEM((heads, width, width), F32),
            pltpu.SemaphoreType.DMA((4,)),
            pltpu.SemaphoreType.DMA((2 * heads + 2 * GROUP,)),
        ],
        compiler_params=pltpu.CompilerParams(vmem_limit_bytes=60 * 1024 * 1024),
        name="local_chunk",
    )(keys, values, decay, beta)


def own_kernel(heads, q_ref, keys_ref, decay_ref, solved_ref, own_ref, through_ref, spread_q):
    tokens = q_ref.shape[0] // heads
    rows = keys_ref.shape[1]
    spread_q[...] = unit_rows(q_ref[...].astype(F32))
    small = thirds(jnp.concatenate([decay_ref[...], jnp.zeros((8 - heads, tokens), F32)], axis=0))
    reached = iota((rows, tokens), 0) // 2 >= iota((rows, tokens), 1)
    cumul_line = picked_line(small, reached)
    cumul_toks = picked(iota((tokens, tokens), 0) >= iota((tokens, tokens), 1), small)
    reached = iota((tokens, rows), 0) >= iota((tokens, rows), 1) // 2
    width = keys_ref.shape[2]
    for head in range(heads):
        lanes = slice(head * width, (head + 1) * width)
        query = spread_q[pl.ds(head, tokens, stride=heads), :]
        cumul = cumul_toks[:, head : head + 1]
        weight = jnp.exp(jnp.where(reached, cumul - cumul_line[head : head + 1, :], -1e30))
        mixed = dot(dot(query, keys_ref[head], 1, 1) * weight, solved_ref[head])
        own_ref[:, lanes] = mixed[:, :width]
        through_ref[:, lanes] = jnp.exp(cumul) * query - mixed[:, width:]


def widen_kernel(in_ref, out_ref, copy_ref):
    out_ref[...] = in_ref[...].astype(F32)
    copy_ref[...] = in_ref[...]


def compose(earlier, later, width):
    both = dot(earlier, later[:width])
    return jnp.concatenate([both[:width], both[width:] + later[width:]], axis=0)


def group_kernel(width, parts_ref, prefix_ref, total_ref):
    count = parts_ref.shape[0]
    runs = [parts_ref[i] for i in range(count)]
    step = 1
    while step < count:
        for start in range(step, count, 2 * step):
            for i in range(start, start + step):
                runs[i] = compose(runs[start - 1], runs[i], width)
        step *= 2
    for i in range(count - 1):
        prefix_ref[i] = runs[i]
    total_ref[...] = runs[count - 1]


def in_order(place, own, arrived):
    is_first = place % 2 == 0
    return jnp.where(is_first, own, arrived), jnp.where(is_first, arrived, own)


def first_kernel(width, place_ref, own_ref, arrived_ref, write_ref):
    earlier, later = in_order(place_ref[0], own_ref[...], arrived_ref[...])
    write_ref[...] = dot(earlier[width:], later[:width]) + later[width:]


def write_kernel(width, place_ref, state_ref, own_ref, arrived_ref, write_ref):
    earlier, later = in_order(place_ref[0], own_ref[...], arrived_ref[...])
    middle = dot(state_ref[...], earlier[:width]) + earlier[width:]
    write_ref[...] = dot(middle, later[:width]) + later[width:]


def start_kernel(width, place_ref, own_ref, *refs):
    swap_refs, state_refs, prefix_ref, out_ref = refs[:4], refs[4:7], refs[7], refs[8]
    place = place_ref[0]
    arrived = swap_refs[0][...]
    for ref in swap_refs[1:]:
        arrived = arrived + ref[...]
    state = state_refs[0][...] + state_refs[1][...] + state_refs[2][...]
    moved = dot(state, arrived[:width]) + arrived[width:]
    state = jnp.where(place % 2 == 1, moved, state)
    out_ref[0] = state
    parts = halves(state)
    for i in range(prefix_ref.shape[0]):
        out_ref[i + 1] = dot_halves(parts, halves(prefix_ref[i, :width])) + prefix_ref[i, width:]


def copy_kernel(in_ref, _, out_ref):
    out_ref[...] = in_ref[...]


def hidden_kernel(heads, spread, core_ref, own_ref, through_ref, state_ref, gain_ref, keep_ref, give_ref):
    width = own_ref.shape[1] // heads
    share = own_ref.shape[0] // spread
    on_first = core_ref[0] == 0
    for head in range(heads):
        lanes = slice(head * width, (head + 1) * width)
        outputs = own_ref[:, lanes] + dot(through_ref[:, lanes], state_ref[head], 1, 1)
        scale = lax.rsqrt(jnp.mean(outputs * outputs, axis=-1, keepdims=True) + 1e-05)
        scaled = outputs * scale * gain_ref[head : head + 1, :]
        even = jnp.concatenate([scaled[i * share : (i + 1) * share] for i in range(0, spread, 2)], axis=0)
        odd = jnp.concatenate([scaled[i * share : (i + 1) * share] for i in range(spread - 1, 0, -2)], axis=0)
        keep_ref[:, lanes] = jnp.where(on_first, even, odd).astype(BF16)
        give_ref[:, lanes] = jnp.where(on_first, odd, even).astype(BF16).astype(F32)


def project_kernel(core_ref, keep_ref, both_ref, own_ref, other_ref, out_ref):
    got = jnp.where(core_ref[0] == 0, both_ref[1], both_ref[0]).astype(BF16)
    out_ref[...] = jnp.dot(keep_ref[...], own_ref[...], preferred_element_type=F32) + jnp.dot(
        got, other_ref[...].astype(BF16), preferred_element_type=F32
    )


def sum_kernel(shares_ref, out_ref):
    total = shares_ref[0]
    for i in range(1, shares_ref.shape[0]):
        total = total + shares_ref[i]
    out_ref[...] = total.astype(BF16)


def per_device(queries, key_rows, value_rows, strengths, log_decay, norm_gain, out_weight):
    tokens, heads, width = queries.shape
    rows = 2 * tokens
    columns = out_weight.shape[1]
    ctx = lax.axis_size("ctx")
    spread = lax.axis_size("head")
    part_rows = width + width * heads // GROUP
    params = pltpu.CompilerParams(vmem_limit_bytes=48 * 1024 * 1024)

    def call(body, out_shape, name, flops=0, in_specs=None, scratch=()):
        extra = {} if in_specs is None else dict(in_specs=in_specs)
        return pl.pallas_call(
            body,
            out_shape=out_shape,
            compiler_params=params,
            name=name,
            cost_estimate=pl.CostEstimate(flops=flops, bytes_accessed=1 << 20, transcendentals=0),
            scratch_shapes=scratch,
            **extra,
        )

    def array(*shape, dtype=F32):
        return jax.ShapeDtypeStruct(shape, dtype)

    def pairs(flip):
        return [[i, i ^ flip] for i in range(ctx) if i < i ^ flip]

    smem = pl.BlockSpec(memory_space=pltpu.SMEM)
    vmem = pl.BlockSpec(memory_space=pltpu.VMEM)
    inner = [[g * GROUP + j for j in range(GROUP)] for g in range(ctx // GROUP)]
    cores = [[i, i + 1] for i in range(0, spread, 2)]
    core = (lax.axis_index("head") % 2).astype(jnp.int32).reshape(1)

    msg, solved, keys = local_call(
        key_rows.reshape(heads * rows, width),
        value_rows.reshape(heads * rows, width),
        log_decay.T,
        strengths.transpose(1, 2, 0).reshape(2 * heads, tokens),
    )
    place = (lax.axis_index("ctx") // GROUP).astype(jnp.int32).reshape(1)
    msg, place, core = lax.optimization_barrier((msg, place, core))
    parts = lax.all_to_all(msg, "ctx", 0, 0, axis_index_groups=inner)
    late_weight, _ = lax.optimization_barrier((out_weight, solved))
    wide, held = call(
        widen_kernel,
        (array(*out_weight.shape), array(*out_weight.shape, dtype=BF16)),
        "widen",
        flops=10**9,
    )(late_weight)
    other = lax.ppermute(wide, "head", [(i, i ^ 1) for i in range(spread)])
    own, through = call(
        functools.partial(own_kernel, heads),
        (array(tokens, heads * width), array(tokens, heads * width)),
        "own_outputs",
        flops=4 * 10**9,
        scratch=[pltpu.VMEM((heads * tokens, width), F32)],
    )(queries.reshape(heads * tokens, width), keys, log_decay.T, solved)
    parts, own, through = lax.optimization_barrier((parts, own, through))
    prefix, total = call(
        functools.partial(group_kernel, width),
        (array(GROUP - 1, part_rows, width), array(part_rows, width)),
        "group_scan",
    )(parts)
    quarter = ctx // 4
    group = [[g * quarter + i for i in range(quarter)] for g in range(4)]

    state_shape = array(part_rows - width, width)
    swapped, arrived, offered = [], [], total
    for g in range(4):
        swapped.append(lax.ppermute(offered, "ctx", [(i, i ^ GROUP) for i in group[g]]))
        if g == 0:
            write = call(
                functools.partial(first_kernel, width), state_shape, "first_write", in_specs=[smem, vmem, vmem]
            )(place, total, swapped[0])
        elif g < 3:
            write = call(
                functools.partial(write_kernel, width),
                state_shape,
                "next_write",
                in_specs=[smem, vmem, vmem, vmem],
            )(place, arrived[-1], total, swapped[g])
        if g < 3:
            came = lax.ppermute(write, "ctx", [(i, j ^ GROUP if g == 2 else j) for i, j in zip(group[g], group[g + 1])])
            arrived.append(call(copy_kernel, state_shape, "state", flops=10**9)(came, came))
            offered = call(copy_kernel, array(part_rows, width), "offer")(total, write)
    starts = call(
        functools.partial(start_kernel, width),
        array(GROUP, part_rows - width, width),
        "start_states",
        in_specs=[smem] + [vmem] * 9,
    )(place, total, *swapped, *arrived, prefix)
    states = lax.all_to_all(starts, "ctx", 0, 0, axis_index_groups=inner)
    keep, give = call(
        functools.partial(hidden_kernel, heads, spread),
        (array(tokens // 2, heads * width, dtype=BF16), array(tokens // 2, heads * width)),
        "hidden",
        in_specs=[smem] + [vmem] * 4,
    )(core, own, through, states.reshape(heads, width, width), norm_gain)
    given = lax.all_gather(give, "head", axis_index_groups=cores)
    sums = call(
        project_kernel,
        array(tokens // 2, columns),
        "project",
        in_specs=[smem] + [vmem] * 4,
    )(core, keep, given, held, other)
    ring = [list(range(0, spread, 2)), list(range(spread - 1, 0, -2))]
    shares = lax.all_to_all(
        sums.reshape(spread // 2, tokens // spread, columns), "head", 0, 0, axis_index_groups=ring
    )
    return call(sum_kernel, array(tokens // spread, columns, dtype=BF16), "row_sums")(shares)


def solution(mesh):
    in_specs = (
        P("ctx", "head", None),
        P("ctx", None, "head", None),
        P("ctx", None, "head", None),
        P("ctx", None, "head"),
        P("ctx", "head"),
        P("head", None),
        P("head", None),
    )
    out_specs = P(("ctx", "head"), None)
    return jax.shard_map(
        per_device, mesh=mesh, in_specs=in_specs, out_specs=out_specs, check_vma=False
    )
```

```python
import functools

import jax
import jax.numpy as jnp
from jax import lax
from jax.experimental import pallas as pl
from jax.experimental.pallas import tpu as pltpu
from jax.sharding import PartitionSpec as P

F32 = jnp.float32
BF16 = jnp.bfloat16
GROUP = 8


def dims(left_dim, right_dim):
    return (((left_dim,), (right_dim,)), ((), ()))


def halves(value):
    high = value.astype(BF16)
    return high, (value - high.astype(F32)).astype(BF16)


def dot_halves(left, right, left_dim=1, right_dim=0):
    mul = functools.partial(
        lax.dot_general, dimension_numbers=dims(left_dim, right_dim), preferred_element_type=F32
    )
    if left_dim == 0:
        return mul(left[0], right[0]) + (mul(left[0], right[1]) + mul(left[1], right[0]))
    count = left[0].shape[0]
    both = mul(jnp.concatenate(left, axis=0), right[0])
    return both[:count] + (both[count:] + mul(left[0], right[1]))


def dot(left, right, left_dim=1, right_dim=0):
    return dot_halves(halves(left), halves(right), left_dim, right_dim)


def unit_rows(rows):
    return rows * lax.rsqrt(jnp.sum(rows * rows, axis=-1, keepdims=True) + 1e-06)


def iota(shape, dim):
    return lax.broadcasted_iota(jnp.int32, shape, dim)


def thirds(value):
    high, rest = halves(value)
    last = (value - high.astype(F32) - rest.astype(F32)).astype(BF16)
    return jnp.concatenate([last.astype(F32), rest.astype(F32), high.astype(F32)], axis=0).astype(BF16)


def picked(mask, small):
    wide = lax.dot_general(
        jnp.where(mask, 1.0, 0.0).astype(BF16), small, dims(1, 1), preferred_element_type=F32
    )
    return wide[:, :8] + wide[:, 8:16] + wide[:, 16:24]


def picked_line(small, mask):
    wide = lax.dot_general(
        small, jnp.where(mask, 1.0, 0.0).astype(BF16), dims(1, 1), preferred_element_type=F32
    )
    return wide[:8] + wide[8:16] + wide[16:24]


def blocks_of(part, count, mask):
    if part.shape[0] % 16:
        part, count = jnp.concatenate([part, part], axis=0), count // 2
    return tuple(jnp.concatenate([piece] * count, axis=0) * mask for piece in halves(part))


def small_inverses(lower, width):
    lanes = 128
    row = iota((width, lanes), 0)
    lane = iota((width, lanes), 1)
    tiles = []
    for start in range(0, lower.shape[0], lanes):
        part = jnp.zeros((width, lanes), F32)
        for block in range(lanes // width):
            first = start + block * width
            part = jnp.where(lane // width == block, lower[first : first + width, start : start + lanes], part)
        inverse = jnp.where(row == lane % width, 1.0, 0.0).astype(F32)
        for column in range(width - 1):
            factor = jnp.take_along_axis(part, lane - lane % width + column, axis=1)
            inverse = inverse - factor * inverse[column : column + 1, :]
        tiles.append(inverse)
    return jnp.concatenate(tiles, axis=1)


def inverse_blocks(lowers, stop):
    size = lowers[0].shape[0]
    width = 16
    rows = iota((size, size), 0)
    cols = iota((size, size), 1)
    inverses = [small_inverses(lower, width) for lower in lowers]
    while width < stop:
        count = size // width
        lane = iota((width, size), 1) // width
        even = lane % 2 == 0
        same = jnp.where(rows // width == cols // width, 1.0, 0.0).astype(BF16)
        below = jnp.where((rows // width == cols // width + 1) & ((cols // width) % 2 == 0), 1.0, 0.0).astype(BF16)
        corners = []
        for lower in lowers:
            part = jnp.zeros((width, size), F32)
            for block in range(0, count, 2):
                part = jnp.where(lane == block, lower[(block + 1) * width : (block + 2) * width], part)
            corners.append(halves(part))
        inner = [dot_halves(c, blocks_of(t, count, same)) for c, t in zip(corners, inverses)]
        outer = [dot_halves(halves(t), blocks_of(y, count, below)) for t, y in zip(inverses, inner)]
        inverses = [
            jnp.concatenate([jnp.where(even, t, 0.0), jnp.where(even, -e, t)], axis=0)
            for t, e in zip(inverses, outer)
        ]
        width *= 2
    return inverses


def slot(core_ref, member):
    return jnp.where(core_ref[0] == 0, member, GROUP - 1 - member)


def local_kernel(
    heads, core_ref, k_hbm, v_hbm, decay_hbm, beta_hbm, msg_hbm, solved_hbm, keys_hbm,
    k_ref, v_ref, small_ref, spread_k, spread_v, keys_ref, solved_ref, carry_ref, write_ref, in_sems, out_sems,
):
    rows = k_ref.shape[0] // heads
    tokens = rows // 2
    width = k_ref.shape[1]
    half = rows // 2
    quarter = width * heads // GROUP
    sends = []

    def send(source, target):
        sends.append(pltpu.make_async_copy(source, target, out_sems.at[len(sends)]))
        sends[-1].start()

    small_ref[3 * heads :] = jnp.zeros((8 - 3 * heads, tokens), F32)
    fetches = [
        pltpu.make_async_copy(source, target, in_sems.at[i])
        for i, (source, target) in enumerate(
            (
                (k_hbm, k_ref),
                (decay_hbm, small_ref.at[:heads]),
                (beta_hbm, small_ref.at[heads : 3 * heads]),
                (v_hbm, v_ref),
            )
        )
    ]
    for fetch in fetches:
        fetch.start()
    row_tok = iota((rows, tokens), 0) // 2
    tok = iota((rows, tokens), 1)
    first = iota((rows, 1), 0) % 2 == 0
    row_ids = iota((rows, rows), 0)
    col_ids = iota((rows, rows), 1)
    eye_k = jnp.where(iota((width, width), 0) == iota((width, width), 1), 1.0, 0.0).astype(F32)
    for fetch in fetches[:3]:
        fetch.wait()
    small = thirds(small_ref[...])
    cumul_rows = picked(row_tok >= tok, small)
    cumul_line = picked_line(small, row_tok >= tok)
    betas = picked(row_tok == tok, small)
    spread_k[...] = unit_rows(k_ref[...].astype(F32))
    keys, lowers, strength = [], [], []
    for head in range(heads):
        unit = spread_k[pl.ds(head, rows, stride=heads), :]
        beta = jnp.where(
            first, betas[:, heads + head : heads + head + 1], betas[:, 2 * heads + head : 2 * heads + head + 1]
        )
        cumul = cumul_rows[:, head : head + 1]
        line = cumul_line[head : head + 1, :]
        weight = jnp.exp(jnp.where(row_ids > col_ids, cumul - line, -1e30))
        parts = halves(unit)
        lowers.append(beta * weight * dot_halves(parts, parts, 1, 1))
        keys.append(unit)
        strength.append(beta)
        keys_ref[head] = unit
        send(keys_ref.at[head], keys_hbm.at[head])
    inverses = inverse_blocks(lowers, half)
    fetches[3].wait()
    spread_v[...] = v_ref[...].astype(F32)
    rights = [
        jnp.concatenate(
            [
                strength[head] * spread_v[pl.ds(head, rows, stride=heads), :],
                (strength[head] * jnp.exp(cumul_rows[:, head : head + 1])) * keys[head],
            ],
            axis=1,
        )
        for head in range(heads)
    ]
    uppers = [dot(inverse[:, :half], right[:half]) for inverse, right in zip(inverses, rights)]
    moved = [
        right[half:] - dot(lower[half:, :half], upper)
        for lower, right, upper in zip(lowers, rights, uppers)
    ]
    unders = [dot(inverse[:, half:], rest) for inverse, rest in zip(inverses, moved)]
    for head in range(heads):
        solved = jnp.concatenate([uppers[head], unders[head]], axis=0)
        solved_ref[head] = solved
        send(solved_ref.at[head], solved_hbm.at[head])
        cumul = cumul_rows[:, head : head + 1]
        last = cumul[rows - 1 : rows, :]
        tail = jnp.exp(last - cumul) * keys[head]
        pair = dot(solved, tail, 0, 0)
        write_ref[head] = pair[:width]
        carry_ref[head] = jnp.exp(last) * eye_k - pair[width:]
        for part in range(GROUP // heads):
            member = slot(core_ref, head * (GROUP // heads) + part)
            send(carry_ref.at[head], msg_hbm.at[member, :width])
            send(write_ref.at[head, part * quarter : (part + 1) * quarter], msg_hbm.at[member, width:])
    for copy in sends:
        copy.wait()


def local_call(core, keys, values, decay, beta):
    heads, tokens = decay.shape
    rows, width = keys.shape[0] // heads, keys.shape[1]
    any_space = pl.BlockSpec(memory_space=pl.ANY)
    return pl.pallas_call(
        functools.partial(local_kernel, heads),
        out_shape=(
            jax.ShapeDtypeStruct((GROUP, width + width * heads // GROUP, width), F32),
            jax.ShapeDtypeStruct((heads, rows, 2 * width), F32),
            jax.ShapeDtypeStruct((heads, rows, width), F32),
        ),
        in_specs=[pl.BlockSpec(memory_space=pltpu.SMEM)] + [any_space] * 4,
        out_specs=(any_space,) * 3,
        scratch_shapes=[
            pltpu.VMEM(keys.shape, BF16),
            pltpu.VMEM(values.shape, BF16),
            pltpu.VMEM((8, tokens), F32),
            pltpu.VMEM(keys.shape, F32),
            pltpu.VMEM(values.shape, F32),
            pltpu.VMEM((heads, rows, width), F32),
            pltpu.VMEM((heads, rows, 2 * width), F32),
            pltpu.VMEM((heads, width, width), F32),
            pltpu.VMEM((heads, width, width), F32),
            pltpu.SemaphoreType.DMA((4,)),
            pltpu.SemaphoreType.DMA((2 * heads + 2 * GROUP,)),
        ],
        compiler_params=pltpu.CompilerParams(vmem_limit_bytes=60 * 1024 * 1024),
        name="local_chunk",
    )(core, keys, values, decay, beta)


def own_kernel(heads, q_ref, keys_ref, decay_ref, solved_ref, own_ref, through_ref, spread_q):
    tokens = q_ref.shape[0] // heads
    rows = keys_ref.shape[1]
    spread_q[...] = unit_rows(q_ref[...].astype(F32))
    small = thirds(jnp.concatenate([decay_ref[...], jnp.zeros((8 - heads, tokens), F32)], axis=0))
    reached = iota((rows, tokens), 0) // 2 >= iota((rows, tokens), 1)
    cumul_line = picked_line(small, reached)
    cumul_toks = picked(iota((tokens, tokens), 0) >= iota((tokens, tokens), 1), small)
    reached = iota((tokens, rows), 0) >= iota((tokens, rows), 1) // 2
    width = keys_ref.shape[2]
    for head in range(heads):
        lanes = slice(head * width, (head + 1) * width)
        query = spread_q[pl.ds(head, tokens, stride=heads), :]
        cumul = cumul_toks[:, head : head + 1]
        weight = jnp.exp(jnp.where(reached, cumul - cumul_line[head : head + 1, :], -1e30))
        mixed = dot(dot(query, keys_ref[head], 1, 1) * weight, solved_ref[head])
        own_ref[:, lanes] = mixed[:, :width]
        through_ref[:, lanes] = jnp.exp(cumul) * query - mixed[:, width:]


def widen_kernel(in_ref, out_ref, copy_ref):
    out_ref[...] = in_ref[...].astype(F32)
    copy_ref[...] = in_ref[...]


def compose(earlier, later, width):
    both = dot(earlier, later[:width])
    return jnp.concatenate([both[:width], both[width:] + later[width:]], axis=0)


def group_kernel(width, core_ref, parts_ref, prefix_ref, total_ref):
    count = parts_ref.shape[0]
    runs = [parts_ref[slot(core_ref, i)] for i in range(count)]
    step = 1
    while step < count:
        for start in range(step, count, 2 * step):
            for i in range(start, start + step):
                runs[i] = compose(runs[start - 1], runs[i], width)
        step *= 2
    for i in range(count - 1):
        prefix_ref[i] = runs[i]
    total_ref[...] = runs[count - 1]


def in_order(place, own, arrived):
    is_first = place % 2 == 0
    return jnp.where(is_first, own, arrived), jnp.where(is_first, arrived, own)


def first_kernel(width, place_ref, own_ref, arrived_ref, write_ref):
    earlier, later = in_order(place_ref[0], own_ref[...], arrived_ref[...])
    write_ref[...] = dot(earlier[width:], later[:width]) + later[width:]


def write_kernel(width, place_ref, state_ref, own_ref, arrived_ref, write_ref):
    earlier, later = in_order(place_ref[0], own_ref[...], arrived_ref[...])
    middle = dot(state_ref[...], earlier[:width]) + earlier[width:]
    write_ref[...] = dot(middle, later[:width]) + later[width:]


def start_kernel(width, place_ref, own_ref, *refs):
    swap_refs, state_refs, prefix_ref, out_ref = refs[:4], refs[4:7], refs[7], refs[8]
    place = place_ref[0]
    arrived = swap_refs[0][...]
    for ref in swap_refs[1:]:
        arrived = arrived + ref[...]
    state = state_refs[0][...] + state_refs[1][...] + state_refs[2][...]
    moved = dot(state, arrived[:width]) + arrived[width:]
    state = jnp.where(place % 2 == 1, moved, state)
    out_ref[0] = state
    parts = halves(state)
    for i in range(prefix_ref.shape[0]):
        out_ref[i + 1] = dot_halves(parts, halves(prefix_ref[i, :width])) + prefix_ref[i, width:]


def copy_kernel(in_ref, _, out_ref):
    out_ref[...] = in_ref[...]


def hidden_kernel(heads, spread, core_ref, own_ref, through_ref, state_ref, gain_ref, keep_ref, give_ref):
    width = own_ref.shape[1] // heads
    share = own_ref.shape[0] // spread
    on_first = core_ref[0] == 0
    for head in range(heads):
        lanes = slice(head * width, (head + 1) * width)
        outputs = own_ref[:, lanes] + dot(through_ref[:, lanes], state_ref[head], 1, 1)
        scale = lax.rsqrt(jnp.mean(outputs * outputs, axis=-1, keepdims=True) + 1e-05)
        scaled = outputs * scale * gain_ref[head : head + 1, :]
        even = jnp.concatenate([scaled[i * share : (i + 1) * share] for i in range(0, spread, 2)], axis=0)
        odd = jnp.concatenate([scaled[i * share : (i + 1) * share] for i in range(spread - 1, 0, -2)], axis=0)
        keep_ref[:, lanes] = jnp.where(on_first, even, odd).astype(BF16)
        give_ref[:, lanes] = jnp.where(on_first, odd, even).astype(BF16).astype(F32)


def project_kernel(core_ref, keep_ref, both_ref, own_ref, other_ref, out_ref):
    got = jnp.where(core_ref[0] == 0, both_ref[1], both_ref[0]).astype(BF16)
    out_ref[...] = jnp.dot(keep_ref[...], own_ref[...], preferred_element_type=F32) + jnp.dot(
        got, other_ref[...].astype(BF16), preferred_element_type=F32
    )


def sum_kernel(shares_ref, out_ref):
    total = shares_ref[0]
    for i in range(1, shares_ref.shape[0]):
        total = total + shares_ref[i]
    out_ref[...] = total.astype(BF16)


def per_device(queries, key_rows, value_rows, strengths, log_decay, norm_gain, out_weight):
    tokens, heads, width = queries.shape
    rows = 2 * tokens
    columns = out_weight.shape[1]
    ctx = lax.axis_size("ctx")
    spread = lax.axis_size("head")
    part_rows = width + width * heads // GROUP
    params = pltpu.CompilerParams(vmem_limit_bytes=48 * 1024 * 1024)

    def call(body, out_shape, name, flops=0, in_specs=None, scratch=()):
        extra = {} if in_specs is None else dict(in_specs=in_specs)
        return pl.pallas_call(
            body,
            out_shape=out_shape,
            compiler_params=params,
            name=name,
            cost_estimate=pl.CostEstimate(flops=flops, bytes_accessed=1 << 20, transcendentals=0),
            scratch_shapes=scratch,
            **extra,
        )

    def array(*shape, dtype=F32):
        return jax.ShapeDtypeStruct(shape, dtype)

    def pairs(flip):
        return [[i, i ^ flip] for i in range(ctx) if i < i ^ flip]

    smem = pl.BlockSpec(memory_space=pltpu.SMEM)
    vmem = pl.BlockSpec(memory_space=pltpu.VMEM)
    inner = [[g * GROUP + j for j in range(GROUP)] for g in range(ctx // GROUP)]
    cores = [[i, i + 1] for i in range(0, spread, 2)]
    core = (lax.axis_index("head") % 2).astype(jnp.int32).reshape(1)

    msg, solved, keys = local_call(
        core,
        key_rows.reshape(heads * rows, width),
        value_rows.reshape(heads * rows, width),
        log_decay.T,
        strengths.transpose(1, 2, 0).reshape(2 * heads, tokens),
    )
    place = (lax.axis_index("ctx") // GROUP).astype(jnp.int32).reshape(1)
    msg, place, core = lax.optimization_barrier((msg, place, core))
    both_ways = [
        [i * spread + h for i in (members[::-1] if h % 2 else members)] for members in inner for h in range(spread)
    ]
    parts = lax.all_to_all(msg, ("ctx", "head"), 0, 0, axis_index_groups=both_ways)
    late_weight, _ = lax.optimization_barrier((out_weight, solved))
    wide, held = call(
        widen_kernel,
        (array(*out_weight.shape), array(*out_weight.shape, dtype=BF16)),
        "widen",
        flops=10**9,
    )(late_weight)
    other = lax.ppermute(wide, "head", [(i, i ^ 1) for i in range(spread)])
    own, through = call(
        functools.partial(own_kernel, heads),
        (array(tokens, heads * width), array(tokens, heads * width)),
        "own_outputs",
        flops=4 * 10**9,
        scratch=[pltpu.VMEM((heads * tokens, width), F32)],
    )(queries.reshape(heads * tokens, width), keys, log_decay.T, solved)
    parts, own, through = lax.optimization_barrier((parts, own, through))
    prefix, total = call(
        functools.partial(group_kernel, width),
        (array(GROUP - 1, part_rows, width), array(part_rows, width)),
        "group_scan",
        in_specs=[smem, vmem],
    )(core, parts)
    quarter = ctx // 4
    group = [[g * quarter + i for i in range(quarter)] for g in range(4)]

    state_shape = array(part_rows - width, width)
    swapped, arrived, offered = [], [], total
    for g in range(4):
        swapped.append(lax.ppermute(offered, "ctx", [(i, i ^ GROUP) for i in group[g]]))
        if g == 0:
            write = call(
                functools.partial(first_kernel, width), state_shape, "first_write", in_specs=[smem, vmem, vmem]
            )(place, total, swapped[0])
        elif g < 3:
            write = call(
                functools.partial(write_kernel, width),
                state_shape,
                "next_write",
                in_specs=[smem, vmem, vmem, vmem],
            )(place, arrived[-1], total, swapped[g])
        if g < 3:
            came = lax.ppermute(write, "ctx", [(i, j ^ GROUP if g == 2 else j) for i, j in zip(group[g], group[g + 1])])
            arrived.append(call(copy_kernel, state_shape, "state", flops=10**9)(came, came))
            offered = call(copy_kernel, array(part_rows, width), "offer")(total, write)
    starts = call(
        functools.partial(start_kernel, width),
        array(GROUP, part_rows - width, width),
        "start_states",
        in_specs=[smem] + [vmem] * 9,
    )(place, total, *swapped, *arrived, prefix)
    states = lax.all_to_all(starts, "ctx", 0, 0, axis_index_groups=inner)
    keep, give = call(
        functools.partial(hidden_kernel, heads, spread),
        (array(tokens // 2, heads * width, dtype=BF16), array(tokens // 2, heads * width)),
        "hidden",
        in_specs=[smem] + [vmem] * 4,
    )(core, own, through, states.reshape(heads, width, width), norm_gain)
    given = lax.all_gather(give, "head", axis_index_groups=cores)
    sums = call(
        project_kernel,
        array(tokens // 2, columns),
        "project",
        in_specs=[smem] + [vmem] * 4,
    )(core, keep, given, held, other)
    ring = [list(range(0, spread, 2)), list(range(spread - 1, 0, -2))]
    shares = lax.all_to_all(
        sums.reshape(spread // 2, tokens // spread, columns), "head", 0, 0, axis_index_groups=ring
    )
    return call(sum_kernel, array(tokens // spread, columns, dtype=BF16), "row_sums")(shares)


def solution(mesh):
    in_specs = (
        P("ctx", "head", None),
        P("ctx", None, "head", None),
        P("ctx", None, "head", None),
        P("ctx", None, "head"),
        P("ctx", "head"),
        P("head", None),
        P("head", None),
    )
    out_specs = P(("ctx", "head"), None)
    return jax.shard_map(
        per_device, mesh=mesh, in_specs=in_specs, out_specs=out_specs, check_vma=False
    )
```

```python
import functools

import jax
import jax.numpy as jnp
from jax import lax
from jax.experimental import pallas as pl
from jax.experimental.pallas import tpu as pltpu
from jax.sharding import PartitionSpec as P

F32 = jnp.float32
BF16 = jnp.bfloat16
GROUP = 8


def dims(left_dim, right_dim):
    return (((left_dim,), (right_dim,)), ((), ()))


def halves(value):
    high = value.astype(BF16)
    return high, (value - high.astype(F32)).astype(BF16)


def dot_halves(left, right, left_dim=1, right_dim=0):
    mul = functools.partial(
        lax.dot_general, dimension_numbers=dims(left_dim, right_dim), preferred_element_type=F32
    )
    if left_dim == 0:
        return mul(left[0], right[0]) + (mul(left[0], right[1]) + mul(left[1], right[0]))
    count = left[0].shape[0]
    both = mul(jnp.concatenate(left, axis=0), right[0])
    return both[:count] + (both[count:] + mul(left[0], right[1]))


def dot(left, right, left_dim=1, right_dim=0):
    return dot_halves(halves(left), halves(right), left_dim, right_dim)


def unit_rows(rows):
    return rows * lax.rsqrt(jnp.sum(rows * rows, axis=-1, keepdims=True) + 1e-06)


def iota(shape, dim):
    return lax.broadcasted_iota(jnp.int32, shape, dim)


def thirds(value):
    high, rest = halves(value)
    last = (value - high.astype(F32) - rest.astype(F32)).astype(BF16)
    return jnp.concatenate([last.astype(F32), rest.astype(F32), high.astype(F32)], axis=0).astype(BF16)


def picked(mask, small):
    wide = lax.dot_general(
        jnp.where(mask, 1.0, 0.0).astype(BF16), small, dims(1, 1), preferred_element_type=F32
    )
    return wide[:, :8] + wide[:, 8:16] + wide[:, 16:24]


def picked_line(small, mask):
    wide = lax.dot_general(
        small, jnp.where(mask, 1.0, 0.0).astype(BF16), dims(1, 1), preferred_element_type=F32
    )
    return wide[:8] + wide[8:16] + wide[16:24]


def blocks_of(part, count, mask):
    if part.shape[0] % 16:
        part, count = jnp.concatenate([part, part], axis=0), count // 2
    return tuple(jnp.concatenate([piece] * count, axis=0) * mask for piece in halves(part))


def small_inverses(lower, width):
    lanes = 128
    row = iota((width, lanes), 0)
    lane = iota((width, lanes), 1)
    tiles = []
    for start in range(0, lower.shape[0], lanes):
        part = jnp.zeros((width, lanes), F32)
        for block in range(lanes // width):
            first = start + block * width
            part = jnp.where(lane // width == block, lower[first : first + width, start : start + lanes], part)
        inverse = jnp.where(row == lane % width, 1.0, 0.0).astype(F32)
        for column in range(width - 1):
            factor = jnp.take_along_axis(part, lane - lane % width + column, axis=1)
            inverse = inverse - factor * inverse[column : column + 1, :]
        tiles.append(inverse)
    return jnp.concatenate(tiles, axis=1)


def inverse_blocks(lowers, stop):
    size = lowers[0].shape[0]
    width = 16
    rows = iota((size, size), 0)
    cols = iota((size, size), 1)
    inverses = [small_inverses(lower, width) for lower in lowers]
    while width < stop:
        count = size // width
        lane = iota((width, size), 1) // width
        even = lane % 2 == 0
        same = jnp.where(rows // width == cols // width, 1.0, 0.0).astype(BF16)
        below = jnp.where((rows // width == cols // width + 1) & ((cols // width) % 2 == 0), 1.0, 0.0).astype(BF16)
        corners = []
        for lower in lowers:
            part = jnp.zeros((width, size), F32)
            for block in range(0, count, 2):
                part = jnp.where(lane == block, lower[(block + 1) * width : (block + 2) * width], part)
            corners.append(halves(part))
        inner = [dot_halves(c, blocks_of(t, count, same)) for c, t in zip(corners, inverses)]
        outer = [dot_halves(halves(t), blocks_of(y, count, below)) for t, y in zip(inverses, inner)]
        inverses = [
            jnp.concatenate([jnp.where(even, t, 0.0), jnp.where(even, -e, t)], axis=0)
            for t, e in zip(inverses, outer)
        ]
        width *= 2
    return inverses


def local_kernel(
    heads, k_hbm, v_hbm, decay_hbm, beta_hbm, msg_hbm, solved_hbm, keys_hbm,
    k_ref, v_ref, small_ref, spread_k, spread_v, keys_ref, solved_ref, carry_ref, write_ref, in_sems, out_sems,
):
    rows = k_ref.shape[0] // heads
    tokens = rows // 2
    width = k_ref.shape[1]
    half = rows // 2
    quarter = width * heads // GROUP
    sends = []

    def send(source, target):
        sends.append(pltpu.make_async_copy(source, target, out_sems.at[len(sends)]))
        sends[-1].start()

    small_ref[3 * heads :] = jnp.zeros((8 - 3 * heads, tokens), F32)
    fetches = [
        pltpu.make_async_copy(source, target, in_sems.at[i])
        for i, (source, target) in enumerate(
            (
                (k_hbm, k_ref),
                (decay_hbm, small_ref.at[:heads]),
                (beta_hbm, small_ref.at[heads : 3 * heads]),
                (v_hbm, v_ref),
            )
        )
    ]
    for fetch in fetches:
        fetch.start()
    row_tok = iota((rows, tokens), 0) // 2
    tok = iota((rows, tokens), 1)
    first = iota((rows, 1), 0) % 2 == 0
    row_ids = iota((rows, rows), 0)
    col_ids = iota((rows, rows), 1)
    eye_k = jnp.where(iota((width, width), 0) == iota((width, width), 1), 1.0, 0.0).astype(F32)
    for fetch in fetches[:3]:
        fetch.wait()
    small = thirds(small_ref[...])
    cumul_rows = picked(row_tok >= tok, small)
    cumul_line = picked_line(small, row_tok >= tok)
    betas = picked(row_tok == tok, small)
    spread_k[...] = unit_rows(k_ref[...].astype(F32))
    keys, lowers, strength = [], [], []
    for head in range(heads):
        unit = spread_k[pl.ds(head, rows, stride=heads), :]
        beta = jnp.where(
            first, betas[:, heads + head : heads + head + 1], betas[:, 2 * heads + head : 2 * heads + head + 1]
        )
        cumul = cumul_rows[:, head : head + 1]
        line = cumul_line[head : head + 1, :]
        weight = jnp.exp(jnp.where(row_ids > col_ids, cumul - line, -1e30))
        parts = halves(unit)
        lowers.append(beta * weight * dot_halves(parts, parts, 1, 1))
        keys.append(unit)
        strength.append(beta)
        keys_ref[head] = unit
        send(keys_ref.at[head], keys_hbm.at[head])
    inverses = inverse_blocks(lowers, half)
    fetches[3].wait()
    spread_v[...] = v_ref[...].astype(F32)
    rights = [
        jnp.concatenate(
            [
                strength[head] * spread_v[pl.ds(head, rows, stride=heads), :],
                (strength[head] * jnp.exp(cumul_rows[:, head : head + 1])) * keys[head],
            ],
            axis=1,
        )
        for head in range(heads)
    ]
    uppers = [dot(inverse[:, :half], right[:half]) for inverse, right in zip(inverses, rights)]
    moved = [
        right[half:] - dot(lower[half:, :half], upper)
        for lower, right, upper in zip(lowers, rights, uppers)
    ]
    unders = [dot(inverse[:, half:], rest) for inverse, rest in zip(inverses, moved)]
    solveds, lasts, tails = [], [], []
    for head in range(heads):
        solveds.append(jnp.concatenate([uppers[head], unders[head]], axis=0))
        solved_ref[head] = solveds[head]
        send(solved_ref.at[head], solved_hbm.at[head])
        cumul = cumul_rows[:, head : head + 1]
        lasts.append(cumul[rows - 1 : rows, :])
        tails.append(jnp.exp(lasts[head] - cumul) * keys[head])
    couples = [dot(solved, tail, 0, 0) for solved, tail in zip(solveds, tails)]
    for head in range(heads):
        pair, last = couples[head], lasts[head]
        write_ref[head] = pair[:width]
        carry_ref[head] = jnp.exp(last) * eye_k - pair[width:]
        for part in range(GROUP // heads):
            member = head * (GROUP // heads) + part
            send(carry_ref.at[head], msg_hbm.at[member, :width])
            send(write_ref.at[head, part * quarter : (part + 1) * quarter], msg_hbm.at[member, width:])
    for copy in sends:
        copy.wait()


def local_call(keys, values, decay, beta):
    heads, tokens = decay.shape
    rows, width = keys.shape[0] // heads, keys.shape[1]
    any_space = pl.BlockSpec(memory_space=pl.ANY)
    return pl.pallas_call(
        functools.partial(local_kernel, heads),
        out_shape=(
            jax.ShapeDtypeStruct((GROUP, width + width * heads // GROUP, width), F32),
            jax.ShapeDtypeStruct((heads, rows, 2 * width), F32),
            jax.ShapeDtypeStruct((heads, rows, width), F32),
        ),
        in_specs=[any_space] * 4,
        out_specs=(any_space,) * 3,
        scratch_shapes=[
            pltpu.VMEM(keys.shape, BF16),
            pltpu.VMEM(values.shape, BF16),
            pltpu.VMEM((8, tokens), F32),
            pltpu.VMEM(keys.shape, F32),
            pltpu.VMEM(values.shape, F32),
            pltpu.VMEM((heads, rows, width), F32),
            pltpu.VMEM((heads, rows, 2 * width), F32),
            pltpu.VMEM((heads, width, width), F32),
            pltpu.VMEM((heads, width, width), F32),
            pltpu.SemaphoreType.DMA((4,)),
            pltpu.SemaphoreType.DMA((2 * heads + 2 * GROUP,)),
        ],
        compiler_params=pltpu.CompilerParams(vmem_limit_bytes=60 * 1024 * 1024),
        name="local_chunk",
    )(keys, values, decay, beta)


def own_kernel(heads, q_ref, keys_ref, decay_ref, solved_ref, own_ref, through_ref, spread_q):
    tokens = q_ref.shape[0] // heads
    rows = keys_ref.shape[1]
    spread_q[...] = unit_rows(q_ref[...].astype(F32))
    small = thirds(jnp.concatenate([decay_ref[...], jnp.zeros((8 - heads, tokens), F32)], axis=0))
    reached = iota((rows, tokens), 0) // 2 >= iota((rows, tokens), 1)
    cumul_line = picked_line(small, reached)
    cumul_toks = picked(iota((tokens, tokens), 0) >= iota((tokens, tokens), 1), small)
    reached = iota((tokens, rows), 0) >= iota((tokens, rows), 1) // 2
    width = keys_ref.shape[2]
    for head in range(heads):
        lanes = slice(head * width, (head + 1) * width)
        query = spread_q[pl.ds(head, tokens, stride=heads), :]
        cumul = cumul_toks[:, head : head + 1]
        weight = jnp.exp(jnp.where(reached, cumul - cumul_line[head : head + 1, :], -1e30))
        mixed = dot(dot(query, keys_ref[head], 1, 1) * weight, solved_ref[head])
        own_ref[:, lanes] = mixed[:, :width]
        through_ref[:, lanes] = jnp.exp(cumul) * query - mixed[:, width:]


def widen_kernel(in_ref, out_ref, copy_ref):
    out_ref[...] = in_ref[...].astype(F32)
    copy_ref[...] = in_ref[...]


def compose(earlier, later, width):
    both = dot(earlier, later[:width])
    return jnp.concatenate([both[:width], both[width:] + later[width:]], axis=0)


def group_kernel(width, parts_ref, prefix_ref, total_ref):
    count = parts_ref.shape[0]
    runs = [parts_ref[i] for i in range(count)]
    step = 1
    while step < count:
        for start in range(step, count, 2 * step):
            for i in range(start, start + step):
                runs[i] = compose(runs[start - 1], runs[i], width)
        step *= 2
    for i in range(count - 1):
        prefix_ref[i] = runs[i]
    total_ref[...] = runs[count - 1]


def in_order(place, own, arrived):
    is_first = place % 2 == 0
    return jnp.where(is_first, own, arrived), jnp.where(is_first, arrived, own)


def first_kernel(width, place_ref, own_ref, arrived_ref, write_ref):
    earlier, later = in_order(place_ref[0], own_ref[...], arrived_ref[...])
    write_ref[...] = dot(earlier[width:], later[:width]) + later[width:]


def write_kernel(width, place_ref, state_ref, own_ref, arrived_ref, write_ref):
    earlier, later = in_order(place_ref[0], own_ref[...], arrived_ref[...])
    middle = dot(state_ref[...], earlier[:width]) + earlier[width:]
    write_ref[...] = dot(middle, later[:width]) + later[width:]


def start_kernel(width, place_ref, own_ref, *refs):
    swap_refs, state_refs, prefix_ref, out_ref = refs[:4], refs[4:7], refs[7], refs[8]
    place = place_ref[0]
    arrived = swap_refs[0][...]
    for ref in swap_refs[1:]:
        arrived = arrived + ref[...]
    state = state_refs[0][...] + state_refs[1][...] + state_refs[2][...]
    moved = dot(state, arrived[:width]) + arrived[width:]
    state = jnp.where(place % 2 == 1, moved, state)
    out_ref[0] = state
    parts = halves(state)
    for i in range(prefix_ref.shape[0]):
        out_ref[i + 1] = dot_halves(parts, halves(prefix_ref[i, :width])) + prefix_ref[i, width:]


def copy_kernel(in_ref, _, out_ref):
    out_ref[...] = in_ref[...]


def hidden_kernel(heads, spread, core_ref, own_ref, through_ref, state_ref, gain_ref, keep_ref, give_ref):
    width = own_ref.shape[1] // heads
    share = own_ref.shape[0] // spread
    on_first = core_ref[0] == 0
    for head in range(heads):
        lanes = slice(head * width, (head + 1) * width)
        outputs = own_ref[:, lanes] + dot(through_ref[:, lanes], state_ref[head], 1, 1)
        scale = lax.rsqrt(jnp.mean(outputs * outputs, axis=-1, keepdims=True) + 1e-05)
        scaled = outputs * scale * gain_ref[head : head + 1, :]
        even = jnp.concatenate([scaled[i * share : (i + 1) * share] for i in range(0, spread, 2)], axis=0)
        odd = jnp.concatenate([scaled[i * share : (i + 1) * share] for i in range(spread - 1, 0, -2)], axis=0)
        keep_ref[:, lanes] = jnp.where(on_first, even, odd).astype(BF16)
        give_ref[:, lanes] = jnp.where(on_first, odd, even).astype(BF16).astype(F32)


def project_kernel(core_ref, keep_ref, both_ref, own_ref, other_ref, out_ref):
    got = jnp.where(core_ref[0] == 0, both_ref[1], both_ref[0]).astype(BF16)
    out_ref[...] = jnp.dot(keep_ref[...], own_ref[...], preferred_element_type=F32) + jnp.dot(
        got, other_ref[...].astype(BF16), preferred_element_type=F32
    )


def sum_kernel(shares_ref, out_ref):
    total = shares_ref[0]
    for i in range(1, shares_ref.shape[0]):
        total = total + shares_ref[i]
    out_ref[...] = total.astype(BF16)


def per_device(queries, key_rows, value_rows, strengths, log_decay, norm_gain, out_weight):
    tokens, heads, width = queries.shape
    rows = 2 * tokens
    columns = out_weight.shape[1]
    ctx = lax.axis_size("ctx")
    spread = lax.axis_size("head")
    part_rows = width + width * heads // GROUP
    params = pltpu.CompilerParams(vmem_limit_bytes=48 * 1024 * 1024)

    def call(body, out_shape, name, flops=0, in_specs=None, scratch=()):
        extra = {} if in_specs is None else dict(in_specs=in_specs)
        return pl.pallas_call(
            body,
            out_shape=out_shape,
            compiler_params=params,
            name=name,
            cost_estimate=pl.CostEstimate(flops=flops, bytes_accessed=1 << 20, transcendentals=0),
            scratch_shapes=scratch,
            **extra,
        )

    def array(*shape, dtype=F32):
        return jax.ShapeDtypeStruct(shape, dtype)

    def pairs(flip):
        return [[i, i ^ flip] for i in range(ctx) if i < i ^ flip]

    smem = pl.BlockSpec(memory_space=pltpu.SMEM)
    vmem = pl.BlockSpec(memory_space=pltpu.VMEM)
    inner = [[g * GROUP + j for j in range(GROUP)] for g in range(ctx // GROUP)]
    cores = [[i, i + 1] for i in range(0, spread, 2)]
    core = (lax.axis_index("head") % 2).astype(jnp.int32).reshape(1)

    msg, solved, keys = local_call(
        key_rows.reshape(heads * rows, width),
        value_rows.reshape(heads * rows, width),
        log_decay.T,
        strengths.transpose(1, 2, 0).reshape(2 * heads, tokens),
    )
    place = (lax.axis_index("ctx") // GROUP).astype(jnp.int32).reshape(1)
    msg, place, core = lax.optimization_barrier((msg, place, core))
    parts = lax.all_to_all(msg, "ctx", 0, 0, axis_index_groups=inner)
    late_weight, _ = lax.optimization_barrier((out_weight, solved))
    wide, held = call(
        widen_kernel,
        (array(*out_weight.shape), array(*out_weight.shape, dtype=BF16)),
        "widen",
        flops=10**9,
    )(late_weight)
    other = lax.ppermute(wide, "head", [(i, i ^ 1) for i in range(spread)])
    own, through = call(
        functools.partial(own_kernel, heads),
        (array(tokens, heads * width), array(tokens, heads * width)),
        "own_outputs",
        flops=4 * 10**9,
        scratch=[pltpu.VMEM((heads * tokens, width), F32)],
    )(queries.reshape(heads * tokens, width), keys, log_decay.T, solved)
    parts, own, through = lax.optimization_barrier((parts, own, through))
    prefix, total = call(
        functools.partial(group_kernel, width),
        (array(GROUP - 1, part_rows, width), array(part_rows, width)),
        "group_scan",
    )(parts)
    quarter = ctx // 4
    group = [[g * quarter + i for i in range(quarter)] for g in range(4)]

    state_shape = array(part_rows - width, width)
    swapped, arrived, offered = [], [], total
    for g in range(4):
        swapped.append(lax.ppermute(offered, "ctx", [(i, i ^ GROUP) for i in group[g]]))
        if g == 0:
            write = call(
                functools.partial(first_kernel, width), state_shape, "first_write", in_specs=[smem, vmem, vmem]
            )(place, total, swapped[0])
        elif g < 3:
            write = call(
                functools.partial(write_kernel, width),
                state_shape,
                "next_write",
                in_specs=[smem, vmem, vmem, vmem],
            )(place, arrived[-1], total, swapped[g])
        if g < 3:
            came = lax.ppermute(write, "ctx", [(i, j ^ GROUP if g == 2 else j) for i, j in zip(group[g], group[g + 1])])
            arrived.append(call(copy_kernel, state_shape, "state", flops=10**9)(came, came))
            offered = call(copy_kernel, array(part_rows, width), "offer")(total, write)
    starts = call(
        functools.partial(start_kernel, width),
        array(GROUP, part_rows - width, width),
        "start_states",
        in_specs=[smem] + [vmem] * 9,
    )(place, total, *swapped, *arrived, prefix)
    states = lax.all_to_all(starts, "ctx", 0, 0, axis_index_groups=inner)
    keep, give = call(
        functools.partial(hidden_kernel, heads, spread),
        (array(tokens // 2, heads * width, dtype=BF16), array(tokens // 2, heads * width)),
        "hidden",
        in_specs=[smem] + [vmem] * 4,
    )(core, own, through, states.reshape(heads, width, width), norm_gain)
    given = lax.all_gather(give, "head", axis_index_groups=cores)
    sums = call(
        project_kernel,
        array(tokens // 2, columns),
        "project",
        in_specs=[smem] + [vmem] * 4,
    )(core, keep, given, held, other)
    ring = [list(range(0, spread, 2)), list(range(spread - 1, 0, -2))]
    shares = lax.all_to_all(
        sums.reshape(spread // 2, tokens // spread, columns), "head", 0, 0, axis_index_groups=ring
    )
    return call(sum_kernel, array(tokens // spread, columns, dtype=BF16), "row_sums")(shares)


def solution(mesh):
    in_specs = (
        P("ctx", "head", None),
        P("ctx", None, "head", None),
        P("ctx", None, "head", None),
        P("ctx", None, "head"),
        P("ctx", "head"),
        P("head", None),
        P("head", None),
    )
    out_specs = P(("ctx", "head"), None)
    return jax.shard_map(
        per_device, mesh=mesh, in_specs=in_specs, out_specs=out_specs, check_vma=False
    )
```
